32 devices in a mesh: stream: 2 (over y), dp: 16 (over z, x, core).
Axes of the slice: x: 2, y: 2, z: 4, core: 2. Of those that a mesh axis runs over, the one named last changes fastest.
Arguments:
- states: bfloat16 [2, 32, 96, 1024], P('stream', 'dp'), may hold values from -6 to 6
- out_grad: bfloat16 [2, 32, 96, 1024], P('stream', 'dp'), may hold values from -6 to 6
- co_params: float32 [2, 8398848], P('stream', 'dp')
- self_params: float32 [2, 7088128], P('stream', 'dp')
- text_lengths: int32 [32], P('dp'), may hold values from 1 to 128, as said below
- region_counts: int32 [32], P('dp'), may hold values from 1 to 96, as said below
Outputs:
- out_states: bfloat16 [2, 32, 96, 1024], P('stream', 'dp')
- states_grad: float32 [2, 32, 96, 1024], P('stream', 'dp')
- co_grad: float32 [2, 8398848], P('stream', 'dp')
- self_grad: float32 [2, 7088128], P('stream', 'dp')
The draws below stay inside these ranges and needn't reach their ends.
Inputs may be any that keep to these rules, and one draw needn't show every extreme that they name: `text_lengths`: some sequence has exactly 128 text tokens. `region_counts`: some image has exactly 96 regions.
All inputs are finite; a program needn't handle non-finite values.
Results may differ from the reference program's by a relative error of at most 0.02.
Values may be sent and summed in bfloat16 or wider, within the bound.
A program may use at most 320 MiB of HBM per device.

```python
import math
import jax
import jax.numpy as jnp
from jax import lax

DT = 768
HT = 12
FT = 3072
DI = 1024
HI = 8
FI = 1024
DC = 1024
HC = 8
LT = 128
LI = 96
SEQ_DEV = 2
SEQS = 32
P_CO = 8398848
P_SA = 7088128
N_DP = 16


def shapes_drawn(model_width, other_width, inner_width, hidden):
    return [(model_width, inner_width), (inner_width,), (other_width, inner_width), (other_width, inner_width), (inner_width,), (inner_width, model_width), (model_width,), (model_width,), (model_width,), (model_width, hidden), (hidden,), (hidden, model_width), (model_width,), (model_width,), (model_width,)]


def draw_stream(stream_key, layout, total_size):
    pieces = []
    for position, piece_shape in enumerate(layout):
        normal_values = jax.random.normal(jax.random.fold_in(stream_key, position), piece_shape, jnp.float32)
        if len(piece_shape) == 2:
            factor = 3.0 if position == 5 else 1.0
            scaled = normal_values * (factor / math.sqrt(piece_shape[0]))
        elif position == 7 or position == 13:
            scaled = 1.0 + 0.1 * normal_values
        else:
            scaled = 0.1 * normal_values
        pieces.append(scaled.reshape(-1))
    flat_values = jnp.concatenate(pieces)
    return jnp.pad(flat_values, (0, total_size - flat_values.shape[0]))


def draw_co_params(key, part):
    key = jax.random.fold_in(key, 1)
    text_row = draw_stream(jax.random.fold_in(key, 0), shapes_drawn(DT, DI, DC, FT), P_CO)
    image_row = draw_stream(jax.random.fold_in(key, 1), shapes_drawn(DI, DT, DC, FI), P_CO)
    return jnp.stack([text_row, image_row])


def draw_self_params(key, part):
    key = jax.random.fold_in(key, 2)
    text_row = draw_stream(jax.random.fold_in(key, 0), shapes_drawn(DT, DT, DT, FT), P_SA)
    image_row = draw_stream(jax.random.fold_in(key, 1), shapes_drawn(DI, DI, DI, FI), P_SA)
    return jnp.stack([text_row, image_row])


def draw_text_lengths(key, part):
    key = jax.random.fold_in(key, 3)
    lengths_drawn = jax.random.randint(jax.random.fold_in(key, 0), (SEQS,), 1, LT + 1, jnp.int32)
    chosen = jax.random.randint(jax.random.fold_in(key, 1), (), 0, SEQS, jnp.int32)
    return jnp.where(jnp.arange(SEQS, dtype=jnp.int32) == chosen, LT, lengths_drawn).astype(jnp.int32)


def draw_region_counts(key, part):
    key = jax.random.fold_in(key, 4)
    first_draw = jax.random.randint(jax.random.fold_in(key, 0), (SEQS,), 1, LI + 1, jnp.int32)
    second_draw = jax.random.randint(jax.random.fold_in(key, 1), (SEQS,), max(LI // 3, 1), LI + 1, jnp.int32)
    counts_drawn = jnp.maximum(first_draw * second_draw // LI, 1)
    chosen = jax.random.randint(jax.random.fold_in(key, 2), (), 0, SEQS, jnp.int32)
    return jnp.where(jnp.arange(SEQS, dtype=jnp.int32) == chosen, LI, counts_drawn).astype(jnp.int32)


def levels(rng, extent, split, smallest, largest):
    level, own = 1.0, jax.random.fold_in(rng, 6)
    for dim, shards_of in split:
        steps = jnp.exp(jax.random.uniform(jax.random.fold_in(own, dim), (shards_of,), jnp.float32, smallest / len(split), largest / len(split)))
        level = level * jnp.repeat(steps, extent[dim] // shards_of).reshape([-1 if axis == dim else 1 for axis in range(len(extent))])
    return level


def scatter_about(rng, shape, scale, limit, cuts=(), held_as=jnp.bfloat16):
    loudness = levels(rng, shape, cuts, -0.22, 0.18) if cuts else 1.0
    entries = jax.random.normal(rng, shape, jnp.float32) * scale * loudness
    return jnp.minimum(jnp.maximum(entries, -limit), limit).astype(held_as)


def setup_inputs(seed: int = 0) -> dict:
    key_of = jax.random.split(jax.random.key(seed), 7)
    return {
        "states": scatter_about(key_of[0], (2, SEQS, LI, DI), 1.0, 6.0, ((0, 2), (1, 16))),
        "out_grad": scatter_about(key_of[1], (2, SEQS, LI, DI), 1.0, 6.0, ((0, 2), (1, 16))),
        "co_params": draw_co_params(jax.random.fold_in(key_of[6], 71), 0),
        "self_params": draw_self_params(jax.random.fold_in(key_of[6], 71), 0),
        "text_lengths": draw_text_lengths(jax.random.fold_in(key_of[6], 71), 0),
        "region_counts": draw_region_counts(jax.random.fold_in(key_of[6], 71), 0),
    }


@jax.custom_vjp
def low(v):
    return lax.optimization_barrier(v.astype(jnp.bfloat16)).astype(jnp.float32)

@jax.custom_vjp
def low_back(v):
    return v

def low_keep(v):
    return (low(v), None)

def low_pass(kept, grad):
    return (grad,)

def back_keep(v):
    return (v, None)

def back_low(kept, grad):
    return (low(grad),)
low.defvjp(low_keep, low_pass)
low_back.defvjp(back_keep, back_low)
norm_eps = 1e-12
masked_score = -1000000000.0
highest = lax.Precision.HIGHEST

def shapes(model_width, other_width, inner_width, hidden):
    return [(model_width, inner_width), (inner_width,), (other_width, inner_width), (other_width, inner_width), (inner_width,), (inner_width, model_width), (model_width,), (model_width,), (model_width,), (model_width, hidden), (hidden,), (hidden, model_width), (model_width,), (model_width,), (model_width,)]

def unpack(flat_values, layout):
    pieces = []
    offset = 0
    for piece_shape in layout:
        piece_count = math.prod(piece_shape)
        pieces.append(flat_values[offset:offset + piece_count].reshape(piece_shape))
        offset += piece_count
    return pieces

def layer_norm(row_values, norm_gain, norm_shift):
    centre = row_values - lax.optimization_barrier(jnp.mean(row_values, axis=-1, keepdims=True))
    spread = lax.optimization_barrier(jnp.mean(centre * centre, axis=-1, keepdims=True))
    return centre * lax.rsqrt(spread + norm_eps) * norm_gain + norm_shift

def linear(row_values, weight_matrix, bias_vector):
    return jnp.matmul(row_values, weight_matrix, precision=highest) + bias_vector

def attend(queries, key_rows, value_rows, key_valid, head_count):
    seq_count, length, inner_width = queries.shape
    head_size = inner_width // head_count
    query_heads = queries.reshape(seq_count, length, head_count, head_size)
    key_heads = key_rows.reshape(seq_count, key_rows.shape[1], head_count, head_size)
    value_heads = value_rows.reshape(seq_count, value_rows.shape[1], head_count, head_size)
    scores = jnp.einsum('sqhd,skhd->shqk', query_heads, key_heads, precision=highest) * (1.0 / math.sqrt(head_size))
    scores = low_back(scores)
    scores = jnp.where(key_valid[:, None, None, :], scores, masked_score)
    attn_probs = low(jax.nn.softmax(scores, axis=-1))
    context = jnp.einsum('shqk,skhd->sqhd', attn_probs, value_heads, precision=highest)
    return context.reshape(seq_count, length, inner_width)

def block(residual, inputs, partner, params, key_valid, head_count):
    query_weight, query_bias, key_weight, value_weight, value_bias, out_weight, out_bias, gain_one, shift_one, up_weight, up_bias, down_weight, down_bias, gain_two, shift_two = params
    queries = low(low_back(linear(inputs, query_weight, query_bias)))
    key_rows = low(low_back(jnp.matmul(partner, key_weight, precision=highest)))
    value_rows = low(low_back(linear(partner, value_weight, value_bias)))
    context = low(low_back(attend(queries, key_rows, value_rows, key_valid, head_count)))
    first = layer_norm(residual + low_back(linear(context, out_weight, out_bias)), gain_one, shift_one)
    up_values = low_back(linear(low(first), up_weight, up_bias))
    active = low(jax.nn.gelu(up_values, approximate=False))
    return layer_norm(first + low_back(linear(active, down_weight, down_bias)), gain_two, shift_two)

def forward(co_flat, self_flat, text_states, image_states, text_valid, image_valid):
    co_low = low(co_flat)
    self_low = low(self_flat)
    co_text = unpack(co_low[0], shapes(DT, DI, DC, FT))
    co_image = unpack(co_low[1], shapes(DI, DT, DC, FI))
    self_text = unpack(self_low[0], shapes(DT, DT, DT, FT))
    self_image = unpack(self_low[1], shapes(DI, DI, DI, FI))
    text_first = block(text_states, text_states, low_back(image_states), co_text, image_valid, HC)
    image_first = block(image_states, image_states, low_back(text_states), co_image, text_valid, HC)
    text_low = low(text_first)
    image_low = low(image_first)
    text_out = block(text_first, text_low, text_low, self_text, text_valid, HT)
    image_out = block(image_first, image_low, image_low, self_image, image_valid, HI)
    return (text_out, image_out)

def reference(states, out_grad, co_params, self_params, text_lengths, region_counts):
    text_states = states[0].astype(jnp.float32).reshape(N_DP, SEQ_DEV, LT, DT)
    image_states = states[1].astype(jnp.float32).reshape(N_DP, SEQ_DEV, LI, DI)
    text_cotangent = out_grad[0].astype(jnp.float32).reshape(N_DP, SEQ_DEV, LT, DT)
    image_cotangent = out_grad[1].astype(jnp.float32).reshape(N_DP, SEQ_DEV, LI, DI)
    text_valid = (jnp.arange(LT, dtype=jnp.int32)[None, :] < text_lengths[:, None]).reshape(N_DP, SEQ_DEV, LT)
    image_valid = (jnp.arange(LI, dtype=jnp.int32)[None, :] < region_counts[:, None]).reshape(N_DP, SEQ_DEV, LI)

    def group_step(running, group_inputs):
        text_group, image_group, text_cot, image_cot, text_mask, image_mask = group_inputs

        def local_forward(co_flat, self_flat, text_part, image_part):
            return forward(co_flat, self_flat, text_part, image_part, text_mask, image_mask)
        outputs, backward = jax.vjp(local_forward, co_params, self_params, text_group, image_group)
        co_term, self_term, text_term, image_term = backward((text_cot, image_cot))
        return ((running[0] + co_term, running[1] + self_term), (outputs[0], outputs[1], text_term, image_term))
    initial = (jnp.zeros(co_params.shape, jnp.float32), jnp.zeros(self_params.shape, jnp.float32))
    totals, results = lax.scan(group_step, initial, (text_states, image_states, text_cotangent, image_cotangent, text_valid, image_valid))
    text_out, image_out, text_back, image_back = results
    out_states = jnp.stack([text_out.reshape(SEQS, LI, DI), image_out.reshape(SEQS, LI, DI)]).astype(jnp.bfloat16)
    states_grad = jnp.stack([text_back.reshape(SEQS, LI, DI), image_back.reshape(SEQS, LI, DI)])
    return (out_states, states_grad, totals[0], totals[1])
```

```python
import functools
import math

import jax
import jax.numpy as jnp
import numpy as np
from jax import lax
from jax.experimental import pallas as pl
from jax.experimental.pallas import tpu as pltpu
from jax.sharding import PartitionSpec as P


MESH_ID = pl.DeviceIdType.MESH
UNITS = 6


def place(line):
    d = lax.axis_index("dp")
    return d // 4, lax.rem(d // 2, 2), lax.rem(d, 2)


def greet(line):
    z, x, c = place(line)
    s = lax.axis_index("stream")
    barrier = pltpu.get_barrier_semaphore()

    def signal(zz, xx, cc):
        pl.semaphore_signal(barrier, inc=1, device_id=(s, (zz * 2 + xx) * 2 + cc), device_id_type=MESH_ID)

    signal(z, 1 - x, c)
    signal(z, x, 1 - c)

    @pl.when(z > 0)
    def _():
        signal(z - 1, x, c)

    @pl.when(z < line - 1)
    def _():
        signal(z + 1, x, c)

    pl.semaphore_wait(barrier, 2 + jnp.minimum(z, 1) + jnp.minimum(line - 1 - z, 1))


def gather_kernel(line, own, out, up_s, dn_s, z_r, x_s, x_r, c_s, c_r, l_s):
    z, x, c = place(line)
    s = lax.axis_index("stream")
    n = own.shape[0] // UNITS
    greet(line)

    def piece(u):
        return pl.ds(u * n, n)

    def copy(src, dst, send, recv, zz, xx, cc):
        return pltpu.make_async_remote_copy(
            src_ref=src, dst_ref=dst, send_sem=send, recv_sem=recv,
            device_id=(s, (zz * 2 + xx) * 2 + cc), device_id_type=MESH_ID)

    def block_of(v):
        return jnp.where(v == UNITS, 1 - x, x), jnp.minimum(v, UNITS - 1)

    def z_copy(zo, v, up, mine=False):
        xb, u = block_of(v)
        place_ = out.at[zo, xb, c, piece(u)]
        src = own.at[piece(u)] if mine else place_
        k = zo * (UNITS + 1) + v
        return copy(src, place_, (up_s if up else dn_s).at[k], z_r.at[k], (z + 1 if up else z - 1), x, c)

    def x_copy(zo, u, mine=False, arriving=False):
        xb = 1 - x if arriving else x
        place_ = out.at[zo, xb, c, piece(u)]
        src = own.at[piece(u)] if mine else place_
        k = zo * UNITS + u
        return copy(src, place_, x_s.at[k], x_r.at[k], z, 1 - x, c)

    def c_copy(zo, xb, u, mine=False):
        place_ = out.at[zo, xb, c, piece(u)]
        src = own.at[piece(u)] if mine else place_
        return copy(src, place_, c_s.at[(zo * 2 + xb) * UNITS + u], c_r, z, x, 1 - c)

    local = pltpu.make_async_copy(own, out.at[z, x, c], l_s)
    local.start()
    has_up, has_dn = z < line - 1, z > 0

    def send_z(zo, v, mine=False):
        @pl.when(has_up)
        def _():
            z_copy(zo, v, True, mine).start()

        @pl.when(has_dn)
        def _():
            z_copy(zo, v, False, mine).start()

    x_copy(z, UNITS - 1, True).start()
    for u in range(UNITS - 1):
        x_copy(z, u, True).start()
        send_z(z, u, True)
    send_z(z, UNITS - 1, True)
    for u in range(UNITS):
        c_copy(z, x, u, True).start()
    x_copy(z, UNITS - 1, arriving=True).wait_recv()
    send_z(z, UNITS)
    c_copy(z, 1 - x, UNITS - 1).start()

    per = UNITS + 1
    slots = per * (line - 1)
    lag = per

    def x_arrival(zo, u):
        x_copy(zo, u, arriving=True).wait_recv()
        c_copy(zo, 1 - x, u).start()

    def slot(t, carry):
        h, v = t // per, lax.rem(t, per)
        xb, u = block_of(v)

        @pl.when(z > h)
        def _():
            zo = z - 1 - h
            z_copy(zo, v, True).wait_recv()

            @pl.when(has_up)
            def _():
                z_copy(zo, v, True).start()

            @pl.when(v < UNITS - 1)
            def _():
                x_copy(zo, u).start()

            c_copy(zo, xb, u).start()

        @pl.when(z + h < line - 1)
        def _():
            zo = z + 1 + h
            z_copy(zo, v, False).wait_recv()

            @pl.when(has_dn)
            def _():
                z_copy(zo, v, False).start()

            @pl.when(v < UNITS - 1)
            def _():
                x_copy(zo, u).start()

            c_copy(zo, xb, u).start()

        late(t - lag)
        return carry

    def late(t):
        @pl.when(jnp.logical_and(t < 0, t + per < UNITS - 1))
        def _():
            x_arrival(z, t + per)

        h, v = t // per, lax.rem(t, per)

        @pl.when(jnp.logical_and(t >= 0, v < UNITS - 1))
        def _():
            @pl.when(z > h)
            def _():
                x_arrival(z - 1 - h, v)

            @pl.when(z + h < line - 1)
            def _():
                x_arrival(z + 1 + h, v)

    lax.fori_loop(0, slots, slot, 0)

    def rest(t, carry):
        late(t)
        return carry

    lax.fori_loop(slots - lag, slots, rest, 0)

    pltpu.make_async_remote_copy(
        src_ref=out.at[:, :, c], dst_ref=out.at[:, :, 1 - c], send_sem=l_s, recv_sem=c_r,
        device_id=(s, (z * 2 + x) * 2 + 1 - c), device_id_type=MESH_ID).wait_recv()
    local.wait()

    def sent(zo, carry):
        for v in range(per):
            @pl.when(jnp.logical_and(has_up, zo <= z))
            def _():
                z_copy(zo, v, True).wait_send()

            @pl.when(jnp.logical_and(has_dn, zo >= z))
            def _():
                z_copy(zo, v, False).wait_send()
        for u in range(UNITS - 1):
            x_copy(zo, u).wait_send()
        @pl.when(zo == z)
        def _():
            x_copy(zo, UNITS - 1).wait_send()
        for xb in range(2):
            for u in range(UNITS):
                c_copy(zo, xb, u).wait_send()
        return carry

    lax.fori_loop(0, line, sent, 0)


def gather(own, line, cid, name):
    rows = own.shape[0]
    dma = pltpu.SemaphoreType.DMA
    per = UNITS + 1
    return pl.pallas_call(
        functools.partial(gather_kernel, line),
        out_shape=jax.ShapeDtypeStruct((line, 2, 2) + own.shape, own.dtype),
        in_specs=[pl.BlockSpec(memory_space=pl.ANY)],
        out_specs=pl.BlockSpec(memory_space=pl.ANY),
        scratch_shapes=[dma((line * per,)), dma((line * per,)), dma((line * per,)), dma((line * UNITS,)), dma((line * UNITS,)),
                        dma((line * 2 * UNITS,)), dma, dma],
        compiler_params=pltpu.CompilerParams(collective_id=cid, has_side_effects=True),
        name=name,
    )(own)


def scatter_kernel(line, lead, g, out, gv, cr, xr, ur, dr, l_s, c_s, c_r, x_s, x_r, u_s, u_r, d_s, d_r):
    z, x, c = place(line)
    s = lax.axis_index("stream")
    per = UNITS + 1
    n = gv.shape[2] // UNITS
    last = line - 1

    def piece(u):
        return pl.ds(u * n, n)

    def copy(src, dst, send, recv, zz, xx, cc):
        return pltpu.make_async_remote_copy(
            src_ref=src, dst_ref=dst, send_sem=send, recv_sem=recv,
            device_id=(s, (zz * 2 + xx) * 2 + cc), device_id_type=MESH_ID)

    def block_of(v):
        return jnp.where(v == 0, 1 - x, x), jnp.where(v < 2, UNITS - 1, v - 2)

    def local(zo, xb, u):
        return pltpu.make_async_copy(g.at[zo, xb, c, piece(u)], gv.at[zo, xb, piece(u)], l_s.at[(zo * 2 + xb) * UNITS + u])

    def c_copy(zo, xb, u):
        k = (zo * 2 + xb) * UNITS + u
        return copy(g.at[zo, xb, 1 - c, piece(u)], cr.at[zo, xb, piece(u)], c_s.at[k], c_r.at[k], z, x, 1 - c)

    def x_copy(zo, u):
        k = zo * UNITS + u
        return copy(gv.at[zo, 1 - x, piece(u)], xr.at[zo, piece(u)], x_s.at[k], x_r.at[k], z, 1 - x, c)

    def z_copy(to, v, up):
        xb, u = block_of(v)
        k = to * per + v
        dst, send, recv = (ur, u_s, u_r) if up else (dr, d_s, d_r)
        return copy(gv.at[to, xb, piece(u)], dst.at[to, pl.ds(v * n, n)], send.at[k], recv.at[k], (z + 1 if up else z - 1), x, c)

    def wide(value):
        return value.astype(jnp.float32)

    def both_cores(zo, xb, u):
        local(zo, xb, u).wait()
        c_copy(zo, xb, u).wait_recv()
        return wide(gv[zo, xb, piece(u)]) + wide(cr[zo, xb, piece(u)])

    def start_block(zo):
        for xb in (1 - x, x):
            for u in range(UNITS):
                local(zo, xb, u).start()

    def send_block(zo):
        for xb in (1 - x, x):
            for u in range(UNITS):
                c_copy(zo, xb, u).start()

    lax.fori_loop(0, line, lambda i, k: (start_block(i), k)[1], 0)
    greet(line)
    lax.fori_loop(0, line, lambda i, k: (send_block(i), k)[1], 0)

    def x_send(zo, u):
        gv[zo, 1 - x, piece(u)] = both_cores(zo, 1 - x, u).astype(gv.dtype)
        x_copy(zo, u).start()

    def z_send(to, v, up):
        xb, u = block_of(v)
        first = z == (0 if up else last)
        got = ur if up else dr

        @pl.when(v < 2)
        def _():
            total = both_cores(to, xb, u)

            @pl.when(first)
            def _():
                gv[to, xb, piece(u)] = total.astype(gv.dtype)

            @pl.when(jnp.logical_not(first))
            def _():
                z_copy(to, v, up).wait_recv()
                gv[to, xb, piece(u)] = (total + wide(got[to, pl.ds(v * n, n)])).astype(gv.dtype)

        @pl.when(v >= 2)
        def _():
            total = both_cores(to, xb, u)
            x_copy(to, u).wait_recv()
            total = total + wide(xr[to, piece(u)])

            @pl.when(first)
            def _():
                gv[to, xb, piece(u)] = total.astype(gv.dtype)

            @pl.when(jnp.logical_not(first))
            def _():
                z_copy(to, v, up).wait_recv()
                gv[to, xb, piece(u)] = (total + wide(got[to, pl.ds(v * n, n)])).astype(gv.dtype)

        z_copy(to, v, up).start()

    def stage(t, act):
        i = t - z
        to = last - i // per

        @pl.when(jnp.logical_and(jnp.logical_and(i >= 0, i < per * last), to > z))
        def _():
            act(to, lax.rem(i, per), True)

        j = t - (last - z)
        to_down = j // per

        @pl.when(jnp.logical_and(jnp.logical_and(j >= 0, j < per * last), to_down < z))
        def _():
            act(to_down, lax.rem(j, per), False)

    def x_stage(to, v, up):
        @pl.when(v >= 2)
        def _():
            x_send(to, v - 2)

    def slot(t, carry):
        stage(t, x_stage)

        own = t - per * last

        @pl.when(jnp.logical_and(own >= 0, own < UNITS - 1))
        def _():
            x_send(z, own)

        stage(t - lead, z_send)
        return carry

    lax.fori_loop(0, per * last + max(lead + last, UNITS - 1), slot, 0)

    def arrived(v, total):
        def plus(up, down):
            value = total
            if up:
                z_copy(z, v, True).wait_recv()
                value = value + wide(ur[z, pl.ds(v * n, n)])
            if down:
                z_copy(z, v, False).wait_recv()
                value = value + wide(dr[z, pl.ds(v * n, n)])
            return value

        return plus

    def finish(v, total, store):
        plus = arrived(v, total)

        @pl.when(z == 0)
        def _():
            store(plus(False, True))

        @pl.when(z == last)
        def _():
            store(plus(True, False))

        @pl.when(jnp.logical_and(z > 0, z < last))
        def _():
            store(plus(True, True))

    def keep(value):
        gv[z, 1 - x, piece(UNITS - 1)] = value.astype(gv.dtype)

    finish(0, both_cores(z, 1 - x, UNITS - 1), keep)
    x_copy(z, UNITS - 1).start()
    for v in tuple(range(2, per)) + (1,):
        u = UNITS - 1 if v == 1 else v - 2
        total = both_cores(z, x, u)
        x_copy(z, u).wait_recv()
        total = total + wide(xr[z, piece(u)])

        def put(value, u=u):
            out[piece(u)] = value

        finish(v, total, put)

    def sent(zo, carry):
        for v in range(per):
            @pl.when(zo > z)
            def _():
                z_copy(zo, v, True).wait_send()

            @pl.when(zo < z)
            def _():
                z_copy(zo, v, False).wait_send()
        for u in range(UNITS - 1):
            x_copy(zo, u).wait_send()

        @pl.when(zo == z)
        def _():
            x_copy(zo, UNITS - 1).wait_send()

        for xb in range(2):
            for u in range(UNITS):
                c_copy(zo, xb, u).wait_send()
        return carry

    lax.fori_loop(0, line, sent, 0)


def scatter(g, line, cid, name, lead=2):
    block = g.shape[3:]
    rows = block[0]
    n = rows // UNITS
    dma = pltpu.SemaphoreType.DMA
    per = UNITS + 1
    items = line * per
    vm = lambda *shape: pltpu.VMEM(shape + block[1:], g.dtype)
    return pl.pallas_call(
        functools.partial(scatter_kernel, line, lead),
        out_shape=jax.ShapeDtypeStruct(block, jnp.float32),
        in_specs=[pl.BlockSpec(memory_space=pl.ANY)],
        out_specs=pl.BlockSpec(memory_space=pltpu.VMEM),
        scratch_shapes=[vm(line, 2, rows), vm(line, 2, rows), vm(line, rows), vm(line, per * n), vm(line, per * n),
                        dma((line * 2 * UNITS,)), dma((line * 2 * UNITS,)), dma((line * 2 * UNITS,)),
                        dma((line * UNITS,)), dma((line * UNITS,)), dma((items,)), dma((items,)), dma((items,)), dma((items,))],
        compiler_params=pltpu.CompilerParams(collective_id=cid, has_side_effects=True, vmem_limit_bytes=50 * 2**20),
        name=name,
    )(g)


F32, BF16 = jnp.float32, jnp.bfloat16
NT = (((1,), (1,)), ((), ()))
TN = (((0,), (0,)), ((), ()))
norm_eps = 1e-12
masked_score = -1000000000.0
other_sequence = -3.0e38


def dot(a, b, dims=(((1,), (0,)), ((), ()))):
    return lax.dot_general(a, b, dims, preferred_element_type=F32)


class Block:
    def __init__(self, width, other, inner, hidden, heads, length, other_length, seqs, base=0):
        self.width, self.other, self.inner, self.hidden, self.heads = width, other, inner, hidden, heads
        self.length, self.other_length, self.seqs = length, other_length, seqs
        self.rows, self.other_rows = length * seqs, other_length * seqs
        self.base = base
        self.place = {}
        self.parts = []
        tile, flat = 0, 0

        def matrix(name, k, n):
            nonlocal tile, flat
            self.place[name] = (tile, k, n)
            self.parts.append((tile, flat, k, k * n // 128, n // 128))
            tile, flat = tile + k * n // 2048, flat + k * n // 128

        def vectors(*names):
            nonlocal tile, flat
            rows = 0
            for name, size in names:
                self.place[name] = (tile, rows, size)
                rows += size // 128
            self.parts.append((tile, flat, 0, rows, 0))
            tile, flat = tile + (rows + 15) // 16, flat + rows

        matrix("q_w", width, inner)
        vectors(("q_b", inner))
        matrix("k_w", other, inner)
        matrix("v_w", other, inner)
        vectors(("v_b", inner))
        matrix("o_w", inner, width)
        vectors(("o_b", width), ("g1", width), ("b1", width))
        matrix("i_w", width, hidden)
        vectors(("i_b", hidden))
        matrix("f_w", hidden, width)
        vectors(("f_b", width), ("g2", width), ("b2", width))
        self.tiles, self.flat_rows = tile, flat


VECS = ("q_b", "v_b", "o_b", "g1", "b1", "i_b", "f_b", "g2", "b2")
GROUPS = (("q_b",), ("v_b",), ("o_b", "g1", "b1"), ("i_b",), ("f_b", "g2", "b2"))


def cols(j, size=256):
    return pl.ds(pl.multiple_of(j * size, size), size)


class Net:
    def __init__(self, b, w, vec, sc):
        self.b, self.w, self.vec, self.s = b, w, vec, sc

    def mat(self, name):
        tile, k, n = self.b.place[name]
        return self.w.at[pl.ds(self.b.base + tile, k * n // 2048)].reshape(k // 16, n // 128, 16, 128)

    def row(self, name, j=None):
        k = VECS.index(name)
        size = self.b.place[name][2]
        return self.vec[k : k + 1, :size] if j is None else self.vec[k : k + 1, cols(j)]

    def load_vectors(self):
        for group in GROUPS:
            tile = self.b.place[group[0]][0]
            rows = sum(self.b.place[g][2] for g in group) // 128
            count = (rows + 15) // 16
            value = self.w[pl.ds(self.b.base + tile, count)].reshape(count * 16, 128).astype(F32)
            r = 0
            for name in group:
                k = VECS.index(name)
                for j in range(self.b.place[name][2] // 128):
                    self.vec[k : k + 1, j * 128 : (j + 1) * 128] = value[r : r + 1]
                    r += 1

    def store_vectors(self, group, scratch):
        tile = self.b.place[group[0]][0]
        rows = sum(self.b.place[g][2] for g in group) // 128
        count = (rows + 15) // 16
        scratch[0 : count * 16] = jnp.zeros((count * 16, 128), F32)
        r = 0
        for name in group:
            k = VECS.index(name)
            for j in range(self.b.place[name][2] // 128):
                scratch[r : r + 1, :] = self.vec[k : k + 1, j * 128 : (j + 1) * 128]
                r += 1
        self.w[pl.ds(self.b.base + tile, count)] = scratch[0 : count * 16].astype(BF16).reshape(count, 16, 128)

    def nn(self, x, name, put, step=256):
        m = self.mat(name)
        k, n = self.b.place[name][1:]

        def body(j, carry):
            per = step // 128
            w = jnp.concatenate([m[:, per * j + i].reshape(k, 128) for i in range(per)], axis=1)
            put(j, dot(x[...], w))
            return carry

        lax.fori_loop(0, n // step, body, 0)

    def nt(self, g, name, put, step=256):
        m = self.mat(name)
        k, n = self.b.place[name][1:]

        def body(j, carry):
            strips = step // 16
            w = jnp.concatenate(
                [m[pl.ds(j * strips, strips), i].reshape(step, 128) for i in range(n // 128)], axis=1)
            put(j, dot(g[...], w, NT))
            return carry

        lax.fori_loop(0, k // step, body, 0)

    def tn(self, a, g, name, step=256):
        m = self.mat(name)
        k, n = self.b.place[name][1:]
        per = step // 128

        def body(j, carry):
            got = dot(a[...], g[:, cols(j, step)], TN).astype(BF16)
            for i in range(per):
                m[:, per * j + i] = got[:, i * 128 : (i + 1) * 128].reshape(k // 16, 16, 128)
            return carry

        lax.fori_loop(0, n // step, body, 0)

    def norm(self, r, gain, shift):
        centre = r - jnp.mean(r, axis=-1, keepdims=True)
        spread = jnp.mean(centre * centre, axis=-1, keepdims=True)
        return centre * lax.rsqrt(spread + norm_eps) * self.row(gain) + self.row(shift)

    def norm_back(self, r, dy, gain, shift):
        centre = r - jnp.mean(r, axis=-1, keepdims=True)
        spread = jnp.mean(centre * centre, axis=-1, keepdims=True)
        s = lax.rsqrt(spread + norm_eps)
        xh = centre * s
        t = dy * self.row(gain)
        dr = s * (t - jnp.mean(t, axis=-1, keepdims=True) - xh * jnp.mean(t * xh, axis=-1, keepdims=True))
        size = self.b.width
        kg, kb = VECS.index(gain), VECS.index(shift)
        self.vec[kg : kg + 1, :size] = jnp.sum(dy * xh, axis=0, keepdims=True)
        self.vec[kb : kb + 1, :size] = jnp.sum(dy, axis=0, keepdims=True)
        return dr

    def put_sum(self, name, ref):
        k = VECS.index(name)
        self.vec[k : k + 1, : self.b.place[name][2]] = jnp.sum(ref[...].astype(F32), axis=0, keepdims=True)

    def mask(self, fill, counts):
        b = self.b
        shape = (b.rows, b.other_rows)
        row = lax.broadcasted_iota(jnp.int32, shape, 0)
        col = lax.broadcasted_iota(jnp.int32, shape, 1)
        value = jnp.full(shape, other_sequence, F32)
        for q in range(b.seqs):
            mine = (row >= q * b.length) & (row < (q + 1) * b.length)
            mine = mine & (col >= q * b.other_length) & (col < (q + 1) * b.other_length)
            value = jnp.where(mine, jnp.where(col < q * b.other_length + counts(q), 1.0, masked_score), value)
        fill[...] = value

    def heads_of(self, refs, g):
        e = self.b.inner // self.b.heads
        values = [ref[:, cols(g, 128)] for ref in refs]
        if e == 128:
            return [values]
        lane = lax.broadcasted_iota(jnp.int32, (1, 128), 1)
        return [
            [jnp.where((lane >= h * e) & (lane < (h + 1) * e), value, jnp.zeros((), BF16)) for value in values]
            for h in range(128 // e)]

    def attend(self, q, k, v, fill, p, c):
        b = self.b
        e = b.inner // b.heads
        scale = 1.0 / math.sqrt(e)
        per = max(128 // e, 1)

        def body(g, carry):
            keys = k[:, cols(g, 128)]
            total = None
            for h, (qh,) in enumerate(self.heads_of([q], g)):
                vh = self.heads_of([v], g)[h][0]
                s = dot(qh, keys, NT) * scale
                f = fill[...]
                s = jnp.where(f > 0, s, f)
                ex = jnp.exp(s - jnp.max(s, axis=-1, keepdims=True))
                probs = (ex * (1.0 / jnp.sum(ex, axis=-1, keepdims=True))).astype(BF16)
                p[g * per + h] = probs
                got = dot(probs, vh)
                total = got if total is None else total + got
            c[:, cols(g, 128)] = total.astype(BF16)
            return carry

        lax.fori_loop(0, b.inner // 128, body, 0)

    def attend_back(self, q, k, v, p, dc, dq, dk, dv):
        b = self.b
        e = b.inner // b.heads
        scale = 1.0 / math.sqrt(e)
        per = max(128 // e, 1)

        def body(g, carry):
            values = v[:, cols(g, 128)]
            sums = None
            for h, (qh, kh, dh) in enumerate(self.heads_of([q, k, dc], g)):
                probs = p[g * per + h]
                dp = dot(dh, values, NT)
                wide = probs.astype(F32)
                ds = (wide * (dp - jnp.sum(wide * dp, axis=-1, keepdims=True))).astype(BF16)
                got = [dot(ds, kh), dot(ds, qh, TN), dot(probs, dh, TN)]
                sums = got if sums is None else [x + y for x, y in zip(sums, got)]
            dq[:, cols(g, 128)] = (sums[0] * scale).astype(BF16)
            dk[:, cols(g, 128)] = (sums[1] * scale).astype(BF16)
            dv[:, cols(g, 128)] = sums[2].astype(BF16)
            return carry

        lax.fori_loop(0, b.inner // 128, body, 0)

    def forward(self, x, u, z, counts):
        s, b = self.s, self.b
        self.load_vectors()
        self.mask(s["fill"], counts)

        def put(ref, bias=None):
            def store(j, value):
                if bias is not None:
                    value = value + self.row(bias, j)
                ref[:, cols(j)] = value.astype(BF16)
            return store

        self.nn(u, "q_w", put(s["q"], "q_b"))
        self.nn(z, "k_w", put(s["k"]))
        self.nn(z, "v_w", put(s["v"], "v_b"))
        self.attend(s["q"], s["k"], s["v"], s["fill"], s["p"], s["c"])

        def first(j, value):
            s["r1"][:, cols(j)] = x[:, cols(j)].astype(F32) + (value + self.row("o_b", j))

        self.nn(s["c"], "o_w", first)
        y1 = self.norm(s["r1"][...], "g1", "b1")
        s["r2"][...] = y1
        s["y1"][...] = y1.astype(BF16)

        def up(j, value):
            value = value + self.row("i_b", j)
            half = 0.5 * (1.0 + lax.erf(value * (1.0 / math.sqrt(2.0))))
            s["a"][:, cols(j)] = (value * half).astype(BF16)
            s["gp"][:, cols(j)] = (half + value * (jnp.exp(-0.5 * value * value) * (1.0 / math.sqrt(2.0 * math.pi)))).astype(BF16)

        self.nn(s["y1"], "i_w", up)

        def second(j, value):
            s["r2"][:, cols(j)] = s["r2"][:, cols(j)] + (value + self.row("f_b", j))

        self.nn(s["a"], "f_w", second)
        return self.norm(s["r2"][...], "g2", "b2")

    def backward(self, dy, u, z, put_resid, put_z, done):
        s, b = self.s, self.b
        small = s["small"]
        dr2 = self.norm_back(s["r2"][...], dy[...], "g2", "b2")
        dy[...] = dr2
        s["m"][...] = dr2.astype(BF16)
        self.put_sum("f_b", s["m"])

        def inner(j, value):
            s["dz"][:, cols(j)] = (value * s["gp"][:, cols(j)].astype(F32)).astype(BF16)

        self.nt(s["m"], "f_w", inner)
        self.store_vectors(GROUPS[4], small)
        self.tn(s["a"], s["m"], "f_w")
        done(("f_w", "f_b"))
        self.put_sum("i_b", s["dz"])

        def mid(j, value):
            dy[:, cols(j)] = dy[:, cols(j)] + value

        self.nt(s["dz"], "i_w", mid)
        self.store_vectors(GROUPS[3], small)
        self.tn(s["y1"], s["dz"], "i_w")
        done(("i_w", "i_b"))
        dr1 = self.norm_back(s["r1"][...], dy[...], "g1", "b1")
        dy[...] = dr1
        s["m"][...] = dr1.astype(BF16)
        self.put_sum("o_b", s["m"])

        def context(j, value):
            s["dc"][:, cols(j)] = value.astype(BF16)

        self.nt(s["m"], "o_w", context)
        self.store_vectors(GROUPS[2], small)
        self.tn(s["c"], s["m"], "o_w")
        done(("o_w", "o_b"))
        self.attend_back(s["q"], s["k"], s["v"], s["p"], s["dc"], s["dq"], s["dk"], s["dv"])

        def resid(j, value):
            put_resid(j, dy[:, cols(j)] + value)

        self.nt(s["dq"], "q_w", resid)
        m = self.mat("v_w")
        mk = self.mat("k_w")
        k, n = b.place["v_w"][1:]

        def body(j, carry):
            def rows_of(mm):
                return jnp.concatenate([mm[pl.ds(j * 16, 16), i].reshape(256, 128) for i in range(n // 128)], axis=1)
            put_z(j, dot(s["dk"][...], rows_of(mk), NT) + dot(s["dv"][...], rows_of(m), NT))
            return carry

        lax.fori_loop(0, k // 256, body, 0)
        self.put_sum("q_b", s["dq"])
        self.put_sum("v_b", s["dv"])
        self.store_vectors(GROUPS[0], small)
        self.store_vectors(GROUPS[1], small)
        self.tn(u, s["dq"], "q_w")
        self.tn(z, s["dk"], "k_w")
        self.tn(z, s["dv"], "v_w")
        done(("q_w", "q_b", "k_w", "v_w", "v_b"))


def scratch_of(b):
    return {
        "q": ((b.rows, b.inner), BF16), "k": ((b.other_rows, b.inner), BF16), "v": ((b.other_rows, b.inner), BF16),
        "p": ((b.heads, b.rows, b.other_rows), BF16), "c": ((b.rows, b.inner), BF16),
        "r1": ((b.rows, b.width), F32), "r2": ((b.rows, b.width), F32), "y1": ((b.rows, b.width), BF16),
        "a": ((b.rows, b.hidden), BF16), "gp": ((b.rows, b.hidden), BF16), "fill": ((b.rows, b.other_rows), F32)}


def scratch_back(bs):
    rows, width = bs[0].rows, bs[0].width
    inner = max(b.inner for b in bs)
    other = max(b.other_rows for b in bs)
    return {
        "m": ((rows, width), BF16), "dz": ((rows, bs[0].hidden), BF16)}


def compute_kernel(co, sa, lens, x, xp, gy, wco, wsa, out, own_grad, sent, gco, gsa, wc, ws, vec, vec2, small, sems, *scr):
    names = sorted(scratch_of(co))
    sc = dict(zip(names, scr[: len(names)]))
    ss = dict(zip(names, scr[len(names) : 2 * len(names)]))
    rest = scr[2 * len(names) :]
    m, dz, dy, h, hb, dqc, dkc, dvc, dcc, dqs, dks, dvs, dcs = rest
    for d, extra in ((sc, (dqc, dkc, dvc, dcc)), (ss, (dqs, dks, dvs, dcs))):
        d["m"], d["dz"], d["small"] = m, dz, small
        d["dq"], d["dk"], d["dv"], d["dc"] = extra
    copies = [pltpu.make_async_copy(wco, wc, sems.at[0]), pltpu.make_async_copy(wsa, ws, sems.at[1])]
    for cp in copies:
        cp.start()
    copies[0].wait()
    a = Net(co, wc, vec, sc)
    bnet = Net(sa, ws, vec2, ss)
    value = a.forward(x, x, xp, lambda q: lens[1, q])
    h[...] = value
    hb[...] = value.astype(BF16)
    copies[1].wait()
    out[...] = bnet.forward(h, hb, hb, lambda q: lens[0, q]).astype(BF16)
    dy[...] = gy[...].astype(F32)

    def put_h(j, value):
        h[:, cols(j)] = value

    def add_h(j, value):
        h[:, cols(j)] = h[:, cols(j)] + value

    bnet.backward(dy, hb, hb, put_h, add_h, lambda names: None)
    back = pltpu.make_async_copy(ws, gsa, sems.at[1])
    back.start()

    def put_own(j, value):
        own_grad[:, cols(j)] = value

    def put_sent(j, value):
        sent[:, cols(j)] = value.astype(BF16)

    a.backward(h, x, xp, put_own, put_sent, lambda names: None)
    back2 = pltpu.make_async_copy(wc, gco, sems.at[0])
    back2.start()
    back.wait()
    back2.wait()


def compute(co, sa, lens, x, xp, gy, wco, wsa):
    any_ = pl.BlockSpec(memory_space=pl.ANY)
    vm = pl.BlockSpec(memory_space=pltpu.VMEM)
    names = sorted(scratch_of(co))
    V = lambda shape, dtype: pltpu.VMEM(shape, dtype)
    scr = [V(wco.shape, BF16), V(wsa.shape, BF16), V((16, 3072), F32), V((16, 3072), F32), V((32, 128), F32), pltpu.SemaphoreType.DMA((2,))]
    scr += [V(*scratch_of(co)[n]) for n in names] + [V(*scratch_of(sa)[n]) for n in names]
    rows, width = co.rows, co.width
    scr += [V((rows, width), BF16), V((rows, co.hidden), BF16), V((rows, width), F32), V((rows, width), F32), V((rows, width), BF16)]
    for b in (co, sa):
        scr += [V((b.rows, b.inner), BF16), V((b.other_rows, b.inner), BF16), V((b.other_rows, b.inner), BF16), V((b.rows, b.inner), BF16)]
    return pl.pallas_call(
        functools.partial(compute_kernel, co, sa),
        out_shape=(jax.ShapeDtypeStruct((rows, width), BF16), jax.ShapeDtypeStruct((rows, width), F32),
                   jax.ShapeDtypeStruct((co.other_rows, co.other), BF16),
                   jax.ShapeDtypeStruct(wco.shape, BF16), jax.ShapeDtypeStruct(wsa.shape, BF16)),
        in_specs=[pl.BlockSpec(memory_space=pltpu.SMEM), vm, vm, vm, any_, any_],
        out_specs=(vm, vm, vm, any_, any_),
        scratch_shapes=scr,
        compiler_params=pltpu.CompilerParams(vmem_limit_bytes=63 * 2**20),
        name="compute",
    )(lens, x, xp, gy, wco, wsa)


DT, HT, FT = 768, 12, 3072
DI, HI, FI = 1024, 8, 1024
DC, HC = 1024, 8
LT, LI = 128, 96
LINE_MAX = 8


def blocks_of(text, seqs):
    if text:
        return (Block(DT, DI, DC, FT, HC, LT, LI, seqs), Block(DT, DT, DT, FT, HT, LT, LT, seqs))
    return (Block(DI, DT, DC, FI, HC, LI, LT, seqs), Block(DI, DI, DI, FI, HI, LI, LI, seqs))


def flat_row(part, tile):
    first, flat, k, rows, nb = part
    t = tile - first
    return flat + (t // nb) * 16 * nb + t % nb if k else flat + t * 16


class Plan:
    def __init__(self, blocks, devices, flat_total):
        self.blocks = blocks
        self.shard = flat_total // 128 // devices
        tiles = max(b.tiles for b in blocks)
        self.rows = -(-tiles // (devices * UNITS)) * UNITS
        self.tiles = self.rows * devices
        before = after = 0
        for b in blocks:
            for d in range(devices):
                lo, hi = self.rows * d, self.rows * (d + 1)
                for part in b.parts:
                    first, flat, k, rows, nb = part
                    count = rows // 16 if k else (rows + 15) // 16
                    a, z = max(lo, first), min(hi, first + count)
                    if a >= z:
                        continue
                    least = min(flat_row(part, t) for t in range(a, min(z, a + max(nb, 1))))
                    reach = 15 * nb if k else 15
                    most = max(flat_row(part, t) for t in range(max(a, z - max(nb, 1)), z)) + reach
                    before = max(before, self.shard * d - least)
                    after = max(after, most + 1 - self.shard * (d + 1))
        self.before = -(-before // 16) * 16
        self.after = -(-after // 16) * 16
        self.window = -(-(self.before + self.shard + self.after) // 8) * 8

    def table(self, b):
        index = np.full((self.tiles * 16,), -1, np.int32)
        for first, flat, k, rows, nb in b.parts:
            if k:
                r, j = np.arange(k)[:, None], np.arange(nb)[None]
                at = first * 16 + ((r // 16) * nb + j) * 16 + r % 16
                index[at.reshape(-1)] = (flat + r * nb + j).reshape(-1)
            else:
                index[first * 16 : first * 16 + rows] = flat + np.arange(rows)
        return index


def each_tile(plan, b, d, act):
    lo = plan.rows * d
    start = plan.shard * d - plan.before
    for part in b.parts:
        first, flat, k, rows, nb = part
        if k:
            count = rows // 16
            a = jnp.clip(lo - first, 0, count)
            z = jnp.clip(lo + plan.rows - first, 0, count)

            def body(t, carry, first=first, flat=flat, nb=nb):
                i = t // nb
                act(first + t - lo, flat + i * 16 * nb + (t - i * nb) - start, nb, 16)
                return carry

            lax.fori_loop(a, z, body, 0)
        else:
            for t in range((rows + 15) // 16):
                here = jnp.logical_and(first + t >= lo, first + t < lo + plan.rows)

                @pl.when(here)
                def _(t=t, first=first, flat=flat, rows=rows):
                    act(first + t - lo, flat + 16 * t - start, 1, min(16, rows - 16 * t))


def to_tiles_kernel(plan, b, d_ref, window, out):
    out[...] = jnp.zeros(out.shape, out.dtype)

    def act(tile, row, stride, rows):
        value = window[pl.ds(row, rows, stride=stride), :]
        if rows < 16:
            value = jnp.concatenate([value, jnp.zeros((16 - rows, 128), value.dtype)], axis=0)
        out[tile] = value.astype(out.dtype)

    each_tile(plan, b, d_ref[0], act)


def from_tiles_kernel(plan, b, d_ref, tiles, window):
    window[...] = jnp.zeros(window.shape, window.dtype)

    def act(tile, row, stride, rows):
        window[pl.ds(row, rows, stride=stride), :] = tiles[tile][:rows]

    each_tile(plan, b, d_ref[0], act)


def by_stream(kernel, plan, text, d, value, shape, dtype, name):
    def call(b):
        def run(d, value):
            return pl.pallas_call(
                functools.partial(kernel, plan, b),
                out_shape=jax.ShapeDtypeStruct(shape, dtype),
                in_specs=[pl.BlockSpec(memory_space=pltpu.SMEM), pl.BlockSpec(memory_space=pltpu.VMEM)],
                out_specs=pl.BlockSpec(memory_space=pltpu.VMEM),
                compiler_params=pltpu.CompilerParams(vmem_limit_bytes=24 * 2**20),
                name=name,
            )(d, value)

        return run

    return lax.cond(text, call(plan.blocks[0]), call(plan.blocks[1]), d, value)


def shifted(value, axis, by):
    n = lax.axis_size(axis)
    return lax.ppermute(value, axis, [(i, i + by) for i in range(n) if 0 <= i + by < n])


def to_tiles(plan, text, d, flat):
    own = flat.reshape(plan.shard, 128)
    before = shifted(own[plan.shard - plan.before :], "dp", 1)
    after = shifted(own[: plan.after], "dp", -1)
    rest = jnp.zeros((plan.window - plan.before - plan.shard - plan.after, 128), own.dtype)
    window = jnp.concatenate([before, own, after, rest], axis=0)
    return by_stream(to_tiles_kernel, plan, text, d, window, (plan.rows, 16, 128), BF16, "to_tiles")


def from_tiles(plan, text, d, tiles):
    window = by_stream(from_tiles_kernel, plan, text, d, tiles, (plan.window, 128), F32, "from_tiles")
    end = plan.before + plan.shard
    own = window[plan.before : end]
    mine = shifted(window[end : end + plan.after], "dp", 1)
    own = own.at[: plan.after].add(mine)
    mine = shifted(window[: plan.before], "dp", -1)
    return own.at[plan.shard - plan.before :].add(mine).reshape(-1)


def gathered(plan, text, flat):
    whole = lax.all_gather(flat.astype(BF16), "dp", axis=0, tiled=True).reshape(-1, 128)
    index = jnp.where(text, *[jnp.asarray(plan.table(b)) for b in plan.blocks])
    rows = jnp.where((index >= 0)[:, None], whole[jnp.maximum(index, 0)], jnp.zeros((), BF16))
    return rows.reshape(plan.tiles, 16, 128)


def scattered(plan, text, tiles, flat_rows):
    tables = []
    for b in plan.blocks:
        table = plan.table(b)
        back = np.full((flat_rows,), -1, np.int32)
        held = np.nonzero(table >= 0)[0]
        back[table[held]] = held
        tables.append(jnp.asarray(back))
    index = jnp.where(text, *tables)
    rows = jnp.where((index >= 0)[:, None], tiles.reshape(-1, 128)[jnp.maximum(index, 0)], jnp.zeros((), BF16))
    return lax.psum_scatter(rows.astype(F32), "dp", scatter_dimension=0, tiled=True).reshape(-1)


def layer(text, counts, own, partner, grad, wco, wsa):
    seqs = own.shape[0]
    co, sa = blocks_of(text, seqs)
    box = own.shape
    lens = counts if text else counts[::-1]
    out, own_grad, sent, gco, gsa = compute(
        co, sa, lens, own.reshape(co.rows, co.width), partner.reshape(co.other_rows, co.other),
        grad.reshape(co.rows, co.width), wco, wsa)
    return out.reshape(box), own_grad.reshape(box), sent.reshape(box), gco, gsa


def body(devices, states, out_grad, co_params, self_params, text_lengths, region_counts):
    own = states[0]
    seqs = own.shape[0]
    text = lax.axis_index("stream") == 0
    d = lax.axis_index("dp").astype(jnp.int32).reshape(1)
    kinds = [[blocks_of(t, seqs)[i] for t in (True, False)] for i in range(2)]
    flats = (co_params[0], self_params[0])
    plans = [Plan(k, devices, f.shape[0] * devices) for k, f in zip(kinds, flats)]
    line = devices // 4
    near = devices % 4 == 0 and line <= LINE_MAX and all(p.before <= p.shard and p.after <= p.shard for p in plans)
    swap = [(0, 1), (1, 0)]
    partner = lax.ppermute(own, "stream", swap)
    if near:
        tiles = [to_tiles(p, text, d, f) for p, f in zip(plans, flats)]
        wco = gather(tiles[0], line, 1, "gather_co").reshape(plans[0].tiles, 16, 128)
        wsa = gather(tiles[1], line, 2, "gather_self").reshape(plans[1].tiles, 16, 128)
    else:
        wco, wsa = [gathered(p, text, f) for p, f in zip(plans, flats)]
    counts = jnp.stack([text_lengths, region_counts])
    out, own_grad, sent, gco, gsa = lax.cond(
        text, functools.partial(layer, True), functools.partial(layer, False),
        counts, own, partner, out_grad[0], wco, wsa)
    returned = lax.ppermute(sent, "stream", swap)
    grads = []
    for plan, g, cid, name in ((plans[1], gsa, 3, "scatter_self"), (plans[0], gco, 4, "scatter_co")):
        if near:
            block = scatter(g.reshape(line, 2, 2, plan.rows, 16, 128), line, cid, name)
            grads.append(from_tiles(plan, text, d, block))
        else:
            grads.append(scattered(plan, text, g, plan.shard * devices))
    states_grad = own_grad + returned.astype(F32)
    return (out[None], states_grad[None], grads[1][None], grads[0][None])


def solution(mesh):
    states = P("stream", "dp", None, None)
    flat = P("stream", "dp")
    return jax.shard_map(
        functools.partial(body, mesh.shape["dp"]), mesh=mesh, in_specs=(states, states, flat, flat, P("dp"), P("dp")),
        out_specs=(states, states, flat, flat), check_vma=False)
```

```python
import functools
import math

import jax
import jax.numpy as jnp
import numpy as np
from jax import lax
from jax.experimental import pallas as pl
from jax.experimental.pallas import tpu as pltpu
from jax.sharding import PartitionSpec as P


MESH_ID = pl.DeviceIdType.MESH
UNITS = 6


def place(line):
    d = lax.axis_index("dp")
    return d // 4, lax.rem(d // 2, 2), lax.rem(d, 2)


F32, BF16 = jnp.float32, jnp.bfloat16
NT = (((1,), (1,)), ((), ()))
TN = (((0,), (0,)), ((), ()))
norm_eps = 1e-12
masked_score = -1000000000.0
other_sequence = -3.0e38


def dot(a, b, dims=(((1,), (0,)), ((), ()))):
    return lax.dot_general(a, b, dims, preferred_element_type=F32)


class Block:
    def __init__(self, width, other, inner, hidden, heads, length, other_length, seqs, base=0):
        self.width, self.other, self.inner, self.hidden, self.heads = width, other, inner, hidden, heads
        self.length, self.other_length, self.seqs = length, other_length, seqs
        self.rows, self.other_rows = length * seqs, other_length * seqs
        self.base = base
        self.place = {}
        self.parts = []
        tile, flat = 0, 0

        def matrix(name, k, n):
            nonlocal tile, flat
            self.place[name] = (tile, k, n)
            self.parts.append((tile, flat, k, k * n // 128, n // 128))
            tile, flat = tile + k * n // 2048, flat + k * n // 128

        def vectors(*names):
            nonlocal tile, flat
            rows = 0
            for name, size in names:
                self.place[name] = (tile, rows, size)
                rows += size // 128
            self.parts.append((tile, flat, 0, rows, 0))
            tile, flat = tile + (rows + 15) // 16, flat + rows

        matrix("q_w", width, inner)
        vectors(("q_b", inner))
        matrix("k_w", other, inner)
        matrix("v_w", other, inner)
        vectors(("v_b", inner))
        matrix("o_w", inner, width)
        vectors(("o_b", width), ("g1", width), ("b1", width))
        matrix("i_w", width, hidden)
        vectors(("i_b", hidden))
        matrix("f_w", hidden, width)
        vectors(("f_b", width), ("g2", width), ("b2", width))
        self.tiles, self.flat_rows = tile, flat


VECS = ("q_b", "v_b", "o_b", "g1", "b1", "i_b", "f_b", "g2", "b2")
GROUPS = (("q_b",), ("v_b",), ("o_b", "g1", "b1"), ("i_b",), ("f_b", "g2", "b2"))


class Cols:
    def __init__(self, j, size):
        self.j, self.size = j, size

    def ds(self):
        return pl.ds(pl.multiple_of(self.j * self.size, self.size), self.size)


def cols(j, size=256):
    return Cols(j, size)


class Pooled:
    def __init__(self, pool, base, rows, width):
        self.pool, self.base, self.rows, self.count = pool, base, rows, width // 128

    def spots(self, index):
        if index is Ellipsis:
            first, count = 0, self.count
        else:
            run = index[1]
            count = run.size // 128
            first = run.j * count
        return [pl.ds(pl.multiple_of(self.base + (first + i) * self.rows, 8), self.rows) for i in range(count)]

    def __getitem__(self, index):
        return jnp.concatenate([self.pool[spot, :] for spot in self.spots(index)], axis=1)

    def __setitem__(self, index, value):
        for i, spot in enumerate(self.spots(index)):
            self.pool[spot, :] = value[:, i * 128 : (i + 1) * 128]


class View:
    def __init__(self, ref, shape):
        self.ref, self.shape = ref, tuple(shape)

    def whole(self, index):
        index = () if index is Ellipsis else index if isinstance(index, tuple) else (index,)
        index = index + (slice(None),) * (len(self.shape) - len(index))
        index = [i.ds() if isinstance(i, Cols) else i for i in index]
        return tuple(slice(0, k) if isinstance(i, slice) and i == slice(None) else i for i, k in zip(index, self.shape))

    def __getitem__(self, index):
        return self.ref[self.whole(index)]

    def __setitem__(self, index, value):
        self.ref[self.whole(index)] = value


class Net:
    def __init__(self, b, w, vec, sc):
        self.b, self.w, self.vec, self.s = b, w, vec, sc

    def mat(self, name):
        tile, k, n = self.b.place[name]
        return self.w.at[pl.ds(self.b.base + tile, k * n // 2048)].reshape(k // 16, n // 128, 16, 128)

    def row(self, name, j=None):
        k = VECS.index(name)
        size = self.b.place[name][2]
        return self.vec[k : k + 1, :size] if j is None else self.vec[k : k + 1, cols(j).ds()]

    def load_vectors(self):
        for group in GROUPS:
            tile = self.b.place[group[0]][0]
            rows = sum(self.b.place[g][2] for g in group) // 128
            count = (rows + 15) // 16
            value = self.w[pl.ds(self.b.base + tile, count)].reshape(count * 16, 128).astype(F32)
            r = 0
            for name in group:
                k = VECS.index(name)
                for j in range(self.b.place[name][2] // 128):
                    self.vec[k : k + 1, j * 128 : (j + 1) * 128] = value[r : r + 1]
                    r += 1

    def store_vectors(self, group, scratch):
        tile = self.b.place[group[0]][0]
        rows = sum(self.b.place[g][2] for g in group) // 128
        count = (rows + 15) // 16
        scratch[0 : count * 16] = jnp.zeros((count * 16, 128), F32)
        r = 0
        for name in group:
            k = VECS.index(name)
            for j in range(self.b.place[name][2] // 128):
                scratch[r : r + 1, :] = self.vec[k : k + 1, j * 128 : (j + 1) * 128]
                r += 1
        self.w[pl.ds(self.b.base + tile, count)] = scratch[0 : count * 16].astype(BF16).reshape(count, 16, 128)

    def nn(self, x, name, put, step=256):
        m = self.mat(name)
        k, n = self.b.place[name][1:]

        def body(j, carry):
            per = step // 128
            w = jnp.concatenate([m[:, per * j + i].reshape(k, 128) for i in range(per)], axis=1)
            put(j, dot(x[...], w))
            return carry

        lax.fori_loop(0, n // step, body, 0)

    def nt(self, g, name, put, step=256):
        m = self.mat(name)
        k, n = self.b.place[name][1:]

        def body(j, carry):
            strips = step // 16
            w = jnp.concatenate(
                [m[pl.ds(j * strips, strips), i].reshape(step, 128) for i in range(n // 128)], axis=1)
            put(j, dot(g[...], w, NT))
            return carry

        lax.fori_loop(0, k // step, body, 0)

    def tn(self, a, g, name, step=256):
        m = self.mat(name)
        k, n = self.b.place[name][1:]
        per = step // 128

        def body(j, carry):
            got = dot(a[...], g[:, cols(j, step)], TN).astype(BF16)
            for i in range(per):
                m[:, per * j + i] = got[:, i * 128 : (i + 1) * 128].reshape(k // 16, 16, 128)
            return carry

        lax.fori_loop(0, n // step, body, 0)

    def norm(self, r, gain, shift):
        centre = r - jnp.mean(r, axis=-1, keepdims=True)
        spread = jnp.mean(centre * centre, axis=-1, keepdims=True)
        return centre * lax.rsqrt(spread + norm_eps) * self.row(gain) + self.row(shift)

    def norm_back(self, r, dy, gain, shift):
        centre = r - jnp.mean(r, axis=-1, keepdims=True)
        spread = jnp.mean(centre * centre, axis=-1, keepdims=True)
        s = lax.rsqrt(spread + norm_eps)
        xh = centre * s
        t = dy * self.row(gain)
        dr = s * (t - jnp.mean(t, axis=-1, keepdims=True) - xh * jnp.mean(t * xh, axis=-1, keepdims=True))
        size = self.b.width
        kg, kb = VECS.index(gain), VECS.index(shift)
        self.vec[kg : kg + 1, :size] = jnp.sum(dy * xh, axis=0, keepdims=True)
        self.vec[kb : kb + 1, :size] = jnp.sum(dy, axis=0, keepdims=True)
        return dr

    def put_sum(self, name, ref):
        k = VECS.index(name)
        self.vec[k : k + 1, : self.b.place[name][2]] = jnp.sum(ref[...].astype(F32), axis=0, keepdims=True)

    def mask(self, fill, counts):
        b = self.b
        shape = (b.rows, b.other_rows)
        row = lax.broadcasted_iota(jnp.int32, shape, 0)
        col = lax.broadcasted_iota(jnp.int32, shape, 1)
        value = jnp.full(shape, other_sequence, F32)
        for q in range(b.seqs):
            mine = (row >= q * b.length) & (row < (q + 1) * b.length)
            mine = mine & (col >= q * b.other_length) & (col < (q + 1) * b.other_length)
            value = jnp.where(mine, jnp.where(col < q * b.other_length + counts(q), 1.0, masked_score), value)
        fill[...] = value

    def heads_of(self, refs, g):
        e = self.b.inner // self.b.heads
        values = [ref[:, cols(g, 128)] for ref in refs]
        if e == 128:
            return [values]
        lane = lax.broadcasted_iota(jnp.int32, (1, 128), 1)
        return [
            [jnp.where((lane >= h * e) & (lane < (h + 1) * e), value, jnp.zeros((), BF16)) for value in values]
            for h in range(128 // e)]

    def attend(self, q, k, v, fill, p, c):
        b = self.b
        e = b.inner // b.heads
        scale = 1.0 / math.sqrt(e)
        per = max(128 // e, 1)

        def body(g, carry):
            keys = k[:, cols(g, 128)]
            total = None
            for h, (qh,) in enumerate(self.heads_of([q], g)):
                vh = self.heads_of([v], g)[h][0]
                s = dot(qh, keys, NT) * scale
                f = fill[...]
                s = jnp.where(f > 0, s, f)
                ex = jnp.exp(s - jnp.max(s, axis=-1, keepdims=True))
                probs = (ex * (1.0 / jnp.sum(ex, axis=-1, keepdims=True))).astype(BF16)
                p[g * per + h] = probs
                got = dot(probs, vh)
                total = got if total is None else total + got
            c[:, cols(g, 128)] = total.astype(BF16)
            return carry

        lax.fori_loop(0, b.inner // 128, body, 0)

    def attend_back(self, q, k, v, p, dc):
        b = self.b
        e = b.inner // b.heads
        scale = 1.0 / math.sqrt(e)
        per = max(128 // e, 1)

        def body(g, carry):
            values = v[:, cols(g, 128)]
            sums = None
            for h, (qh, kh, dh) in enumerate(self.heads_of([q, k, dc], g)):
                probs = p[g * per + h]
                dp = dot(dh, values, NT)
                wide = probs.astype(F32)
                ds = (wide * (dp - jnp.sum(wide * dp, axis=-1, keepdims=True))).astype(BF16)
                got = [dot(ds, kh), dot(ds, qh, TN), dot(probs, dh, TN)]
                sums = got if sums is None else [x + y for x, y in zip(sums, got)]
            q[:, cols(g, 128)] = (sums[0] * scale).astype(BF16)
            k[:, cols(g, 128)] = (sums[1] * scale).astype(BF16)
            v[:, cols(g, 128)] = sums[2].astype(BF16)
            return carry

        lax.fori_loop(0, b.inner // 128, body, 0)

    def forward(self, x, u, z, counts, tick=lambda k=1: None):
        s, b = self.s, self.b
        self.load_vectors()
        self.mask(s["fill"], counts)

        def put(ref, bias=None):
            def store(j, value):
                if bias is not None:
                    value = value + self.row(bias, j)
                ref[:, cols(j)] = value.astype(BF16)
            return store

        tick()
        self.nn(u, "q_w", put(s["q"], "q_b"))
        self.nn(z, "k_w", put(s["k"]))
        tick()
        self.nn(z, "v_w", put(s["v"], "v_b"))
        tick()
        self.attend(s["q"], s["k"], s["v"], s["fill"], s["p"], s["c"])

        tick()

        def first(j, value):
            s["r1"][:, cols(j)] = x[:, cols(j)].astype(F32) + (value + self.row("o_b", j))

        self.nn(s["c"], "o_w", first)
        y1 = self.norm(s["r1"][...], "g1", "b1")
        s["r2"][...] = y1
        s["y1"][...] = y1.astype(BF16)

        def up(j, value):
            value = value + self.row("i_b", j)
            half = 0.5 * (1.0 + lax.erf(value * (1.0 / math.sqrt(2.0))))
            s["a"][:, cols(j)] = (value * half).astype(BF16)
            s["gp"][:, cols(j)] = (half + value * (jnp.exp(-0.5 * value * value) * (1.0 / math.sqrt(2.0 * math.pi)))).astype(BF16)

        tick()
        self.nn(s["y1"], "i_w", up)
        tick()

        def second(j, value):
            s["r2"][:, cols(j)] = s["r2"][:, cols(j)] + (value + self.row("f_b", j))

        self.nn(s["a"], "f_w", second)
        return self.norm(s["r2"][...], "g2", "b2")

    def backward(self, dy, u, z, put_resid, put_z, done, tick=lambda k=1: None):
        s, b = self.s, self.b
        small = s["small"]
        dr2 = self.norm_back(s["r2"][...], dy[...], "g2", "b2")
        dy[...] = dr2
        s["m"][...] = dr2.astype(BF16)
        self.put_sum("f_b", s["m"])

        def inner(j, value):
            s["gp"][:, cols(j)] = (value * s["gp"][:, cols(j)].astype(F32)).astype(BF16)

        self.nt(s["m"], "f_w", inner)
        self.store_vectors(GROUPS[4], small)
        self.tn(s["a"], s["m"], "f_w")
        done("f_w")
        tick()
        self.put_sum("i_b", s["gp"])

        def mid(j, value):
            dy[:, cols(j)] = dy[:, cols(j)] + value

        self.nt(s["gp"], "i_w", mid)
        tick()
        self.store_vectors(GROUPS[3], small)
        self.tn(s["y1"], s["gp"], "i_w")
        done("i_w")
        tick()
        dr1 = self.norm_back(s["r1"][...], dy[...], "g1", "b1")
        dy[...] = dr1
        s["m"][...] = dr1.astype(BF16)
        self.put_sum("o_b", s["m"])

        def context(j, value):
            s["dc"][:, cols(j)] = value.astype(BF16)

        self.nt(s["m"], "o_w", context)
        self.store_vectors(GROUPS[2], small)
        self.tn(s["c"], s["m"], "o_w")
        done("o_w")
        tick(2)
        self.attend_back(s["q"], s["k"], s["v"], s["p"], s["dc"])

        tick(2)

        def resid(j, value):
            put_resid(j, dy[:, cols(j)] + value)

        self.nt(s["q"], "q_w", resid)
        m = self.mat("v_w")
        mk = self.mat("k_w")
        k, n = b.place["v_w"][1:]

        def body(j, carry):
            def rows_of(mm):
                return jnp.concatenate([mm[pl.ds(j * 16, 16), i].reshape(256, 128) for i in range(n // 128)], axis=1)
            put_z(j, dot(s["k"][...], rows_of(mk), NT) + dot(s["v"][...], rows_of(m), NT))
            return carry

        lax.fori_loop(0, k // 256, body, 0)
        tick()
        self.put_sum("q_b", s["q"])
        self.put_sum("v_b", s["v"])
        self.store_vectors(GROUPS[0], small)
        self.store_vectors(GROUPS[1], small)
        self.tn(u, s["q"], "q_w")
        self.tn(z, s["k"], "k_w")
        self.tn(z, s["v"], "v_w")
        done("q_w")
        tick()


def scratch_of(b):
    return {
        "q": ((b.rows, b.inner), BF16), "k": ((b.other_rows, b.inner), BF16), "v": ((b.other_rows, b.inner), BF16),
        "p": ((b.heads, b.rows, b.other_rows), BF16), "c": ((b.rows, b.inner), BF16),
        "r1": ((b.rows, b.width), F32), "r2": ((b.rows, b.width), F32), "y1": ((b.rows, b.width), BF16),
        "a": ((b.rows, b.hidden), BF16), "gp": ((b.rows, b.hidden), BF16), "fill": ((b.rows, b.other_rows), F32)}


def compute_kernel(co, sa, lens, x, xp, gy, wco, wsa, out, own_grad, sent, gco, gsa, wc, ws, vec, vec2, small, sems, *scr):
    names = sorted(scratch_of(co))
    sc = dict(zip(names, scr[: len(names)]))
    ss = dict(zip(names, scr[len(names) : 2 * len(names)]))
    rest = scr[2 * len(names) :]
    m, dy, h, hb, dcc, dcs = rest
    for d, dc in ((sc, dcc), (ss, dcs)):
        d["m"], d["small"], d["dc"] = m, small, dc
    x, xp = View(x, (co.rows, co.width)), View(xp, (co.other_rows, co.other))
    own_grad, sent = View(own_grad, (co.rows, co.width)), View(sent, (co.other_rows, co.other))
    h, hb, dy = [View(r, (co.rows, co.width)) for r in (h, hb, dy)]
    for b, d in ((co, sc), (sa, ss)):
        shapes = {**{n: k[0] for n, k in scratch_of(b).items()}, "m": (b.rows, b.width), "dc": (b.rows, b.inner)}
        for n, shape in shapes.items():
            d[n] = View(d[n], shape)
    copies = [pltpu.make_async_copy(wco, wc, sems.at[0]), pltpu.make_async_copy(wsa, ws, sems.at[1])]
    for cp in copies:
        cp.start()
    copies[0].wait()
    a = Net(co, wc, vec, sc)
    bnet = Net(sa, ws, vec2, ss)
    value = a.forward(x, x, xp, lambda q: lens[1, q])
    h[...] = value
    hb[...] = value.astype(BF16)
    copies[1].wait()
    out[...] = bnet.forward(h, hb, hb, lambda q: lens[0, q]).astype(BF16)
    dy[...] = gy[...].astype(F32)

    def put_h(j, value):
        h[:, cols(j)] = value

    def add_h(j, value):
        h[:, cols(j)] = h[:, cols(j)] + value

    bnet.backward(dy, hb, hb, put_h, add_h, lambda name: None)
    back = pltpu.make_async_copy(ws, gsa, sems.at[1])
    back.start()

    def put_own(j, value):
        own_grad[:, cols(j)] = value

    def put_sent(j, value):
        sent[:, cols(j)] = value.astype(BF16)

    a.backward(h, x, xp, put_own, put_sent, lambda name: None)
    back2 = pltpu.make_async_copy(wc, gco, sems.at[0])
    back2.start()
    back.wait()
    back2.wait()


def compute(co, sa, lens, x, xp, gy, wco, wsa):
    any_ = pl.BlockSpec(memory_space=pl.ANY)
    vm = pl.BlockSpec(memory_space=pltpu.VMEM)
    names = sorted(scratch_of(co))
    V = lambda shape, dtype: pltpu.VMEM(shape, dtype)
    scr = [V(wco.shape, BF16), V(wsa.shape, BF16), V((16, 3072), F32), V((16, 3072), F32), V((32, 128), F32), pltpu.SemaphoreType.DMA((2,))]
    scr += [V(*scratch_of(co)[n]) for n in names] + [V(*scratch_of(sa)[n]) for n in names]
    rows, width = co.rows, co.width
    scr += [V((rows, width), BF16), V((rows, width), F32), V((rows, width), F32), V((rows, width), BF16)]
    scr += [V((b.rows, b.inner), BF16) for b in (co, sa)]
    return pl.pallas_call(
        functools.partial(compute_kernel, co, sa),
        out_shape=(jax.ShapeDtypeStruct((rows, width), BF16), jax.ShapeDtypeStruct((rows, width), F32),
                   jax.ShapeDtypeStruct((co.other_rows, co.other), BF16),
                   jax.ShapeDtypeStruct(wco.shape, BF16), jax.ShapeDtypeStruct(wsa.shape, BF16)),
        in_specs=[pl.BlockSpec(memory_space=pltpu.SMEM), vm, vm, vm, any_, any_],
        out_specs=(vm, vm, vm, any_, any_),
        scratch_shapes=scr,
        compiler_params=pltpu.CompilerParams(vmem_limit_bytes=63 * 2**20),
        name="compute",
    )(lens, x, xp, gy, wco, wsa)


PER = UNITS + 1
BEHIND = 4
LEAD = 3


class Where:
    def __init__(self, line):
        self.line, self.last = line, line - 1
        self.z, self.x, self.c = place(line)
        self.s = lax.axis_index("stream")

    def copy(self, src, dst, send, recv, z, x, c, s=None):
        return pltpu.make_async_remote_copy(
            src_ref=src, dst_ref=dst, send_sem=send, recv_sem=recv,
            device_id=(self.s if s is None else s, (z * 2 + x) * 2 + c), device_id_type=MESH_ID)

    def greet(self):
        z, x, c, s = self.z, self.x, self.c, self.s
        barrier = pltpu.get_barrier_semaphore()

        def signal(zz, xx, cc, ss):
            pl.semaphore_signal(barrier, inc=1, device_id=(ss, (zz * 2 + xx) * 2 + cc), device_id_type=MESH_ID)

        signal(z, 1 - x, c, s)
        signal(z, x, 1 - c, s)
        signal(z, x, c, 1 - s)
        d = (z * 2 + x) * 2 + c
        beside = (1 - c) * jnp.minimum(d, 1) + c * jnp.minimum(4 * self.line - 1 - d, 1)

        @pl.when(beside > 0)
        def _():
            pl.semaphore_signal(barrier, inc=1, device_id=(s, d - 1 + 2 * c), device_id_type=MESH_ID)

        @pl.when(z > 0)
        def _():
            signal(z - 1, x, c, s)

        @pl.when(z < self.last)
        def _():
            signal(z + 1, x, c, s)

        pl.semaphore_wait(barrier, 3 + jnp.minimum(z, 1) + jnp.minimum(self.last - z, 1) + beside)


class Gather:
    def __init__(self, at, rows, w, sems):
        self.at, self.rows, self.w = at, rows, w
        self.n = self.rows // UNITS
        self.up_s, self.dn_s, self.z_r, self.x_s, self.x_r, self.c_s, self.c_r, self.o_s = sems

    def spot(self, zo, xb, cc, u):
        return self.w.at[pl.ds(((zo * 2 + xb) * 2 + cc) * self.rows + u * self.n, self.n)]

    def block_of(self, v):
        x = self.at.x
        return jnp.where(v == UNITS, 1 - x, x), jnp.minimum(v, UNITS - 1)

    def z_copy(self, zo, v, up):
        at = self.at
        xb, u = self.block_of(v)
        spot = self.spot(zo, xb, at.c, u)
        return at.copy(spot, spot, (self.up_s if up else self.dn_s).at[zo], self.z_r.at[zo * PER + v], at.z + 1 if up else at.z - 1, at.x, at.c)

    def x_copy(self, zo, u, arriving=False, first=False):
        at = self.at
        spot = self.spot(zo, 1 - at.x if arriving else at.x, at.c, u)
        return at.copy(spot, spot, self.o_s if first else self.x_s.at[zo], self.x_r.at[zo * UNITS + u], at.z, 1 - at.x, at.c)

    def c_copy(self, zo, xb, u):
        at = self.at
        spot = self.spot(zo, xb, at.c, u)
        return at.copy(spot, spot, self.c_s.at[zo], self.c_r.at[zo], at.z, at.x, 1 - at.c)

    def send_z(self, zo, v, up):
        at = self.at

        @pl.when(at.z < at.last if up else at.z > 0)
        def _():
            self.z_copy(zo, v, up).start()

    def first(self):
        self.x_copy(self.at.z, UNITS - 1, first=True).start()

    def start(self, up):
        at = self.at
        z, x = at.z, at.x
        for u in range(UNITS - 1):
            self.x_copy(z, u).start()
            self.send_z(z, u, False)
            if up:
                self.send_z(z, u, True)
        self.send_z(z, UNITS - 1, False)
        if up:
            self.send_z(z, UNITS - 1, True)
        for u in range(UNITS):
            self.c_copy(z, x, u).start()

    def other_last(self, up):
        at = self.at
        self.x_copy(at.z, UNITS - 1, arriving=True).wait_recv()
        self.send_z(at.z, UNITS, False)
        if up:
            self.send_z(at.z, UNITS, True)
        self.c_copy(at.z, 1 - at.x, UNITS - 1).start()

    def onward(self, zo, v, up):
        xb, u = self.block_of(v)
        self.z_copy(zo, v, up).wait_recv()
        self.send_z(zo, v, up)

        @pl.when(v < UNITS - 1)
        def _():
            self.x_copy(zo, u).start()

        self.c_copy(zo, xb, u).start()

    def from_below(self, t):
        h, v = t // PER, lax.rem(t, PER)

        @pl.when(self.at.z > h)
        def _():
            self.onward(self.at.z - 1 - h, v, True)

    def from_above(self, t):
        h, v = t // PER, lax.rem(t, PER)

        @pl.when(self.at.z + h < self.at.last)
        def _():
            self.onward(self.at.z + 1 + h, v, False)

    def in_order(self, i):
        z = self.at.z
        zo, v = i // PER, lax.rem(i, PER)

        @pl.when(jnp.logical_and(i >= 0, zo < z))
        def _():
            self.onward(zo, v, True)

        @pl.when(jnp.logical_and(i >= 0, zo == z))
        def _():
            self.send_z(z, v, True)

    def x_arrival(self, zo, u):
        self.x_copy(zo, u, arriving=True).wait_recv()
        self.c_copy(zo, 1 - self.at.x, u).start()

    def beside_own(self):
        for u in range(UNITS - 1):
            self.x_arrival(self.at.z, u)

    def beside_far(self, t):
        at = self.at
        h, v = t // PER, lax.rem(t, PER)

        @pl.when(jnp.logical_and(t >= 0, v < UNITS - 1))
        def _():
            @pl.when(at.z > h)
            def _():
                self.x_arrival(at.z - 1 - h, v)

            @pl.when(at.z + h < at.last)
            def _():
                self.x_arrival(at.z + 1 + h, v)

    def beside_order(self, i):
        zo, v = i // PER, lax.rem(i, PER)

        @pl.when(jnp.logical_and(jnp.logical_and(i >= 0, v < UNITS - 1), zo < self.at.z))
        def _():
            self.x_arrival(zo, v)

    def beside_above(self, t):
        at = self.at
        h, v = t // PER, lax.rem(t, PER)

        @pl.when(jnp.logical_and(jnp.logical_and(t >= 0, v < UNITS - 1), at.z + h < at.last))
        def _():
            self.x_arrival(at.z + 1 + h, v)

    def arrived(self, zo):
        at = self.at
        spot = self.w.at[pl.ds(0, 2 * self.rows)]
        at.copy(spot, spot, self.o_s, self.c_r.at[zo], at.z, at.x, 1 - at.c).wait_recv()

    def sent(self):
        at = self.at
        z = at.z

        def wait(tiles, sem):
            spot = self.w.at[pl.ds(0, tiles)]
            at.copy(spot, spot, sem, self.c_r.at[0], z, at.x, 1 - at.c).wait_send()

        def each(zo, carry):
            @pl.when(jnp.logical_and(z < at.last, zo <= z))
            def _():
                wait(PER * self.n, self.up_s.at[zo])

            @pl.when(jnp.logical_and(z > 0, zo >= z))
            def _():
                wait(PER * self.n, self.dn_s.at[zo])

            wait((UNITS - 1) * self.n, self.x_s.at[zo])
            wait(2 * self.rows, self.c_s.at[zo])
            return carry

        lax.fori_loop(0, at.line, each, 0)
        wait(self.n, self.o_s)


def gather_sems(line):
    dma = pltpu.SemaphoreType.DMA
    return [dma((line,)), dma((line,)), dma((line * PER,)), dma((line,)), dma((line * UNITS,)), dma((line,)), dma((line,)), dma]


class Scatter:
    def __init__(self, at, g, rows, cr, xr, zr, keep, stage, wide_stage, behind, sems):
        self.at, self.g, self.rows, self.n = at, g, rows, rows // UNITS
        self.cr, self.xr, self.zr, self.keep, self.stage, self.wide = cr, xr, zr, keep, stage, wide_stage
        self.c_s, self.c_r, self.x_s, self.x_r, self.z_s, self.z_r, self.l_s, self.b_s = sems
        self.behind = behind
        self.items = at.last * PER
        self.final = self.items + LEAD + at.last + behind
        self.slots = self.final + PER

    def mine(self, zo, xb, u):
        return pl.ds(((zo * 2 + xb) * 2 + self.at.c) * self.rows + u * self.n, self.n)

    def block_of(self, v):
        x = self.at.x
        return jnp.where(v == 0, 1 - x, x), jnp.where(v == 0, UNITS - 1, v - 1)

    def c_copy(self, zo, xb):
        at = self.at
        src = self.g.at[pl.ds(((zo * 2 + xb) * 2 + 1 - at.c) * self.rows, self.rows)]
        k = zo * 2 + xb
        return at.copy(src, self.cr.at[k], self.c_s.at[zo], self.c_r.at[k], at.z, at.x, 1 - at.c)

    def x_copy(self, zo, u, last=False):
        at = self.at
        k = zo * UNITS + u
        return at.copy(self.g.at[self.mine(zo, 1 - at.x, u)], self.xr.at[k], self.b_s if last else self.x_s.at[zo], self.x_r.at[k],
                       at.z, 1 - at.x, at.c)

    def z_copy(self, to, v, up):
        at = self.at
        xb, u = self.block_of(v)
        there = at.z + 1 if up else at.z - 1
        k = (to if up else jnp.where(to == there, at.line, to)) * PER + v
        return at.copy(self.g.at[self.mine(to, xb, u)], self.zr.at[k], self.z_s.at[to], self.z_r.at[k], there, at.x, at.c)

    def z_wait(self, k):
        at = self.at
        spot = self.zr.at[k]
        at.copy(spot, spot, self.z_s.at[0], self.z_r.at[k], at.z, 1 - at.x, at.c).wait_recv()

    def ready(self, zo):
        for xb in range(2):
            self.c_copy(zo, xb).start()

    def load(self, src, slot):
        return pltpu.make_async_copy(src, self.stage.at[slot, pl.ds(0, self.n)], self.l_s.at[slot])

    def core_part(self, zo, xb, u):
        return self.cr.at[zo * 2 + xb, pl.ds(u * self.n, self.n)]

    def way(self, t, up):
        at = self.at
        i = t - (at.z if up else at.last - at.z + self.behind)
        to = (at.last if up else at.last - 1) - i // PER
        here = jnp.logical_and(jnp.logical_and(i >= 0, i < self.items), to > at.z if up else to < at.z)
        return to, lax.rem(i, PER), here

    def crossings(self, t):
        at = self.at
        found = []
        for up, slot in ((True, 0), (False, 11)):
            to, v, here = self.way(t, up)
            found.append((to, v - 1, jnp.logical_and(here, jnp.logical_and(v >= 1, v < UNITS)), slot))
        u = t - self.items - self.behind - 1
        found.append((at.z, u, jnp.logical_and(u >= 0, u < UNITS - 1), 0))
        return found

    def parts(self, t, finals):
        found = [self.way(t - LEAD, up) + (up, slot) for up, slot in ((True, 1), (False, 4))]
        own = t - self.final
        return found + [(self.at.z, own, jnp.logical_and(own >= 0, own < PER), None, 7)] * finals

    def prepare(self, t, finals=False):
        at = self.at
        for to, u, here, slot in self.crossings(t):
            @pl.when(here)
            def _(to=to, u=u, slot=slot):
                @pl.when(u == 0)
                def _():
                    for xb in range(2):
                        self.c_copy(to, xb).wait_recv()

                self.load(self.core_part(to, 1 - at.x, u), slot).start()

        for to, v, here, up, slot in self.parts(t, finals):
            @pl.when(here)
            def _(to=to, v=v, up=up, slot=slot):
                xb, u = self.block_of(v)
                self.load(self.core_part(to, xb, u), slot).start()

                @pl.when(jnp.logical_and(v >= 1, v < (UNITS if up is not None else PER)))
                def _():
                    self.x_copy(to, u).wait_recv()
                    self.load(self.xr.at[to * UNITS + u], slot + 1).start()

                if up is None:
                    @pl.when(at.z > 0)
                    def _():
                        self.z_wait(to * PER + v)
                        self.load(self.zr.at[to * PER + v], slot + 2).start()

                    @pl.when(at.z < at.last)
                    def _():
                        self.z_wait(at.line * PER + v)
                        self.load(self.zr.at[at.line * PER + v], slot + 3).start()
                else:
                    @pl.when(at.z != (0 if up else at.last))
                    def _():
                        self.z_wait(to * PER + v)
                        self.load(self.zr.at[to * PER + v], slot + 2).start()

    def take(self, slot):
        self.load(self.xr.at[0], slot).wait()
        return self.stage[slot].astype(F32)

    def act(self, t, finals):
        at = self.at
        for to, v, here, up, slot in self.parts(t, finals):
            @pl.when(here)
            def _(to=to, v=v, up=up, slot=slot):
                xb, u = self.block_of(v)
                spot = self.mine(to, xb, u)
                acc = self.wide

                acc[: self.n] = self.g[spot].astype(F32) + self.take(slot)

                def more(k):
                    acc[: self.n] = acc[: self.n] + self.take(slot + k)

                @pl.when(jnp.logical_and(v >= 1, v < (UNITS if up is not None else PER)))
                def _():
                    more(1)

                if up is None:
                    @pl.when(at.z > 0)
                    def _():
                        more(2)

                    @pl.when(at.z < at.last)
                    def _():
                        more(3)

                    @pl.when(v == 0)
                    def _():
                        self.g[spot] = acc[: self.n].astype(BF16)
                        self.x_copy(to, UNITS - 1, True).start()

                    @pl.when(v >= 1)
                    def _():
                        self.keep(u)
                else:
                    @pl.when(at.z != (0 if up else at.last))
                    def _():
                        more(2)

                    self.g[spot] = acc[: self.n].astype(BF16)
                    self.z_copy(to, v, up).start()

        for to, u, here, slot in self.crossings(t):
            @pl.when(here)
            def _(to=to, u=u, slot=slot):
                spot = self.mine(to, 1 - at.x, u)
                self.g[spot] = (self.g[spot].astype(F32) + self.take(slot)).astype(BF16)
                self.x_copy(to, u).start()

    def slot(self, t, finals=False):
        self.act(t, finals)
        self.prepare(t + 1, finals)

    def sent(self):
        at = self.at
        z = at.z

        def wait(tiles, sem):
            spot = self.g.at[pl.ds(0, tiles)]
            at.copy(spot, spot, sem, self.c_r.at[0], z, at.x, 1 - at.c).wait_send()

        def each(zo, carry):
            @pl.when(zo != z)
            def _():
                wait(PER * self.n, self.z_s.at[zo])

            wait((UNITS - 1) * self.n, self.x_s.at[zo])
            wait(2 * self.rows, self.c_s.at[zo])
            return carry

        lax.fori_loop(0, at.line, each, 0)
        wait(self.n, self.b_s)


def scatter_sems(line):
    dma = pltpu.SemaphoreType.DMA
    return [dma((line,)), dma((line * 2,)), dma((line,)), dma((line * UNITS,)), dma((line,)), dma(((line + 1) * PER,)), dma((12,)), dma]


def landing(line, rows):
    n = rows // UNITS
    shape = lambda *s: jax.ShapeDtypeStruct(s + (16, 128), BF16)
    return [shape(line * 2, rows), shape(line * UNITS, n), shape((line + 1) * PER, n)]


class Edges:
    def __init__(self, at, plan, window, first, spare, land, sems):
        self.at, self.plan, self.window, self.first, self.spare, self.land = at, plan, window, first, spare, land
        self.f_s, self.f_r, self.l_s, self.e_s, self.e_r = sems
        self.d = (at.z * 2 + at.x) * 2 + at.c
        self.end = plan.before + plan.shard

    def over(self, src, dst, send, recv, by):
        return pltpu.make_async_remote_copy(
            src_ref=src, dst_ref=dst, send_sem=send, recv_sem=recv, device_id=(self.at.s, self.d + by), device_id_type=MESH_ID)

    def both(self, up, down):
        @pl.when(self.d < 4 * self.at.line - 1)
        def _():
            up()

        @pl.when(self.d > 0)
        def _():
            down()

    def lands(self, ref):
        plan = self.plan
        return ref.at[pl.ds(0, plan.before)], ref.at[pl.ds(plan.before, plan.after)]

    def outer(self, own):
        plan = self.plan
        before, after = self.lands(self.first)
        return (self.over(own.at[pl.ds(plan.shard - plan.before, plan.before), 0], before, self.f_s.at[0], self.f_r.at[0], 1),
                self.over(own.at[pl.ds(0, plan.after), 0], after, self.f_s.at[1], self.f_r.at[1], -1))

    def send(self, own):
        up, down = self.outer(own)
        self.both(up.start, down.start)

    def inner(self, own):
        return pltpu.make_async_copy(own.at[:, 0], self.window.at[pl.ds(self.plan.before, self.plan.shard)], self.l_s)

    def tiles(self, kinds, own, w):
        plan = self.plan
        up, down = self.outer(own)
        lo = plan.rows * self.d
        w[pl.ds(lo, plan.rows)] = jnp.zeros((plan.rows, 16, 128), w.dtype)

        def above():
            down.wait_recv()
            self.window[self.end : self.end + plan.after, :] = self.first[plan.before : plan.before + plan.after, :]

        def below():
            up.wait_recv()
            self.window[: plan.before, :] = self.first[: plan.before, :]

        self.both(above, below)
        self.inner(own).wait()

        def act(tile, row, stride, rows):
            value = self.window[pl.ds(row, rows, stride=stride), :]
            if rows < 16:
                value = jnp.concatenate([value, jnp.zeros((16 - rows, 128), value.dtype)], axis=0)
            w[tile] = value.astype(w.dtype)

        self.by_stream(kinds, lo, lo + plan.rows, act)
        self.both(up.wait_send, down.wait_send)

    def by_stream(self, kinds, lo, hi, act):
        start = self.plan.shard * self.d - self.plan.before
        for s, b in enumerate(kinds):
            @pl.when(self.at.s == s)
            def _(b=b):
                each_tile(b, lo, hi, start, act)

    def clear(self):
        self.window[...] = jnp.zeros(self.window.shape, F32)

    def take(self, kinds, acc, n):
        def keep(u):
            lo = self.plan.rows * self.d + u * n

            def act(tile, row, stride, rows):
                self.window[pl.ds(row, rows, stride=stride), :] = acc[tile - lo][:rows]

            self.by_stream(kinds, lo, lo + n, act)

        return keep

    def back(self):
        plan = self.plan
        front, rear = self.lands(self.land)
        return (self.over(self.spare.at[pl.ds(0, plan.after)], rear, self.e_s.at[0], self.e_r.at[0], 1),
                self.over(self.window.at[pl.ds(0, plan.before)], front, self.e_s.at[1], self.e_r.at[1], -1))

    def give(self):
        self.spare[: self.plan.after, :] = self.window[self.end : self.end + self.plan.after, :]
        up, down = self.back()
        self.both(up.start, down.start)

    def finish(self, out):
        plan = self.plan
        up, down = self.back()

        def above():
            down.wait_recv()
            spot = slice(self.end - plan.before, self.end)
            self.window[spot, :] = self.window[spot, :] + self.land[: plan.before, :]

        def below():
            up.wait_recv()
            spot = slice(plan.before, plan.before + plan.after)
            self.window[spot, :] = self.window[spot, :] + self.land[plan.before : plan.before + plan.after, :]

        self.both(above, below)
        self.leave(out).start()

    def leave(self, out):
        return pltpu.make_async_copy(self.window.at[pl.ds(self.plan.before, self.plan.shard)], out.at[:, 0], self.l_s)

    def done(self, out):
        self.leave(out).wait()
        up, down = self.back()
        self.both(up.wait_send, down.wait_send)


def edge_sems():
    dma = pltpu.SemaphoreType.DMA
    return [dma((2,)), dma((2,)), dma, dma((2,)), dma((2,))]


def to_flat(flat, box):
    count = box.shape[1] // 128
    for b in range(count):
        flat[pl.ds(b, box.shape[0], stride=count), :] = box[:, b * 128 : (b + 1) * 128].astype(F32)


def from_flat(flat, rows, count, put):
    for j in range(count):
        put(j, flat[pl.ds(j, rows, stride=count), :])


def layer_kernel(plans, line, lens, xbox, gbox, co_flat, sa_flat, *refs):
    kinds = list(zip(plans[0].blocks, plans[1].blocks))
    outs, refs = refs[:10], refs[10:]
    out_box, grad_box, co_out, sa_out = outs[:4]
    wc, ws, vec, vec2, small, pool, land, xp, xin, ret, stage_c, stage_s, acc = refs[:13]
    refs = refs[13:]
    names = sorted(KEPT)
    sc = dict(zip(names, refs[: len(names)]))
    refs = refs[len(names) :]
    ss = dict(zip(names, refs[: len(names)]))
    refs = refs[len(names) :]
    shared = dict(zip(sorted(SHARED), refs[: len(SHARED)]))
    refs = refs[len(SHARED) :]
    ag_c, ag_s, rs_c, rs_s, ed_c, ed_s, y_s, y_r = refs[:8], refs[8:16], refs[16:24], refs[24:32], refs[32:37], refs[37:42], refs[42], refs[43]
    sent = shared["dc"]
    span = pool_span(plans)
    flat = pool.at[pl.ds(6 * span, span)]

    at = Where(line)
    last = at.last
    gc, gs = Gather(at, plans[0].rows, wc, ag_c), Gather(at, plans[1].rows, ws, ag_s)
    edges = []
    rest = max(p.window for p in plans)
    for k, (p, sems) in enumerate(zip(plans, (ed_c, ed_s))):
        sizes = [q.before + q.after for q in plans]
        edges.append(Edges(at, p, pool.at[pl.ds(0, p.window)], pool.at[pl.ds(rest + k * sizes[0], sizes[k])], pool.at[pl.ds(rest, p.after)],
                           land.at[pl.ds(k * sizes[0], sizes[k])], sems))
    ec, es = edges
    own_kinds = [[k[i] for k in kinds] for i in range(2)]
    rc = Scatter(at, wc, plans[0].rows, *outs[4:7], ec.take(own_kinds[0], acc, gc.n), stage_c, acc, 0, rs_c)
    rs = Scatter(at, ws, plans[1].rows, *outs[7:10], es.take(own_kinds[1], acc, gs.n), stage_s, acc, BEHIND, rs_s)

    def over(k, src, dst):
        return at.copy(src, dst, y_s.at[k], y_r.at[k], at.z, at.x, at.c, 1 - at.s)

    ec.inner(co_flat).start()
    at.greet()
    ec.send(co_flat)
    es.send(sa_flat)
    ec.tiles(own_kinds[0], co_flat, wc)
    gc.first()
    gc.start(True)
    es.inner(sa_flat).start()
    states = over(0, xbox, xp)
    states.start()
    es.tiles(own_kinds[1], sa_flat, ws)
    gs.first()
    gc.other_last(True)

    steps = PER * last
    early = PER

    def co_step(t, carry):
        gc.from_below(t)
        gc.from_above(t)

        @pl.when(t < UNITS - 1)
        def _():
            gc.x_arrival(at.z, t)

        gc.beside_far(t - PER)

        @pl.when(jnp.logical_and(t >= steps - early, at.z < last))
        def _():
            gs.in_order(t - (steps - early) - at.z)

        return carry

    lax.fori_loop(0, steps - early, co_step, 0)
    gs.start(False)
    gs.other_last(False)
    lax.fori_loop(steps - early, steps, co_step, 0)

    def co_rest(t, carry):
        gc.beside_far(t)
        return carry

    lax.fori_loop(steps - PER, steps, co_rest, 0)
    gs.beside_own()
    for zo in range(line):
        gc.arrived(zo)
    states.wait_recv()

    ahead = jnp.where(at.z < last, early - at.z, 0)

    def self_step(t, carry):
        gs.in_order(t + ahead)
        gs.from_above(t)
        self_beside(t - PER)
        return carry

    def self_beside(t):
        gs.beside_order(t + ahead)
        gs.beside_above(t)

    def self_steps(a, b):
        lax.fori_loop(a, b, self_step, 0)

    gather_steps = steps
    scatter_ticks = 20

    def run(text, co, sa):
        rows, width = co.rows, co.width

        def view(refs, b):
            d = {name: View(ref, kept_shapes(b)[name]) for name, ref in refs.items()}
            for name, ref in shared.items():
                d[name] = View(ref, shared_shapes(b)[name])
            for k, name in enumerate(("r1", "r2")):
                d[name] = Pooled(pool, (2 * (b is sa) + k) * span, b.rows, b.width)
            d["h"], d["dy"] = [Pooled(pool, k * span, b.rows, b.width) for k in (4, 5)]
            d["small"] = small
            return d

        a = Net(co, wc, vec, view(sc, co))
        b = Net(sa, ws, vec2, view(ss, sa))
        h, hb, dy = b.s["h"], b.s["hb"], b.s["dy"]

        own_in = View(xin, (rows, width))
        if text:
            to_flat(flat, xbox)

            def put(j, value):
                own_in[:, cols(j, 128)] = value.astype(BF16)

            from_flat(flat, rows, width // 128, put)
            x, z = own_in, View(xp, xp.shape)
        else:
            to_flat(flat, xp)
            other = View(xin, (co.other_rows, co.other))

            def put(j, value):
                other[:, cols(j, 128)] = value.astype(BF16)

            from_flat(flat, co.other_rows, co.other // 128, put)
            x, z = View(xbox, xbox.shape), other

        done_steps = [0]

        def tick(k=1):
            a0 = done_steps[0]
            self_steps(a0, a0 + k)
            done_steps[0] = a0 + k

        value = a.forward(x, x, z, lambda q: lens[1, q], tick)
        h[...] = value
        hb[...] = value.astype(BF16)
        gc.sent()
        if done_steps[0] < gather_steps:
            self_steps(done_steps[0], gather_steps)
        marks = [gather_steps - PER]

        def tick_late(k=1):
            a0 = marks[0]
            b0 = min(a0 + k, gather_steps)
            marks[0] = b0
            if b0 > a0:
                lax.fori_loop(a0, b0, lambda t, carry: (self_beside(t), carry)[1], 0)

        tick_late(PER)
        for zo in range(line):
            gs.arrived(zo)
        value = b.forward(h, hb, hb, lambda q: lens[0, q], lambda k=1: None)
        gs.sent()

        def box_out(dst, value_ref, dtype):
            for j in range(width // 128):
                flat[pl.ds(j, rows, stride=width // 128), :] = value_ref[:, cols(j, 128)]

            def put(j, value):
                dst[:, j * 128 : (j + 1) * 128] = value.astype(dtype)

            from_flat(flat, dst.shape[0], dst.shape[1] // 128, put)

        if text:
            dy[...] = value
            box_out(out_box, dy, BF16)
            to_flat(flat, gbox)

            def put(j, value):
                dy[:, cols(j, 128)] = value

            from_flat(flat, rows, width // 128, put)
        else:
            out_box[...] = value.astype(BF16)
            dy[...] = gbox[...].astype(F32)

        def put_h(j, value):
            h[:, cols(j)] = value

        def add_h(j, value):
            h[:, cols(j)] = h[:, cols(j)] + value

        ticks = [0]

        def hooks(scatter, block):
            state = [line]

            def done(name):
                tile = block.place[name][0]
                ready = -(-tile // (4 * scatter.rows))
                while state[0] > ready:
                    state[0] -= 1
                    scatter.ready(state[0])
                    if scatter is rs and state[0] == last:
                        rs.prepare(0)

            return done

        def rs_tick(k=1):
            a0 = ticks[0]
            ticks[0] = a0 + k
            lax.fori_loop(a0, a0 + k, lambda t, carry: (rs.slot(t), carry)[1], 0)

        b.backward(dy, hb, hb, put_h, add_h, hooks(rs, sa), rs_tick)

        def put_own(j, value):
            dy[:, cols(j)] = value

        sent_rows = View(sent, (co.other_rows, co.other))

        def put_sent(j, value):
            sent_rows[:, cols(j)] = value.astype(BF16)

        a.backward(h, x, z, put_own, put_sent, hooks(rc, co), rs_tick)
        over(1, sent, ret).start()
        assert ticks[0] <= scatter_ticks, ticks[0]
        if ticks[0] < scatter_ticks:
            rs_tick(scatter_ticks - ticks[0])

    for s, (co, sa) in enumerate(kinds):
        @pl.when(at.s == s)
        def _(s=s, co=co, sa=sa):
            run(s == 0, co, sa)

    rc.prepare(0)
    es.clear()
    shift = rs.items
    steps = shift + rc.slots

    def both(t, carry):
        @pl.when(t < rs.slots)
        def _():
            rs.slot(t, True)

        @pl.when(t == rs.slots)
        def _():
            es.give()

        @pl.when(t == rs.slots + 2)
        def _():
            es.finish(sa_out)

        @pl.when(t == rs.slots + 4)
        def _():
            es.done(sa_out)
            ec.clear()

        @pl.when(t >= shift)
        def _():
            rc.slot(t - shift, True)

        return carry

    assert rs.slots + 4 < shift + rc.final
    lax.fori_loop(scatter_ticks, steps, both, 0)
    ec.give()

    back = over(1, sent, ret)
    back.wait_recv()
    for s, (co, sa) in enumerate(kinds):
        @pl.when(at.s == s)
        def _(s=s, co=co):
            mine = Pooled(pool, 5 * span, co.rows, co.width)
            got = View(ret, (co.rows, co.width))
            if s == 0:
                count = co.width // 128
                for j in range(count):
                    flat[pl.ds(j, co.rows, stride=count), :] = mine[:, cols(j, 128)] + got[:, cols(j, 128)].astype(F32)

                def put(j, value):
                    grad_box[:, j * 128 : (j + 1) * 128] = value

                from_flat(flat, grad_box.shape[0], grad_box.shape[1] // 128, put)
            else:
                grad_box[...] = mine[...] + got[...].astype(F32)

    ec.finish(co_out)
    back.wait_send()
    states.wait_send()
    rs.sent()
    rc.sent()
    ec.done(co_out)


KEPT = ("q", "k", "v", "p", "c", "y1", "a", "gp")
SHARED = ("fill", "m", "hb", "dc")


def kept_shapes(b):
    return {k: v[0] for k, v in scratch_of(b).items()}


def shared_shapes(b):
    rows, width = b.rows, b.width
    return {"fill": (b.rows, b.other_rows), "m": (rows, width), "hb": (rows, width), "dc": (rows, b.inner)}


SHARED_TYPES = {"fill": F32}


def most(shapes):
    return tuple(max(k) for k in zip(*shapes))


def pool_span(plans):
    return max(b.rows * b.width // 128 for p in plans for b in p.blocks)


def layer_call(plans, line, lens, xbox, gbox, co_flat, sa_flat, cid):
    vm = pl.BlockSpec(memory_space=pltpu.VMEM)
    any_ = pl.BlockSpec(memory_space=pl.ANY)
    rows_c, rows_s = [p.rows for p in plans]
    V = pltpu.VMEM
    cos, sas = [p.blocks for p in plans]
    wide = most([(b.rows, b.width) for b in cos] + [(b.other_rows, b.other) for b in cos])
    n = max(rows_c, rows_s) // UNITS
    edge = sum(p.before + p.after for p in plans)
    assert max(p.window for p in plans) + edge <= 5 * pool_span(plans)
    scr = [V((plans[0].tiles, 16, 128), BF16), V((plans[1].tiles, 16, 128), BF16), V((16, 3072), F32), V((16, 3072), F32), V((32, 128), F32),
           V((7 * pool_span(plans), 128), F32), V((edge, 128), F32), V(xbox.shape, BF16), V(wide, BF16), V(wide, BF16),
           V((12, rows_c // UNITS, 16, 128), BF16), V((12, rows_s // UNITS, 16, 128), BF16), V((n, 16, 128), F32)]
    for bs in (cos, sas):
        for name in sorted(KEPT):
            scr.append(V(most([kept_shapes(b)[name] for b in bs]), scratch_of(bs[0])[name][1]))
    for name in sorted(SHARED):
        shape = most([shared_shapes(b)[name] for b in cos + sas] + ([wide] if name == "dc" else []))
        scr.append(V(shape, SHARED_TYPES.get(name, BF16)))
    dma = pltpu.SemaphoreType.DMA
    scr += gather_sems(line) + gather_sems(line) + scatter_sems(line) + scatter_sems(line) + edge_sems() + edge_sems() + [dma((2,)), dma((2,))]
    struct = jax.ShapeDtypeStruct
    outs = [struct(xbox.shape, BF16), struct(xbox.shape, F32), struct(co_flat.shape, F32), struct(sa_flat.shape, F32)]
    outs += landing(line, rows_c) + landing(line, rows_s)
    return pl.pallas_call(
        functools.partial(layer_kernel, plans, line),
        out_shape=outs,
        in_specs=[pl.BlockSpec(memory_space=pltpu.SMEM), vm, vm, any_, any_],
        out_specs=[vm, vm] + [any_] * 8,
        scratch_shapes=scr,
        compiler_params=pltpu.CompilerParams(collective_id=cid, has_side_effects=True, vmem_limit_bytes=64 * 2**20 - 2**16),
        name="layer",
    )(lens, xbox, gbox, co_flat, sa_flat)[:4]


DT, HT, FT = 768, 12, 3072
DI, HI, FI = 1024, 8, 1024
DC, HC = 1024, 8
LT, LI = 128, 96
LINE_MAX = 8


def blocks_of(text, seqs):
    if text:
        return (Block(DT, DI, DC, FT, HC, LT, LI, seqs), Block(DT, DT, DT, FT, HT, LT, LT, seqs))
    return (Block(DI, DT, DC, FI, HC, LI, LT, seqs), Block(DI, DI, DI, FI, HI, LI, LI, seqs))


class Plan:
    def __init__(self, blocks, devices, flat_total):
        self.blocks = blocks
        self.shard = flat_total // 128 // devices
        tiles = max(b.tiles for b in blocks)
        self.rows = -(-tiles // (devices * UNITS)) * UNITS
        self.tiles = self.rows * devices
        tables = [self.table(b).reshape(self.tiles, 16) for b in blocks]
        before = after = 0
        for table in tables:
            most = table.max(axis=1)
            least = np.where(table >= 0, table, flat_total).min(axis=1)
            for d in range(devices):
                lo, hi, start, end = self.rows * d, self.rows * (d + 1), self.shard * d, self.shard * (d + 1)
                held = np.nonzero(most[lo:hi] >= 0)[0] + lo
                if held.size:
                    before = max(before, start - least[held].min())
                    after = max(after, most[held].max() + 1 - end)
        self.before, self.after = [max(-(-int(k) // 16) * 16, 16) for k in (before, after)]
        self.window = -(-(self.before + self.shard + self.after) // 8) * 8
        self.near = max(self.before, self.after) <= self.shard

    def table(self, b):
        index = np.full((self.tiles * 16,), -1, np.int32)
        for first, flat, k, rows, nb in b.parts:
            if k:
                r, j = np.arange(k)[:, None], np.arange(nb)[None]
                at = first * 16 + ((r // 16) * nb + j) * 16 + r % 16
                index[at.reshape(-1)] = (flat + r * nb + j).reshape(-1)
            else:
                index[first * 16 : first * 16 + rows] = flat + np.arange(rows)
        return index


def each_tile(b, lo, hi, start, act):
    for first, flat, k, rows, nb in b.parts:
        if k:
            count = rows // 16
            a = jnp.clip(lo - first, 0, count)
            z = jnp.clip(hi - first, 0, count)

            def body(t, carry, first=first, flat=flat, nb=nb):
                i = t // nb
                act(first + t, flat + i * 16 * nb + (t - i * nb) - start, nb, 16)
                return carry

            lax.fori_loop(a, z, body, 0)
        else:
            for t in range((rows + 15) // 16):
                @pl.when(jnp.logical_and(first + t >= lo, first + t < hi))
                def _(t=t, first=first, flat=flat, rows=rows):
                    act(first + t, flat + 16 * t - start, 1, min(16, rows - 16 * t))


def gathered(plan, text, flat):
    whole = lax.all_gather(flat.astype(BF16), "dp", axis=0, tiled=True).reshape(-1, 128)
    index = jnp.where(text, *[jnp.asarray(plan.table(b)) for b in plan.blocks])
    rows = jnp.where((index >= 0)[:, None], whole[jnp.maximum(index, 0)], jnp.zeros((), BF16))
    return rows.reshape(plan.tiles, 16, 128)


def scattered(plan, text, tiles, flat_rows):
    tables = []
    for b in plan.blocks:
        table = plan.table(b)
        back = np.full((flat_rows,), -1, np.int32)
        held = np.nonzero(table >= 0)[0]
        back[table[held]] = held
        tables.append(jnp.asarray(back))
    index = jnp.where(text, *tables)
    rows = jnp.where((index >= 0)[:, None], tiles.reshape(-1, 128)[jnp.maximum(index, 0)], jnp.zeros((), BF16))
    return lax.psum_scatter(rows.astype(F32), "dp", scatter_dimension=0, tiled=True).reshape(-1)


def layer_alone(text, counts, own, partner, grad, wco, wsa):
    seqs = own.shape[0]
    co, sa = blocks_of(text, seqs)
    box = own.shape
    lens = counts if text else counts[::-1]
    out, own_grad, sent, gco, gsa = compute(
        co, sa, lens, own.reshape(co.rows, co.width), partner.reshape(co.other_rows, co.other),
        grad.reshape(co.rows, co.width), wco, wsa)
    return out.reshape(box), own_grad.reshape(box), sent.reshape(box), gco, gsa


def body(devices, states, out_grad, co_params, self_params, text_lengths, region_counts):
    own = states[0]
    seqs = own.shape[0]
    text = lax.axis_index("stream") == 0
    flats = (co_params[0], self_params[0])
    streams = [blocks_of(t, seqs) for t in (True, False)]
    plans = [Plan([k[i] for k in streams], devices, f.shape[0] * devices) for i, f in enumerate(flats)]
    line = devices // 4
    counts = jnp.stack([text_lengths, region_counts])
    if devices % 4 == 0 and line <= LINE_MAX and all(p.near for p in plans):
        lens = jnp.where(text, counts, counts[::-1])
        box = (own.shape[0] * own.shape[1], own.shape[2])
        flats = [f.reshape(p.shard, 1, 128) for p, f in zip(plans, flats)]
        out, grad, co_grad, sa_grad = layer_call(plans, line, lens, own.reshape(box), out_grad[0].reshape(box), *flats, 1)
        return (out.reshape(states.shape), grad.reshape(states.shape), co_grad.reshape(co_params.shape), sa_grad.reshape(self_params.shape))
    swap = [(0, 1), (1, 0)]
    partner = lax.ppermute(own, "stream", swap)
    wco, wsa = [gathered(p, text, f) for p, f in zip(plans, flats)]
    out, own_grad, sent, gco, gsa = lax.cond(
        text, functools.partial(layer_alone, True), functools.partial(layer_alone, False),
        counts, own, partner, out_grad[0], wco, wsa)
    returned = lax.ppermute(sent, "stream", swap)
    flats = [scattered(p, text, g, p.shard * devices) for p, g in zip(plans, (gco, gsa))]
    return (out[None], (own_grad + returned.astype(F32))[None], flats[0][None], flats[1][None])


def solution(mesh):
    states = P("stream", "dp", None, None)
    flat = P("stream", "dp")
    return jax.shard_map(
        functools.partial(body, mesh.shape["dp"]), mesh=mesh, in_specs=(states, states, flat, flat, P("dp"), P("dp")),
        out_specs=(states, states, flat, flat), check_vma=False)
```

```python
import functools
import math

import jax
import jax.numpy as jnp
import numpy as np
from jax import lax
from jax.experimental import pallas as pl
from jax.experimental.pallas import tpu as pltpu
from jax.sharding import PartitionSpec as P


MESH_ID = pl.DeviceIdType.MESH
UNITS = 6


def place(line):
    d = lax.axis_index("dp")
    return d // 4, lax.rem(d // 2, 2), lax.rem(d, 2)


F32, BF16 = jnp.float32, jnp.bfloat16
NT = (((1,), (1,)), ((), ()))
TN = (((0,), (0,)), ((), ()))
norm_eps = 1e-12
masked_score = -1000000000.0
other_sequence = -3.0e38


def dot(a, b, dims=(((1,), (0,)), ((), ()))):
    return lax.dot_general(a, b, dims, preferred_element_type=F32)


class Block:
    def __init__(self, width, other, inner, hidden, heads, length, other_length, seqs, base=0):
        self.width, self.other, self.inner, self.hidden, self.heads = width, other, inner, hidden, heads
        self.length, self.other_length, self.seqs = length, other_length, seqs
        self.rows, self.other_rows = length * seqs, other_length * seqs
        self.base = base
        self.place = {}
        self.parts = []
        tile, flat = 0, 0

        def matrix(name, k, n):
            nonlocal tile, flat
            self.place[name] = (tile, k, n)
            self.parts.append((tile, flat, k, k * n // 128, n // 128))
            tile, flat = tile + k * n // 2048, flat + k * n // 128

        def vectors(*names):
            nonlocal tile, flat
            rows = 0
            for name, size in names:
                self.place[name] = (tile, rows, size)
                rows += size // 128
            self.parts.append((tile, flat, 0, rows, 0))
            tile, flat = tile + (rows + 15) // 16, flat + rows

        matrix("q_w", width, inner)
        vectors(("q_b", inner))
        matrix("k_w", other, inner)
        matrix("v_w", other, inner)
        vectors(("v_b", inner))
        matrix("o_w", inner, width)
        vectors(("o_b", width), ("g1", width), ("b1", width))
        matrix("i_w", width, hidden)
        vectors(("i_b", hidden))
        matrix("f_w", hidden, width)
        vectors(("f_b", width), ("g2", width), ("b2", width))
        self.tiles, self.flat_rows = tile, flat


VECS = ("q_b", "v_b", "o_b", "g1", "b1", "i_b", "f_b", "g2", "b2")
GROUPS = (("q_b",), ("v_b",), ("o_b", "g1", "b1"), ("i_b",), ("f_b", "g2", "b2"))


class Cols:
    def __init__(self, j, size):
        self.j, self.size = j, size

    def ds(self):
        return pl.ds(pl.multiple_of(self.j * self.size, self.size), self.size)


def cols(j, size=256):
    return Cols(j, size)


class Pooled:
    def __init__(self, pool, base, rows, width):
        self.pool, self.base, self.rows, self.count = pool, base, rows, width // 128

    def spots(self, index):
        if index is Ellipsis:
            first, count = 0, self.count
        else:
            run = index[1]
            count = run.size // 128
            first = run.j * count
        return [pl.ds(pl.multiple_of(self.base + (first + i) * self.rows, 8), self.rows) for i in range(count)]

    def __getitem__(self, index):
        return jnp.concatenate([self.pool[spot, :] for spot in self.spots(index)], axis=1)

    def __setitem__(self, index, value):
        for i, spot in enumerate(self.spots(index)):
            self.pool[spot, :] = value[:, i * 128 : (i + 1) * 128]


class View:
    def __init__(self, ref, shape):
        self.ref, self.shape = ref, tuple(shape)

    def whole(self, index):
        index = () if index is Ellipsis else index if isinstance(index, tuple) else (index,)
        index = index + (slice(None),) * (len(self.shape) - len(index))
        index = [i.ds() if isinstance(i, Cols) else i for i in index]
        return tuple(slice(0, k) if isinstance(i, slice) and i == slice(None) else i for i, k in zip(index, self.shape))

    def __getitem__(self, index):
        return self.ref[self.whole(index)]

    def __setitem__(self, index, value):
        self.ref[self.whole(index)] = value


NN_STEP, NT_STEP, TN_STEP, TN_WIDE = 1024, 1024, 1024, 768


def step_of(n, most):
    return max(k for k in range(256, most + 1, 256) if n % k == 0)


class Net:
    def __init__(self, b, w, vec, sc):
        self.b, self.w, self.vec, self.s = b, w, vec, sc

    def mat(self, name):
        tile, k, n = self.b.place[name]
        return self.w.at[pl.ds(self.b.base + tile, k * n // 2048)].reshape(k // 16, n // 128, 16, 128)

    def row(self, name, c=None):
        k = VECS.index(name)
        size = self.b.place[name][2]
        return self.vec[k : k + 1, :size] if c is None else self.vec[k : k + 1, c.ds()]

    def load_vectors(self, groups):
        for group in groups:
            tile = self.b.place[group[0]][0]
            rows = sum(self.b.place[g][2] for g in group) // 128
            count = (rows + 15) // 16
            value = self.w[pl.ds(self.b.base + tile, count)].reshape(count * 16, 128).astype(F32)
            r = 0
            for name in group:
                k = VECS.index(name)
                for j in range(self.b.place[name][2] // 128):
                    self.vec[k : k + 1, j * 128 : (j + 1) * 128] = value[r : r + 1]
                    r += 1

    def store_vectors(self, group, scratch):
        tile = self.b.place[group[0]][0]
        rows = sum(self.b.place[g][2] for g in group) // 128
        count = (rows + 15) // 16
        scratch[0 : count * 16] = jnp.zeros((count * 16, 128), F32)
        r = 0
        for name in group:
            k = VECS.index(name)
            for j in range(self.b.place[name][2] // 128):
                scratch[r : r + 1, :] = self.vec[k : k + 1, j * 128 : (j + 1) * 128]
                r += 1
        self.w[pl.ds(self.b.base + tile, count)] = scratch[0 : count * 16].astype(BF16).reshape(count, 16, 128)

    def nn(self, x, name, put):
        m = self.mat(name)
        k, n = self.b.place[name][1:]
        step = step_of(n, NN_STEP)

        def body(j, carry):
            per = step // 128
            w = jnp.concatenate([m[:, per * j + i].reshape(k, 128) for i in range(per)], axis=1)
            put(cols(j, step), dot(x[...], w))
            return carry

        lax.fori_loop(0, n // step, body, 0)

    def rows_of(self, name, j, step):
        m = self.mat(name)
        strips = step // 16
        return jnp.concatenate([m[pl.ds(j * strips, strips), i].reshape(step, 128) for i in range(m.shape[1])], axis=1)

    def nt(self, g, name, put):
        k, n = self.b.place[name][1:]
        step = step_of(k, NT_STEP)

        def body(j, carry):
            put(cols(j, step), dot(g[...], self.rows_of(name, j, step), NT))
            return carry

        lax.fori_loop(0, k // step, body, 0)

    def tn(self, a, g, name):
        m = self.mat(name)
        k, n = self.b.place[name][1:]
        step, wide = step_of(k, TN_STEP), step_of(n, TN_WIDE)
        strips = step // 16

        def body(j, carry):
            left = a[:, cols(j, step)].T
            for i in range(n // wide):
                got = dot(left, g[:, cols(i, wide)]).astype(BF16)
                for c in range(wide // 128):
                    m[pl.ds(j * strips, strips), i * (wide // 128) + c] = got[:, c * 128 : (c + 1) * 128].reshape(strips, 16, 128)
            return carry

        lax.fori_loop(0, k // step, body, 0)

    def norm(self, r, gain, shift):
        centre = r - jnp.mean(r, axis=-1, keepdims=True)
        spread = jnp.mean(centre * centre, axis=-1, keepdims=True)
        return centre * lax.rsqrt(spread + norm_eps) * self.row(gain) + self.row(shift)

    def norm_back(self, r, dy, gain, shift):
        centre = r - jnp.mean(r, axis=-1, keepdims=True)
        spread = jnp.mean(centre * centre, axis=-1, keepdims=True)
        s = lax.rsqrt(spread + norm_eps)
        xh = centre * s
        t = dy * self.row(gain)
        dr = s * (t - jnp.mean(t, axis=-1, keepdims=True) - xh * jnp.mean(t * xh, axis=-1, keepdims=True))
        size = self.b.width
        kg, kb = VECS.index(gain), VECS.index(shift)
        self.vec[kg : kg + 1, :size] = jnp.sum(dy * xh, axis=0, keepdims=True)
        self.vec[kb : kb + 1, :size] = jnp.sum(dy, axis=0, keepdims=True)
        return dr

    def put_sum(self, name, ref):
        k = VECS.index(name)
        self.vec[k : k + 1, : self.b.place[name][2]] = jnp.sum(ref[...].astype(F32), axis=0, keepdims=True)

    def mask(self, fill, counts):
        b = self.b
        shape = (b.rows, b.other_rows)
        row = lax.broadcasted_iota(jnp.int32, shape, 0)
        col = lax.broadcasted_iota(jnp.int32, shape, 1)
        value = jnp.full(shape, other_sequence, F32)
        for q in range(b.seqs):
            mine = (row >= q * b.length) & (row < (q + 1) * b.length)
            mine = mine & (col >= q * b.other_length) & (col < (q + 1) * b.other_length)
            value = jnp.where(mine, jnp.where(col < q * b.other_length + counts(q), 1.0, masked_score), value)
        fill[...] = value

    def heads_of(self, refs, g):
        e = self.b.inner // self.b.heads
        values = [ref[:, cols(g, 128)] for ref in refs]
        if e == 128:
            return [values]
        lane = lax.broadcasted_iota(jnp.int32, (1, 128), 1)
        return [
            [jnp.where((lane >= h * e) & (lane < (h + 1) * e), value, jnp.zeros((), BF16)) for value in values]
            for h in range(128 // e)]

    def attend(self, q, k, v, fill, p, c):
        b = self.b
        e = b.inner // b.heads
        scale = 1.0 / math.sqrt(e)
        per = max(128 // e, 1)

        def body(g, carry):
            keys = k[:, cols(g, 128)]
            total = None
            for h, (qh,) in enumerate(self.heads_of([q], g)):
                vh = self.heads_of([v], g)[h][0]
                s = dot(qh, keys, NT) * scale
                f = fill[...]
                s = jnp.where(f > 0, s, f)
                ex = jnp.exp(s - jnp.max(s, axis=-1, keepdims=True))
                probs = (ex * (1.0 / jnp.sum(ex, axis=-1, keepdims=True))).astype(BF16)
                p[g * per + h] = probs
                got = dot(probs, vh)
                total = got if total is None else total + got
            c[:, cols(g, 128)] = total.astype(BF16)
            return carry

        lax.fori_loop(0, b.inner // 128, body, 0, unroll=True)

    def attend_back(self, q, k, v, p, dc):
        b = self.b
        e = b.inner // b.heads
        scale = 1.0 / math.sqrt(e)
        per = max(128 // e, 1)

        def body(g, carry):
            values = v[:, cols(g, 128)]
            sums = None
            for h, (qh, kh, dh) in enumerate(self.heads_of([q, k, dc], g)):
                probs = p[g * per + h]
                dp = dot(dh, values, NT)
                wide = probs.astype(F32)
                ds = (wide * (dp - jnp.sum(wide * dp, axis=-1, keepdims=True))).astype(BF16)
                got = [dot(ds, kh), dot(ds, qh, TN), dot(probs, dh, TN)]
                sums = got if sums is None else [x + y for x, y in zip(sums, got)]
            q[:, cols(g, 128)] = (sums[0] * scale).astype(BF16)
            k[:, cols(g, 128)] = (sums[1] * scale).astype(BF16)
            v[:, cols(g, 128)] = sums[2].astype(BF16)
            return carry

        lax.fori_loop(0, b.inner // 128, body, 0, unroll=True)

    def forward(self, x, u, z, counts, tick=lambda k=1: None, need=lambda name: None):
        s, b = self.s, self.b
        need("o_w")
        self.load_vectors(GROUPS[:3])
        self.mask(s["fill"], counts)

        def put(ref, bias=None):
            def store(c, value):
                if bias is not None:
                    value = value + self.row(bias, c)
                ref[:, c] = value.astype(BF16)
            return store

        tick()
        self.nn(u, "q_w", put(s["q"], "q_b"))
        self.nn(z, "k_w", put(s["k"]))
        tick()
        self.nn(z, "v_w", put(s["v"], "v_b"))
        tick()
        self.attend(s["q"], s["k"], s["v"], s["fill"], s["p"], s["c"])

        tick()

        def first(c, value):
            s["r1"][:, c] = x[:, c].astype(F32) + (value + self.row("o_b", c))

        self.nn(s["c"], "o_w", first)
        y1 = self.norm(s["r1"][...], "g1", "b1")
        s["r2"][...] = y1
        s["y1"][...] = y1.astype(BF16)

        def up(c, value):
            value = value + self.row("i_b", c)
            half = 0.5 * (1.0 + lax.erf(value * (1.0 / math.sqrt(2.0))))
            s["a"][:, c] = (value * half).astype(BF16)
            s["gp"][:, c] = (half + value * (jnp.exp(-0.5 * value * value) * (1.0 / math.sqrt(2.0 * math.pi)))).astype(BF16)

        tick()
        need("i_w")
        self.load_vectors(GROUPS[3:4])
        self.nn(s["y1"], "i_w", up)
        tick()
        need("f_w")
        self.load_vectors(GROUPS[4:])

        def second(c, value):
            s["r2"][:, c] = s["r2"][:, c] + (value + self.row("f_b", c))

        self.nn(s["a"], "f_w", second)
        return self.norm(s["r2"][...], "g2", "b2")

    def backward(self, dy, u, z, put_resid, put_z, done, tick=lambda k=1: None):
        s, b = self.s, self.b
        small = s["small"]
        dr2 = self.norm_back(s["r2"][...], dy[...], "g2", "b2")
        dy[...] = dr2
        s["m"][...] = dr2.astype(BF16)
        self.put_sum("f_b", s["m"])

        def inner(c, value):
            s["gp"][:, c] = (value * s["gp"][:, c].astype(F32)).astype(BF16)

        self.nt(s["m"], "f_w", inner)
        self.store_vectors(GROUPS[4], small)
        self.tn(s["a"], s["m"], "f_w")
        done("f_w")
        tick()
        self.put_sum("i_b", s["gp"])

        def mid(c, value):
            dy[:, c] = dy[:, c] + value

        self.nt(s["gp"], "i_w", mid)
        tick()
        self.store_vectors(GROUPS[3], small)
        self.tn(s["y1"], s["gp"], "i_w")
        done("i_w")
        tick()
        dr1 = self.norm_back(s["r1"][...], dy[...], "g1", "b1")
        dy[...] = dr1
        s["m"][...] = dr1.astype(BF16)
        self.put_sum("o_b", s["m"])

        def context(c, value):
            s["dc"][:, c] = value.astype(BF16)

        self.nt(s["m"], "o_w", context)
        self.store_vectors(GROUPS[2], small)
        self.tn(s["c"], s["m"], "o_w")
        done("o_w")
        tick(2)
        self.attend_back(s["q"], s["k"], s["v"], s["p"], s["dc"])

        tick(2)

        def resid(c, value):
            put_resid(c, dy[:, c] + value)

        self.nt(s["q"], "q_w", resid)
        k = b.place["v_w"][1]
        step = step_of(k, NT_STEP)

        def body(j, carry):
            value = dot(s["k"][...], self.rows_of("k_w", j, step), NT) + dot(s["v"][...], self.rows_of("v_w", j, step), NT)
            put_z(cols(j, step), value)
            return carry

        lax.fori_loop(0, k // step, body, 0)
        tick()
        self.put_sum("q_b", s["q"])
        self.put_sum("v_b", s["v"])
        self.store_vectors(GROUPS[0], small)
        self.store_vectors(GROUPS[1], small)
        self.tn(u, s["q"], "q_w")
        self.tn(z, s["k"], "k_w")
        self.tn(z, s["v"], "v_w")
        done("q_w")
        tick()


def scratch_of(b):
    return {
        "q": ((b.rows, b.inner), BF16), "k": ((b.other_rows, b.inner), BF16), "v": ((b.other_rows, b.inner), BF16),
        "p": ((b.heads, b.rows, b.other_rows), BF16), "c": ((b.rows, b.inner), BF16),
        "r1": ((b.rows, b.width), F32), "r2": ((b.rows, b.width), F32), "y1": ((b.rows, b.width), BF16),
        "a": ((b.rows, b.hidden), BF16), "gp": ((b.rows, b.hidden), BF16), "fill": ((b.rows, b.other_rows), F32)}


def compute_kernel(co, sa, lens, x, xp, gy, wco, wsa, out, own_grad, sent, gco, gsa, wc, ws, vec, vec2, small, sems, *scr):
    names = sorted(scratch_of(co))
    sc = dict(zip(names, scr[: len(names)]))
    ss = dict(zip(names, scr[len(names) : 2 * len(names)]))
    rest = scr[2 * len(names) :]
    m, dy, h, hb, dcc, dcs = rest
    for d, dc in ((sc, dcc), (ss, dcs)):
        d["m"], d["small"], d["dc"] = m, small, dc
    x, xp = View(x, (co.rows, co.width)), View(xp, (co.other_rows, co.other))
    own_grad, sent = View(own_grad, (co.rows, co.width)), View(sent, (co.other_rows, co.other))
    h, hb, dy = [View(r, (co.rows, co.width)) for r in (h, hb, dy)]
    for b, d in ((co, sc), (sa, ss)):
        shapes = {**{n: k[0] for n, k in scratch_of(b).items()}, "m": (b.rows, b.width), "dc": (b.rows, b.inner)}
        for n, shape in shapes.items():
            d[n] = View(d[n], shape)
    copies = [pltpu.make_async_copy(wco, wc, sems.at[0]), pltpu.make_async_copy(wsa, ws, sems.at[1])]
    for cp in copies:
        cp.start()
    copies[0].wait()
    a = Net(co, wc, vec, sc)
    bnet = Net(sa, ws, vec2, ss)
    value = a.forward(x, x, xp, lambda q: lens[1, q])
    h[...] = value
    hb[...] = value.astype(BF16)
    copies[1].wait()
    out[...] = bnet.forward(h, hb, hb, lambda q: lens[0, q]).astype(BF16)
    dy[...] = gy[...].astype(F32)

    def put_h(c, value):
        h[:, c] = value

    def add_h(c, value):
        h[:, c] = h[:, c] + value

    bnet.backward(dy, hb, hb, put_h, add_h, lambda name: None)
    back = pltpu.make_async_copy(ws, gsa, sems.at[1])
    back.start()

    def put_own(c, value):
        own_grad[:, c] = value

    def put_sent(c, value):
        sent[:, c] = value.astype(BF16)

    a.backward(h, x, xp, put_own, put_sent, lambda name: None)
    back2 = pltpu.make_async_copy(wc, gco, sems.at[0])
    back2.start()
    back.wait()
    back2.wait()


def compute(co, sa, lens, x, xp, gy, wco, wsa):
    any_ = pl.BlockSpec(memory_space=pl.ANY)
    vm = pl.BlockSpec(memory_space=pltpu.VMEM)
    names = sorted(scratch_of(co))
    V = lambda shape, dtype: pltpu.VMEM(shape, dtype)
    scr = [V(wco.shape, BF16), V(wsa.shape, BF16), V((16, 3072), F32), V((16, 3072), F32), V((32, 128), F32), pltpu.SemaphoreType.DMA((2,))]
    scr += [V(*scratch_of(co)[n]) for n in names] + [V(*scratch_of(sa)[n]) for n in names]
    rows, width = co.rows, co.width
    scr += [V((rows, width), BF16), V((rows, width), F32), V((rows, width), F32), V((rows, width), BF16)]
    scr += [V((b.rows, b.inner), BF16) for b in (co, sa)]
    return pl.pallas_call(
        functools.partial(compute_kernel, co, sa),
        out_shape=(jax.ShapeDtypeStruct((rows, width), BF16), jax.ShapeDtypeStruct((rows, width), F32),
                   jax.ShapeDtypeStruct((co.other_rows, co.other), BF16),
                   jax.ShapeDtypeStruct(wco.shape, BF16), jax.ShapeDtypeStruct(wsa.shape, BF16)),
        in_specs=[pl.BlockSpec(memory_space=pltpu.SMEM), vm, vm, vm, any_, any_],
        out_specs=(vm, vm, vm, any_, any_),
        scratch_shapes=scr,
        compiler_params=pltpu.CompilerParams(vmem_limit_bytes=63 * 2**20),
        name="compute",
    )(lens, x, xp, gy, wco, wsa)


PER = UNITS + 1
BEHIND = 4
LEAD = 3


class Where:
    def __init__(self, line):
        self.line, self.last = line, line - 1
        self.z, self.x, self.c = place(line)
        self.s = lax.axis_index("stream")

    def copy(self, src, dst, send, recv, z, x, c, s=None):
        return pltpu.make_async_remote_copy(
            src_ref=src, dst_ref=dst, send_sem=send, recv_sem=recv,
            device_id=(self.s if s is None else s, (z * 2 + x) * 2 + c), device_id_type=MESH_ID)

    def greet(self):
        z, x, c, s = self.z, self.x, self.c, self.s
        barrier = pltpu.get_barrier_semaphore()

        def signal(zz, xx, cc, ss):
            pl.semaphore_signal(barrier, inc=1, device_id=(ss, (zz * 2 + xx) * 2 + cc), device_id_type=MESH_ID)

        signal(z, 1 - x, c, s)
        signal(z, x, 1 - c, s)
        signal(z, x, c, 1 - s)
        d = (z * 2 + x) * 2 + c
        beside = (1 - c) * jnp.minimum(d, 1) + c * jnp.minimum(4 * self.line - 1 - d, 1)

        @pl.when(beside > 0)
        def _():
            pl.semaphore_signal(barrier, inc=1, device_id=(s, d - 1 + 2 * c), device_id_type=MESH_ID)

        @pl.when(z > 0)
        def _():
            signal(z - 1, x, c, s)

        @pl.when(z < self.last)
        def _():
            signal(z + 1, x, c, s)

        pl.semaphore_wait(barrier, 3 + jnp.minimum(z, 1) + jnp.minimum(self.last - z, 1) + beside)


class Gather:
    def __init__(self, at, rows, w, sems):
        self.at, self.rows, self.w = at, rows, w
        self.n = self.rows // UNITS
        self.up_s, self.dn_s, self.z_r, self.x_s, self.x_r, self.c_s, self.c_r, self.o_s = sems

    def spot(self, zo, xb, cc, u):
        return self.w.at[pl.ds(((zo * 2 + xb) * 2 + cc) * self.rows + u * self.n, self.n)]

    def block_of(self, v):
        x = self.at.x
        return jnp.where(v == UNITS, 1 - x, x), jnp.minimum(v, UNITS - 1)

    def z_copy(self, zo, v, up):
        at = self.at
        xb, u = self.block_of(v)
        spot = self.spot(zo, xb, at.c, u)
        return at.copy(spot, spot, (self.up_s if up else self.dn_s).at[zo], self.z_r.at[zo * PER + v], at.z + 1 if up else at.z - 1, at.x, at.c)

    def x_copy(self, zo, u, arriving=False, first=False):
        at = self.at
        spot = self.spot(zo, 1 - at.x if arriving else at.x, at.c, u)
        return at.copy(spot, spot, self.o_s if first else self.x_s.at[zo], self.x_r.at[zo * UNITS + u], at.z, 1 - at.x, at.c)

    def c_copy(self, zo, xb, u):
        at = self.at
        spot = self.spot(zo, xb, at.c, u)
        return at.copy(spot, spot, self.c_s.at[zo], self.c_r.at[zo], at.z, at.x, 1 - at.c)

    def send_z(self, zo, v, up):
        at = self.at

        @pl.when(at.z < at.last if up else at.z > 0)
        def _():
            self.z_copy(zo, v, up).start()

    def first(self):
        self.x_copy(self.at.z, UNITS - 1, first=True).start()

    def start(self, up):
        at = self.at
        z, x = at.z, at.x
        for u in range(UNITS - 1):
            self.x_copy(z, u).start()
            self.send_z(z, u, False)
            if up:
                self.send_z(z, u, True)
        self.send_z(z, UNITS - 1, False)
        if up:
            self.send_z(z, UNITS - 1, True)
        for u in range(UNITS):
            self.c_copy(z, x, u).start()

    def other_last(self, up):
        at = self.at
        self.x_copy(at.z, UNITS - 1, arriving=True).wait_recv()
        self.send_z(at.z, UNITS, False)
        if up:
            self.send_z(at.z, UNITS, True)
        self.c_copy(at.z, 1 - at.x, UNITS - 1).start()

    def onward(self, zo, v, up):
        xb, u = self.block_of(v)
        self.z_copy(zo, v, up).wait_recv()
        self.send_z(zo, v, up)

        @pl.when(v < UNITS - 1)
        def _():
            self.x_copy(zo, u).start()

        self.c_copy(zo, xb, u).start()

    def from_below(self, t):
        h, v = t // PER, lax.rem(t, PER)

        @pl.when(self.at.z > h)
        def _():
            self.onward(self.at.z - 1 - h, v, True)

    def from_above(self, t):
        h, v = t // PER, lax.rem(t, PER)

        @pl.when(self.at.z + h < self.at.last)
        def _():
            self.onward(self.at.z + 1 + h, v, False)

    def in_order(self, i):
        z = self.at.z
        zo, v = i // PER, lax.rem(i, PER)

        @pl.when(jnp.logical_and(i >= 0, zo < z))
        def _():
            self.onward(zo, v, True)

        @pl.when(jnp.logical_and(i >= 0, zo == z))
        def _():
            self.send_z(z, v, True)

    def x_arrival(self, zo, u):
        self.x_copy(zo, u, arriving=True).wait_recv()
        self.c_copy(zo, 1 - self.at.x, u).start()

    def beside_own(self):
        for u in range(UNITS - 1):
            self.x_arrival(self.at.z, u)

    def beside_far(self, t):
        at = self.at
        h, v = t // PER, lax.rem(t, PER)

        @pl.when(jnp.logical_and(t >= 0, v < UNITS - 1))
        def _():
            @pl.when(at.z > h)
            def _():
                self.x_arrival(at.z - 1 - h, v)

            @pl.when(at.z + h < at.last)
            def _():
                self.x_arrival(at.z + 1 + h, v)

    def beside_order(self, i):
        zo, v = i // PER, lax.rem(i, PER)

        @pl.when(jnp.logical_and(jnp.logical_and(i >= 0, v < UNITS - 1), zo < self.at.z))
        def _():
            self.x_arrival(zo, v)

    def beside_above(self, t):
        at = self.at
        h, v = t // PER, lax.rem(t, PER)

        @pl.when(jnp.logical_and(jnp.logical_and(t >= 0, v < UNITS - 1), at.z + h < at.last))
        def _():
            self.x_arrival(at.z + 1 + h, v)

    def arrived(self, zo):
        at = self.at
        spot = self.w.at[pl.ds(0, 2 * self.rows)]
        at.copy(spot, spot, self.o_s, self.c_r.at[zo], at.z, at.x, 1 - at.c).wait_recv()

    def sent(self):
        at = self.at
        z = at.z

        def wait(tiles, sem):
            spot = self.w.at[pl.ds(0, tiles)]
            at.copy(spot, spot, sem, self.c_r.at[0], z, at.x, 1 - at.c).wait_send()

        def each(zo, carry):
            @pl.when(jnp.logical_and(z < at.last, zo <= z))
            def _():
                wait(PER * self.n, self.up_s.at[zo])

            @pl.when(jnp.logical_and(z > 0, zo >= z))
            def _():
                wait(PER * self.n, self.dn_s.at[zo])

            wait((UNITS - 1) * self.n, self.x_s.at[zo])
            wait(2 * self.rows, self.c_s.at[zo])
            return carry

        lax.fori_loop(0, at.line, each, 0)
        wait(self.n, self.o_s)


def gather_sems(line):
    dma = pltpu.SemaphoreType.DMA
    return [dma((line,)), dma((line,)), dma((line * PER,)), dma((line,)), dma((line * UNITS,)), dma((line,)), dma((line,)), dma]


class Scatter:
    def __init__(self, at, g, rows, cr, xr, zr, keep, stage, wide_stage, behind, sems):
        self.at, self.g, self.rows, self.n = at, g, rows, rows // UNITS
        self.cr, self.xr, self.zr, self.keep, self.stage, self.wide = cr, xr, zr, keep, stage, wide_stage
        self.c_s, self.c_r, self.x_s, self.x_r, self.z_s, self.z_r, self.l_s, self.b_s = sems
        self.behind = behind
        self.items = at.last * PER
        self.final = self.items + LEAD + at.last + behind
        self.slots = self.final + PER

    def mine(self, zo, xb, u):
        return pl.ds(((zo * 2 + xb) * 2 + self.at.c) * self.rows + u * self.n, self.n)

    def block_of(self, v):
        x = self.at.x
        return jnp.where(v == 0, 1 - x, x), jnp.where(v == 0, UNITS - 1, v - 1)

    def c_copy(self, zo, xb):
        at = self.at
        src = self.g.at[pl.ds(((zo * 2 + xb) * 2 + 1 - at.c) * self.rows, self.rows)]
        k = zo * 2 + xb
        return at.copy(src, self.cr.at[k], self.c_s.at[zo], self.c_r.at[k], at.z, at.x, 1 - at.c)

    def x_copy(self, zo, u, last=False):
        at = self.at
        k = zo * UNITS + u
        return at.copy(self.g.at[self.mine(zo, 1 - at.x, u)], self.xr.at[k], self.b_s if last else self.x_s.at[zo], self.x_r.at[k],
                       at.z, 1 - at.x, at.c)

    def z_copy(self, to, v, up):
        at = self.at
        xb, u = self.block_of(v)
        there = at.z + 1 if up else at.z - 1
        k = (to if up else jnp.where(to == there, at.line, to)) * PER + v
        return at.copy(self.g.at[self.mine(to, xb, u)], self.zr.at[k], self.z_s.at[to], self.z_r.at[k], there, at.x, at.c)

    def z_wait(self, k):
        at = self.at
        spot = self.zr.at[k]
        at.copy(spot, spot, self.z_s.at[0], self.z_r.at[k], at.z, 1 - at.x, at.c).wait_recv()

    def ready(self, zo):
        for xb in range(2):
            self.c_copy(zo, xb).start()

    def load(self, src, slot):
        return pltpu.make_async_copy(src, self.stage.at[slot, pl.ds(0, self.n)], self.l_s.at[slot])

    def core_part(self, zo, xb, u):
        return self.cr.at[zo * 2 + xb, pl.ds(u * self.n, self.n)]

    def way(self, t, up):
        at = self.at
        i = t - (at.z if up else at.last - at.z + self.behind)
        to = (at.last if up else at.last - 1) - i // PER
        here = jnp.logical_and(jnp.logical_and(i >= 0, i < self.items), to > at.z if up else to < at.z)
        return to, lax.rem(i, PER), here

    def crossings(self, t):
        at = self.at
        found = []
        for up, slot in ((True, 0), (False, 11)):
            to, v, here = self.way(t, up)
            found.append((to, v - 1, jnp.logical_and(here, jnp.logical_and(v >= 1, v < UNITS)), slot))
        u = t - self.items - self.behind - 1
        found.append((at.z, u, jnp.logical_and(u >= 0, u < UNITS - 1), 0))
        return found

    def parts(self, t, finals):
        found = [self.way(t - LEAD, up) + (up, slot) for up, slot in ((True, 1), (False, 4))]
        own = t - self.final
        return found + [(self.at.z, own, jnp.logical_and(own >= 0, own < PER), None, 7)] * finals

    def prepare(self, t, finals=False):
        at = self.at
        for to, u, here, slot in self.crossings(t):
            @pl.when(here)
            def _(to=to, u=u, slot=slot):
                @pl.when(u == 0)
                def _():
                    for xb in range(2):
                        self.c_copy(to, xb).wait_recv()

                self.load(self.core_part(to, 1 - at.x, u), slot).start()

        for to, v, here, up, slot in self.parts(t, finals):
            @pl.when(here)
            def _(to=to, v=v, up=up, slot=slot):
                xb, u = self.block_of(v)
                self.load(self.core_part(to, xb, u), slot).start()

                @pl.when(jnp.logical_and(v >= 1, v < (UNITS if up is not None else PER)))
                def _():
                    self.x_copy(to, u).wait_recv()
                    self.load(self.xr.at[to * UNITS + u], slot + 1).start()

                if up is None:
                    @pl.when(at.z > 0)
                    def _():
                        self.z_wait(to * PER + v)
                        self.load(self.zr.at[to * PER + v], slot + 2).start()

                    @pl.when(at.z < at.last)
                    def _():
                        self.z_wait(at.line * PER + v)
                        self.load(self.zr.at[at.line * PER + v], slot + 3).start()
                else:
                    @pl.when(at.z != (0 if up else at.last))
                    def _():
                        self.z_wait(to * PER + v)
                        self.load(self.zr.at[to * PER + v], slot + 2).start()

    def take(self, slot):
        self.load(self.xr.at[0], slot).wait()
        return self.stage[slot].astype(F32)

    def act(self, t, finals):
        at = self.at
        for to, v, here, up, slot in self.parts(t, finals):
            @pl.when(here)
            def _(to=to, v=v, up=up, slot=slot):
                xb, u = self.block_of(v)
                spot = self.mine(to, xb, u)
                acc = self.wide

                acc[: self.n] = self.g[spot].astype(F32) + self.take(slot)

                def more(k):
                    acc[: self.n] = acc[: self.n] + self.take(slot + k)

                @pl.when(jnp.logical_and(v >= 1, v < (UNITS if up is not None else PER)))
                def _():
                    more(1)

                if up is None:
                    @pl.when(at.z > 0)
                    def _():
                        more(2)

                    @pl.when(at.z < at.last)
                    def _():
                        more(3)

                    @pl.when(v == 0)
                    def _():
                        self.g[spot] = acc[: self.n].astype(BF16)
                        self.x_copy(to, UNITS - 1, True).start()

                    @pl.when(v >= 1)
                    def _():
                        self.keep(u)
                else:
                    @pl.when(at.z != (0 if up else at.last))
                    def _():
                        more(2)

                    self.g[spot] = acc[: self.n].astype(BF16)
                    self.z_copy(to, v, up).start()

        for to, u, here, slot in self.crossings(t):
            @pl.when(here)
            def _(to=to, u=u, slot=slot):
                spot = self.mine(to, 1 - at.x, u)
                self.g[spot] = (self.g[spot].astype(F32) + self.take(slot)).astype(BF16)
                self.x_copy(to, u).start()

    def slot(self, t, finals=False):
        self.act(t, finals)
        self.prepare(t + 1, finals)

    def sent(self):
        at = self.at
        z = at.z

        def wait(tiles, sem):
            spot = self.g.at[pl.ds(0, tiles)]
            at.copy(spot, spot, sem, self.c_r.at[0], z, at.x, 1 - at.c).wait_send()

        def each(zo, carry):
            @pl.when(zo != z)
            def _():
                wait(PER * self.n, self.z_s.at[zo])

            wait((UNITS - 1) * self.n, self.x_s.at[zo])
            wait(2 * self.rows, self.c_s.at[zo])
            return carry

        lax.fori_loop(0, at.line, each, 0)
        wait(self.n, self.b_s)


def scatter_sems(line):
    dma = pltpu.SemaphoreType.DMA
    return [dma((line,)), dma((line * 2,)), dma((line,)), dma((line * UNITS,)), dma((line,)), dma(((line + 1) * PER,)), dma((12,)), dma]


def landing(line, rows):
    n = rows // UNITS
    shape = lambda *s: jax.ShapeDtypeStruct(s + (16, 128), BF16)
    return [shape(line * 2, rows), shape(line * UNITS, n), shape((line + 1) * PER, n)]


class Edges:
    def __init__(self, at, plan, window, first, spare, land, sems):
        self.at, self.plan, self.window, self.first, self.spare, self.land = at, plan, window, first, spare, land
        self.f_s, self.f_r, self.l_s, self.e_s, self.e_r = sems
        self.d = (at.z * 2 + at.x) * 2 + at.c
        self.end = plan.before + plan.shard

    def over(self, src, dst, send, recv, by):
        return pltpu.make_async_remote_copy(
            src_ref=src, dst_ref=dst, send_sem=send, recv_sem=recv, device_id=(self.at.s, self.d + by), device_id_type=MESH_ID)

    def both(self, up, down):
        @pl.when(self.d < 4 * self.at.line - 1)
        def _():
            up()

        @pl.when(self.d > 0)
        def _():
            down()

    def lands(self, ref):
        plan = self.plan
        return ref.at[pl.ds(0, plan.before)], ref.at[pl.ds(plan.before, plan.after)]

    def outer(self, own):
        plan = self.plan
        before, after = self.lands(self.first)
        return (self.over(own.at[pl.ds(plan.shard - plan.before, plan.before), 0], before, self.f_s.at[0], self.f_r.at[0], 1),
                self.over(own.at[pl.ds(0, plan.after), 0], after, self.f_s.at[1], self.f_r.at[1], -1))

    def send(self, own):
        up, down = self.outer(own)
        self.both(up.start, down.start)

    def inner(self, own):
        return pltpu.make_async_copy(own.at[:, 0], self.window.at[pl.ds(self.plan.before, self.plan.shard)], self.l_s)

    def tiles(self, kinds, own, w):
        plan = self.plan
        up, down = self.outer(own)
        lo = plan.rows * self.d
        w[pl.ds(lo, plan.rows)] = jnp.zeros((plan.rows, 16, 128), w.dtype)

        def above():
            down.wait_recv()
            self.window[self.end : self.end + plan.after, :] = self.first[plan.before : plan.before + plan.after, :]

        def below():
            up.wait_recv()
            self.window[: plan.before, :] = self.first[: plan.before, :]

        self.both(above, below)
        self.inner(own).wait()

        def act(tile, row, stride, rows):
            value = self.window[pl.ds(row, rows, stride=stride), :]
            if rows < 16:
                value = jnp.concatenate([value, jnp.zeros((16 - rows, 128), value.dtype)], axis=0)
            w[tile] = value.astype(w.dtype)

        self.by_stream(kinds, lo, lo + plan.rows, act)
        self.both(up.wait_send, down.wait_send)

    def by_stream(self, kinds, lo, hi, act):
        start = self.plan.shard * self.d - self.plan.before
        for s, b in enumerate(kinds):
            @pl.when(self.at.s == s)
            def _(b=b):
                each_tile(b, lo, hi, start, act)

    def clear(self):
        self.window[...] = jnp.zeros(self.window.shape, F32)

    def take(self, kinds, acc, n):
        def keep(u):
            lo = self.plan.rows * self.d + u * n

            def act(tile, row, stride, rows):
                self.window[pl.ds(row, rows, stride=stride), :] = acc[tile - lo][:rows]

            self.by_stream(kinds, lo, lo + n, act)

        return keep

    def back(self):
        plan = self.plan
        front, rear = self.lands(self.land)
        return (self.over(self.spare.at[pl.ds(0, plan.after)], rear, self.e_s.at[0], self.e_r.at[0], 1),
                self.over(self.window.at[pl.ds(0, plan.before)], front, self.e_s.at[1], self.e_r.at[1], -1))

    def give(self):
        self.spare[: self.plan.after, :] = self.window[self.end : self.end + self.plan.after, :]
        up, down = self.back()
        self.both(up.start, down.start)

    def finish(self, out):
        plan = self.plan
        up, down = self.back()

        def above():
            down.wait_recv()
            spot = slice(self.end - plan.before, self.end)
            self.window[spot, :] = self.window[spot, :] + self.land[: plan.before, :]

        def below():
            up.wait_recv()
            spot = slice(plan.before, plan.before + plan.after)
            self.window[spot, :] = self.window[spot, :] + self.land[plan.before : plan.before + plan.after, :]

        self.both(above, below)
        self.leave(out).start()

    def leave(self, out):
        return pltpu.make_async_copy(self.window.at[pl.ds(self.plan.before, self.plan.shard)], out.at[:, 0], self.l_s)

    def done(self, out):
        self.leave(out).wait()
        up, down = self.back()
        self.both(up.wait_send, down.wait_send)


def edge_sems():
    dma = pltpu.SemaphoreType.DMA
    return [dma((2,)), dma((2,)), dma, dma((2,)), dma((2,))]


def to_flat(flat, box):
    count = box.shape[1] // 128
    for b in range(count):
        flat[pl.ds(b, box.shape[0], stride=count), :] = box[:, b * 128 : (b + 1) * 128].astype(F32)


def from_flat(flat, rows, count, put):
    for j in range(count):
        put(j, flat[pl.ds(j, rows, stride=count), :])


def layer_kernel(plans, line, lens, xbox, gbox, co_flat, sa_flat, *refs):
    kinds = list(zip(plans[0].blocks, plans[1].blocks))
    outs, refs = refs[:10], refs[10:]
    out_box, grad_box, co_out, sa_out = outs[:4]
    wc, ws, vec, vec2, small, pool, land, xp, xin, ret, stage_c, stage_s, acc = refs[:13]
    refs = refs[13:]
    names = sorted(KEPT)
    sc = dict(zip(names, refs[: len(names)]))
    refs = refs[len(names) :]
    ss = dict(zip(names, refs[: len(names)]))
    refs = refs[len(names) :]
    shared = dict(zip(sorted(SHARED), refs[: len(SHARED)]))
    refs = refs[len(SHARED) :]
    ag_c, ag_s, rs_c, rs_s, ed_c, ed_s, y_s, y_r = refs[:8], refs[8:16], refs[16:24], refs[24:32], refs[32:37], refs[37:42], refs[42], refs[43]
    sent = shared["dc"]
    span = pool_span(plans)
    flat = pool.at[pl.ds(6 * span, span)]

    at = Where(line)
    last = at.last
    gc, gs = Gather(at, plans[0].rows, wc, ag_c), Gather(at, plans[1].rows, ws, ag_s)
    edges = []
    rest = max(p.window for p in plans)
    for k, (p, sems) in enumerate(zip(plans, (ed_c, ed_s))):
        sizes = [q.before + q.after for q in plans]
        edges.append(Edges(at, p, pool.at[pl.ds(0, p.window)], pool.at[pl.ds(rest + k * sizes[0], sizes[k])], pool.at[pl.ds(rest, p.after)],
                           land.at[pl.ds(k * sizes[0], sizes[k])], sems))
    ec, es = edges
    own_kinds = [[k[i] for k in kinds] for i in range(2)]
    rc = Scatter(at, wc, plans[0].rows, *outs[4:7], ec.take(own_kinds[0], acc, gc.n), stage_c, acc, 0, rs_c)
    rs = Scatter(at, ws, plans[1].rows, *outs[7:10], es.take(own_kinds[1], acc, gs.n), stage_s, acc, BEHIND, rs_s)

    def over(k, src, dst):
        return at.copy(src, dst, y_s.at[k], y_r.at[k], at.z, at.x, at.c, 1 - at.s)

    ec.inner(co_flat).start()
    at.greet()
    ec.send(co_flat)
    es.send(sa_flat)
    ec.tiles(own_kinds[0], co_flat, wc)
    gc.first()
    gc.start(True)
    es.inner(sa_flat).start()
    states = over(0, xbox, xp)
    states.start()
    es.tiles(own_kinds[1], sa_flat, ws)
    gs.first()
    gc.other_last(True)

    steps = PER * last
    early = PER

    def co_step(t, carry):
        gc.from_below(t)
        gc.from_above(t)

        @pl.when(t < UNITS - 1)
        def _():
            gc.x_arrival(at.z, t)

        gc.beside_far(t - PER)

        @pl.when(jnp.logical_and(t >= steps - early, at.z < last))
        def _():
            gs.in_order(t - (steps - early) - at.z)

        return carry

    lax.fori_loop(0, steps - early, co_step, 0)
    gs.start(False)
    gs.other_last(False)
    lax.fori_loop(steps - early, steps, co_step, 0)

    def co_rest(t, carry):
        gc.beside_far(t)
        return carry

    lax.fori_loop(steps - PER, steps, co_rest, 0)
    gs.beside_own()
    for zo in range(line):
        gc.arrived(zo)
    states.wait_recv()

    ahead = jnp.where(at.z < last, early - at.z, 0)

    def self_beside(t):
        gs.beside_order(t + ahead)
        gs.beside_above(t)

    def self_steps(a, b, lag):
        def step(t, carry):
            gs.in_order(t + ahead)
            gs.from_above(t)
            self_beside(t - lag)
            return carry

        lax.fori_loop(a, b, step, 0)

    def self_rest(a, b):
        lax.fori_loop(a, b, lambda t, carry: (self_beside(t), carry)[1], 0)

    gather_steps = steps
    scatter_ticks = 20

    def run(text, co, sa):
        rows, width = co.rows, co.width

        def view(refs, b):
            d = {name: View(ref, kept_shapes(b)[name]) for name, ref in refs.items()}
            for name, ref in shared.items():
                d[name] = View(ref, shared_shapes(b)[name])
            for k, name in enumerate(("r1", "r2")):
                d[name] = Pooled(pool, (2 * (b is sa) + k) * span, b.rows, b.width)
            d["h"], d["dy"] = [Pooled(pool, k * span, b.rows, b.width) for k in (4, 5)]
            d["small"] = small
            return d

        a = Net(co, wc, vec, view(sc, co))
        b = Net(sa, ws, vec2, view(ss, sa))
        h, hb, dy = b.s["h"], b.s["hb"], b.s["dy"]

        own_in = View(xin, (rows, width))
        if text:
            to_flat(flat, xbox)

            def put(j, value):
                own_in[:, cols(j, 128)] = value.astype(BF16)

            from_flat(flat, rows, width // 128, put)
            x, z = own_in, View(xp, xp.shape)
        else:
            to_flat(flat, xp)
            other = View(xin, (co.other_rows, co.other))

            def put(j, value):
                other[:, cols(j, 128)] = value.astype(BF16)

            from_flat(flat, co.other_rows, co.other // 128, put)
            x, z = View(xbox, xbox.shape), other

        steps_done, beside_done, places = [0], [-PER], [0]

        def tick(k=1):
            a0 = steps_done[0]
            b0 = min(a0 + k, gather_steps)
            if b0 > a0:
                self_steps(a0, b0, a0 - beside_done[0])
                beside_done[0] += b0 - a0
                steps_done[0] = b0

        def need(name):
            later = [sa.place[n][0] for n in ("i_w", "f_w") if sa.place[n][0] > sa.place[name][0]]
            top = -(-min(later + [sa.tiles]) // (4 * gs.rows))
            wanted = min(PER * top, gather_steps)
            tick(min(wanted + 3, gather_steps) - steps_done[0])
            if beside_done[0] < wanted:
                self_rest(beside_done[0], wanted)
                beside_done[0] = wanted
            for zo in range(places[0], top):
                gs.arrived(zo)
            places[0] = max(places[0], top)

        value = a.forward(x, x, z, lambda q: lens[1, q], tick)
        h[...] = value
        hb[...] = value.astype(BF16)
        gc.sent()
        if text:
            to_flat(flat, gbox)

            def put(j, value):
                dy[:, cols(j, 128)] = value

            from_flat(flat, rows, width // 128, put)
        else:
            dy[...] = gbox[...].astype(F32)
        value = b.forward(h, hb, hb, lambda q: lens[0, q], tick, need)
        if text:
            for j in range(width // 128):
                flat[pl.ds(j, rows, stride=width // 128), :] = value[:, j * 128 : (j + 1) * 128]
        else:
            out_box[...] = value.astype(BF16)
        gs.sent()

        def put_h(c, value):
            h[:, c] = value

        def add_h(c, value):
            h[:, c] = h[:, c] + value

        ticks = [0]

        def hooks(scatter, block):
            state = [line]

            def done(name):
                tile = block.place[name][0]
                ready = -(-tile // (4 * scatter.rows))
                while state[0] > ready:
                    state[0] -= 1
                    scatter.ready(state[0])
                    if scatter is rs and state[0] == last:
                        rs.prepare(0)

            return done

        def rs_tick(k=1):
            a0 = ticks[0]
            ticks[0] = a0 + k
            lax.fori_loop(a0, a0 + k, lambda t, carry: (rs.slot(t), carry)[1], 0)

        b.backward(dy, hb, hb, put_h, add_h, hooks(rs, sa), rs_tick)
        if text:
            def put(j, value):
                out_box[:, j * 128 : (j + 1) * 128] = value.astype(BF16)

            from_flat(flat, out_box.shape[0], out_box.shape[1] // 128, put)

        def put_own(c, value):
            dy[:, c] = value

        sent_rows = View(sent, (co.other_rows, co.other))

        def put_sent(c, value):
            sent_rows[:, c] = value.astype(BF16)

        a.backward(h, x, z, put_own, put_sent, hooks(rc, co), rs_tick)
        over(1, sent, ret).start()
        assert ticks[0] <= scatter_ticks, ticks[0]
        if ticks[0] < scatter_ticks:
            rs_tick(scatter_ticks - ticks[0])

    for s, (co, sa) in enumerate(kinds):
        @pl.when(at.s == s)
        def _(s=s, co=co, sa=sa):
            run(s == 0, co, sa)

    rc.prepare(0)
    es.clear()
    shift = rs.items
    steps = shift + rc.slots

    def both(t, carry):
        @pl.when(t < rs.slots)
        def _():
            rs.slot(t, True)

        @pl.when(t == rs.slots)
        def _():
            es.give()

        @pl.when(t == rs.slots + 2)
        def _():
            es.finish(sa_out)

        @pl.when(t == rs.slots + 4)
        def _():
            es.done(sa_out)
            ec.clear()

        @pl.when(t >= shift)
        def _():
            rc.slot(t - shift, True)

        return carry

    assert rs.slots + 4 < shift + rc.final
    lax.fori_loop(scatter_ticks, steps, both, 0)
    ec.give()

    back = over(1, sent, ret)
    back.wait_recv()
    for s, (co, sa) in enumerate(kinds):
        @pl.when(at.s == s)
        def _(s=s, co=co):
            mine = Pooled(pool, 5 * span, co.rows, co.width)
            got = View(ret, (co.rows, co.width))
            if s == 0:
                count = co.width // 128
                for j in range(count):
                    flat[pl.ds(j, co.rows, stride=count), :] = mine[:, cols(j, 128)] + got[:, cols(j, 128)].astype(F32)

                def put(j, value):
                    grad_box[:, j * 128 : (j + 1) * 128] = value

                from_flat(flat, grad_box.shape[0], grad_box.shape[1] // 128, put)
            else:
                grad_box[...] = mine[...] + got[...].astype(F32)

    ec.finish(co_out)
    back.wait_send()
    states.wait_send()
    rs.sent()
    rc.sent()
    ec.done(co_out)


KEPT = ("q", "k", "v", "p", "c", "y1", "a", "gp")
SHARED = ("fill", "m", "hb", "dc")


def kept_shapes(b):
    return {k: v[0] for k, v in scratch_of(b).items()}


def shared_shapes(b):
    rows, width = b.rows, b.width
    return {"fill": (b.rows, b.other_rows), "m": (rows, width), "hb": (rows, width), "dc": (rows, b.inner)}


SHARED_TYPES = {"fill": F32}


def most(shapes):
    return tuple(max(k) for k in zip(*shapes))


def pool_span(plans):
    return max(b.rows * b.width // 128 for p in plans for b in p.blocks)


def layer_call(plans, line, lens, xbox, gbox, co_flat, sa_flat, cid):
    vm = pl.BlockSpec(memory_space=pltpu.VMEM)
    any_ = pl.BlockSpec(memory_space=pl.ANY)
    rows_c, rows_s = [p.rows for p in plans]
    V = pltpu.VMEM
    cos, sas = [p.blocks for p in plans]
    wide = most([(b.rows, b.width) for b in cos] + [(b.other_rows, b.other) for b in cos])
    n = max(rows_c, rows_s) // UNITS
    edge = sum(p.before + p.after for p in plans)
    assert max(p.window for p in plans) + edge <= 5 * pool_span(plans)
    scr = [V((plans[0].tiles, 16, 128), BF16), V((plans[1].tiles, 16, 128), BF16), V((16, 3072), F32), V((16, 3072), F32), V((32, 128), F32),
           V((7 * pool_span(plans), 128), F32), V((edge, 128), F32), V(xbox.shape, BF16), V(wide, BF16), V(wide, BF16),
           V((12, rows_c // UNITS, 16, 128), BF16), V((12, rows_s // UNITS, 16, 128), BF16), V((n, 16, 128), F32)]
    for bs in (cos, sas):
        for name in sorted(KEPT):
            scr.append(V(most([kept_shapes(b)[name] for b in bs]), scratch_of(bs[0])[name][1]))
    for name in sorted(SHARED):
        shape = most([shared_shapes(b)[name] for b in cos + sas] + ([wide] if name == "dc" else []))
        scr.append(V(shape, SHARED_TYPES.get(name, BF16)))
    dma = pltpu.SemaphoreType.DMA
    scr += gather_sems(line) + gather_sems(line) + scatter_sems(line) + scatter_sems(line) + edge_sems() + edge_sems() + [dma((2,)), dma((2,))]
    struct = jax.ShapeDtypeStruct
    outs = [struct(xbox.shape, BF16), struct(xbox.shape, F32), struct(co_flat.shape, F32), struct(sa_flat.shape, F32)]
    outs += landing(line, rows_c) + landing(line, rows_s)
    return pl.pallas_call(
        functools.partial(layer_kernel, plans, line),
        out_shape=outs,
        in_specs=[pl.BlockSpec(memory_space=pltpu.SMEM), vm, vm, any_, any_],
        out_specs=[vm, vm] + [any_] * 8,
        scratch_shapes=scr,
        compiler_params=pltpu.CompilerParams(collective_id=cid, has_side_effects=True, vmem_limit_bytes=64 * 2**20 - 2**16),
        name="layer",
    )(lens, xbox, gbox, co_flat, sa_flat)[:4]


DT, HT, FT = 768, 12, 3072
DI, HI, FI = 1024, 8, 1024
DC, HC = 1024, 8
LT, LI = 128, 96
LINE_MAX = 8


def blocks_of(text, seqs):
    if text:
        return (Block(DT, DI, DC, FT, HC, LT, LI, seqs), Block(DT, DT, DT, FT, HT, LT, LT, seqs))
    return (Block(DI, DT, DC, FI, HC, LI, LT, seqs), Block(DI, DI, DI, FI, HI, LI, LI, seqs))


class Plan:
    def __init__(self, blocks, devices, flat_total):
        self.blocks = blocks
        self.shard = flat_total // 128 // devices
        tiles = max(b.tiles for b in blocks)
        self.rows = -(-tiles // (devices * UNITS)) * UNITS
        self.tiles = self.rows * devices
        tables = [self.table(b).reshape(self.tiles, 16) for b in blocks]
        before = after = 0
        for table in tables:
            most = table.max(axis=1)
            least = np.where(table >= 0, table, flat_total).min(axis=1)
            for d in range(devices):
                lo, hi, start, end = self.rows * d, self.rows * (d + 1), self.shard * d, self.shard * (d + 1)
                held = np.nonzero(most[lo:hi] >= 0)[0] + lo
                if held.size:
                    before = max(before, start - least[held].min())
                    after = max(after, most[held].max() + 1 - end)
        self.before, self.after = [max(-(-int(k) // 16) * 16, 16) for k in (before, after)]
        self.window = -(-(self.before + self.shard + self.after) // 8) * 8
        self.near = max(self.before, self.after) <= self.shard

    def table(self, b):
        index = np.full((self.tiles * 16,), -1, np.int32)
        for first, flat, k, rows, nb in b.parts:
            if k:
                r, j = np.arange(k)[:, None], np.arange(nb)[None]
                at = first * 16 + ((r // 16) * nb + j) * 16 + r % 16
                index[at.reshape(-1)] = (flat + r * nb + j).reshape(-1)
            else:
                index[first * 16 : first * 16 + rows] = flat + np.arange(rows)
        return index


def each_tile(b, lo, hi, start, act):
    for first, flat, k, rows, nb in b.parts:
        if k:
            count = rows // 16
            a = jnp.clip(lo - first, 0, count)
            z = jnp.clip(hi - first, 0, count)

            def body(t, carry, first=first, flat=flat, nb=nb):
                i = t // nb
                act(first + t, flat + i * 16 * nb + (t - i * nb) - start, nb, 16)
                return carry

            lax.fori_loop(a, z, body, 0)
        else:
            for t in range((rows + 15) // 16):
                @pl.when(jnp.logical_and(first + t >= lo, first + t < hi))
                def _(t=t, first=first, flat=flat, rows=rows):
                    act(first + t, flat + 16 * t - start, 1, min(16, rows - 16 * t))


def gathered(plan, text, flat):
    whole = lax.all_gather(flat.astype(BF16), "dp", axis=0, tiled=True).reshape(-1, 128)
    index = jnp.where(text, *[jnp.asarray(plan.table(b)) for b in plan.blocks])
    rows = jnp.where((index >= 0)[:, None], whole[jnp.maximum(index, 0)], jnp.zeros((), BF16))
    return rows.reshape(plan.tiles, 16, 128)


def scattered(plan, text, tiles, flat_rows):
    tables = []
    for b in plan.blocks:
        table = plan.table(b)
        back = np.full((flat_rows,), -1, np.int32)
        held = np.nonzero(table >= 0)[0]
        back[table[held]] = held
        tables.append(jnp.asarray(back))
    index = jnp.where(text, *tables)
    rows = jnp.where((index >= 0)[:, None], tiles.reshape(-1, 128)[jnp.maximum(index, 0)], jnp.zeros((), BF16))
    return lax.psum_scatter(rows.astype(F32), "dp", scatter_dimension=0, tiled=True).reshape(-1)


def layer_alone(text, counts, own, partner, grad, wco, wsa):
    seqs = own.shape[0]
    co, sa = blocks_of(text, seqs)
    box = own.shape
    lens = counts if text else counts[::-1]
    out, own_grad, sent, gco, gsa = compute(
        co, sa, lens, own.reshape(co.rows, co.width), partner.reshape(co.other_rows, co.other),
        grad.reshape(co.rows, co.width), wco, wsa)
    return out.reshape(box), own_grad.reshape(box), sent.reshape(box), gco, gsa


def body(devices, states, out_grad, co_params, self_params, text_lengths, region_counts):
    own = states[0]
    seqs = own.shape[0]
    text = lax.axis_index("stream") == 0
    flats = (co_params[0], self_params[0])
    streams = [blocks_of(t, seqs) for t in (True, False)]
    plans = [Plan([k[i] for k in streams], devices, f.shape[0] * devices) for i, f in enumerate(flats)]
    line = devices // 4
    counts = jnp.stack([text_lengths, region_counts])
    if devices % 4 == 0 and line <= LINE_MAX and all(p.near for p in plans):
        lens = jnp.where(text, counts, counts[::-1])
        box = (own.shape[0] * own.shape[1], own.shape[2])
        flats = [f.reshape(p.shard, 1, 128) for p, f in zip(plans, flats)]
        out, grad, co_grad, sa_grad = layer_call(plans, line, lens, own.reshape(box), out_grad[0].reshape(box), *flats, 1)
        return (out.reshape(states.shape), grad.reshape(states.shape), co_grad.reshape(co_params.shape), sa_grad.reshape(self_params.shape))
    swap = [(0, 1), (1, 0)]
    partner = lax.ppermute(own, "stream", swap)
    wco, wsa = [gathered(p, text, f) for p, f in zip(plans, flats)]
    out, own_grad, sent, gco, gsa = lax.cond(
        text, functools.partial(layer_alone, True), functools.partial(layer_alone, False),
        counts, own, partner, out_grad[0], wco, wsa)
    returned = lax.ppermute(sent, "stream", swap)
    flats = [scattered(p, text, g, p.shard * devices) for p, g in zip(plans, (gco, gsa))]
    return (out[None], (own_grad + returned.astype(F32))[None], flats[0][None], flats[1][None])


def solution(mesh):
    states = P("stream", "dp", None, None)
    flat = P("stream", "dp")
    return jax.shard_map(
        functools.partial(body, mesh.shape["dp"]), mesh=mesh, in_specs=(states, states, flat, flat, P("dp"), P("dp")),
        out_specs=(states, states, flat, flat), check_vma=False)
```

```python
import functools
import math

import jax
import jax.numpy as jnp
import numpy as np
from jax import lax
from jax.experimental import pallas as pl
from jax.experimental.pallas import tpu as pltpu
from jax.sharding import PartitionSpec as P


MESH_ID = pl.DeviceIdType.MESH
UNITS = 6


def place(line):
    d = lax.axis_index("dp")
    return d // 4, lax.rem(d // 2, 2), lax.rem(d, 2)


F32, BF16 = jnp.float32, jnp.bfloat16
NT = (((1,), (1,)), ((), ()))
TN = (((0,), (0,)), ((), ()))
norm_eps = 1e-12
masked_score = -1000000000.0
other_sequence = -3.0e38


def dot(a, b, dims=(((1,), (0,)), ((), ()))):
    return lax.dot_general(a, b, dims, preferred_element_type=F32)


class Block:
    def __init__(self, width, other, inner, hidden, heads, length, other_length, seqs, base=0):
        self.width, self.other, self.inner, self.hidden, self.heads = width, other, inner, hidden, heads
        self.length, self.other_length, self.seqs = length, other_length, seqs
        self.rows, self.other_rows = length * seqs, other_length * seqs
        self.base = base
        self.place = {}
        self.parts = []
        tile, flat = 0, 0

        def matrix(name, k, n):
            nonlocal tile, flat
            self.place[name] = (tile, k, n)
            self.parts.append((tile, flat, k, k * n // 128, n // 128))
            tile, flat = tile + k * n // 2048, flat + k * n // 128

        def vectors(*names):
            nonlocal tile, flat
            rows = 0
            for name, size in names:
                self.place[name] = (tile, rows, size)
                rows += size // 128
            self.parts.append((tile, flat, 0, rows, 0))
            tile, flat = tile + (rows + 15) // 16, flat + rows

        matrix("q_w", width, inner)
        vectors(("q_b", inner))
        matrix("k_w", other, inner)
        matrix("v_w", other, inner)
        vectors(("v_b", inner))
        matrix("o_w", inner, width)
        vectors(("o_b", width), ("g1", width), ("b1", width))
        matrix("i_w", width, hidden)
        vectors(("i_b", hidden))
        matrix("f_w", hidden, width)
        vectors(("f_b", width), ("g2", width), ("b2", width))
        self.tiles, self.flat_rows = tile, flat


VECS = ("q_b", "v_b", "o_b", "g1", "b1", "i_b", "f_b", "g2", "b2")
GROUPS = (("q_b",), ("v_b",), ("o_b", "g1", "b1"), ("i_b",), ("f_b", "g2", "b2"))


class Cols:
    def __init__(self, j, size):
        self.j, self.size = j, size

    def ds(self):
        return pl.ds(pl.multiple_of(self.j * self.size, self.size), self.size)


def cols(j, size=256):
    return Cols(j, size)


class Pooled:
    def __init__(self, pool, base, rows, width):
        self.pool, self.base, self.rows, self.count = pool, base, rows, width // 128

    def spots(self, index):
        if index is Ellipsis:
            first, count = 0, self.count
        else:
            run = index[1]
            count = run.size // 128
            first = run.j * count
        return [pl.ds(pl.multiple_of(self.base + (first + i) * self.rows, 8), self.rows) for i in range(count)]

    def __getitem__(self, index):
        return jnp.concatenate([self.pool[spot, :] for spot in self.spots(index)], axis=1)

    def __setitem__(self, index, value):
        for i, spot in enumerate(self.spots(index)):
            self.pool[spot, :] = value[:, i * 128 : (i + 1) * 128]


class View:
    def __init__(self, ref, shape):
        self.ref, self.shape = ref, tuple(shape)

    def whole(self, index):
        index = () if index is Ellipsis else index if isinstance(index, tuple) else (index,)
        index = index + (slice(None),) * (len(self.shape) - len(index))
        index = [i.ds() if isinstance(i, Cols) else i for i in index]
        return tuple(slice(0, k) if isinstance(i, slice) and i == slice(None) else i for i, k in zip(index, self.shape))

    def __getitem__(self, index):
        return self.ref[self.whole(index)]

    def __setitem__(self, index, value):
        self.ref[self.whole(index)] = value


NN_STEP, NT_STEP, TN_STEP, TN_WIDE = 1024, 1024, 1024, 768


def step_of(n, most):
    return max(k for k in range(256, most + 1, 256) if n % k == 0)


class Net:
    def __init__(self, b, w, vec, sc):
        self.b, self.w, self.vec, self.s = b, w, vec, sc

    def mat(self, name):
        tile, k, n = self.b.place[name]
        return self.w.at[pl.ds(self.b.base + tile, k * n // 2048)].reshape(k // 16, n // 128, 16, 128)

    def row(self, name, c=None):
        k = VECS.index(name)
        size = self.b.place[name][2]
        return self.vec[k : k + 1, :size] if c is None else self.vec[k : k + 1, c.ds()]

    def load_vectors(self, groups):
        for group in groups:
            tile = self.b.place[group[0]][0]
            rows = sum(self.b.place[g][2] for g in group) // 128
            count = (rows + 15) // 16
            value = self.w[pl.ds(self.b.base + tile, count)].reshape(count * 16, 128).astype(F32)
            r = 0
            for name in group:
                k = VECS.index(name)
                for j in range(self.b.place[name][2] // 128):
                    self.vec[k : k + 1, j * 128 : (j + 1) * 128] = value[r : r + 1]
                    r += 1

    def store_vectors(self, group, scratch):
        tile = self.b.place[group[0]][0]
        rows = sum(self.b.place[g][2] for g in group) // 128
        count = (rows + 15) // 16
        scratch[0 : count * 16] = jnp.zeros((count * 16, 128), F32)
        r = 0
        for name in group:
            k = VECS.index(name)
            for j in range(self.b.place[name][2] // 128):
                scratch[r : r + 1, :] = self.vec[k : k + 1, j * 128 : (j + 1) * 128]
                r += 1
        self.w[pl.ds(self.b.base + tile, count)] = scratch[0 : count * 16].astype(BF16).reshape(count, 16, 128)

    def nn(self, x, name, put):
        m = self.mat(name)
        k, n = self.b.place[name][1:]
        step = step_of(n, NN_STEP)

        def body(j, carry):
            per = step // 128
            w = jnp.concatenate([m[:, per * j + i].reshape(k, 128) for i in range(per)], axis=1)
            put(cols(j, step), dot(x[...], w))
            return carry

        lax.fori_loop(0, n // step, body, 0)

    def rows_of(self, name, j, step):
        m = self.mat(name)
        strips = step // 16
        return jnp.concatenate([m[pl.ds(j * strips, strips), i].reshape(step, 128) for i in range(m.shape[1])], axis=1)

    def nt(self, g, name, put):
        k, n = self.b.place[name][1:]
        step = step_of(k, NT_STEP)

        def body(j, carry):
            put(cols(j, step), dot(g[...], self.rows_of(name, j, step), NT))
            return carry

        lax.fori_loop(0, k // step, body, 0)

    def tn(self, a, g, name):
        m = self.mat(name)
        k, n = self.b.place[name][1:]
        step, wide = step_of(k, TN_STEP), step_of(n, TN_WIDE)
        strips = step // 16

        def body(j, carry):
            left = a[:, cols(j, step)].T
            for i in range(n // wide):
                got = dot(left, g[:, cols(i, wide)]).astype(BF16)
                for c in range(wide // 128):
                    m[pl.ds(j * strips, strips), i * (wide // 128) + c] = got[:, c * 128 : (c + 1) * 128].reshape(strips, 16, 128)
            return carry

        lax.fori_loop(0, k // step, body, 0)

    def norm(self, r, gain, shift):
        centre = r - jnp.mean(r, axis=-1, keepdims=True)
        spread = jnp.mean(centre * centre, axis=-1, keepdims=True)
        return centre * lax.rsqrt(spread + norm_eps) * self.row(gain) + self.row(shift)

    def norm_back(self, r, dy, gain, shift):
        centre = r - jnp.mean(r, axis=-1, keepdims=True)
        spread = jnp.mean(centre * centre, axis=-1, keepdims=True)
        s = lax.rsqrt(spread + norm_eps)
        xh = centre * s
        t = dy * self.row(gain)
        dr = s * (t - jnp.mean(t, axis=-1, keepdims=True) - xh * jnp.mean(t * xh, axis=-1, keepdims=True))
        size = self.b.width
        kg, kb = VECS.index(gain), VECS.index(shift)
        self.vec[kg : kg + 1, :size] = jnp.sum(dy * xh, axis=0, keepdims=True)
        self.vec[kb : kb + 1, :size] = jnp.sum(dy, axis=0, keepdims=True)
        return dr

    def put_sum(self, name, ref):
        k = VECS.index(name)
        self.vec[k : k + 1, : self.b.place[name][2]] = jnp.sum(ref[...].astype(F32), axis=0, keepdims=True)

    def mask(self, fill, counts):
        b = self.b
        shape = (b.rows, b.other_rows)
        row = lax.broadcasted_iota(jnp.int32, shape, 0)
        col = lax.broadcasted_iota(jnp.int32, shape, 1)
        value = jnp.full(shape, other_sequence, F32)
        for q in range(b.seqs):
            mine = (row >= q * b.length) & (row < (q + 1) * b.length)
            mine = mine & (col >= q * b.other_length) & (col < (q + 1) * b.other_length)
            value = jnp.where(mine, jnp.where(col < q * b.other_length + counts(q), 1.0, masked_score), value)
        fill[...] = value

    def heads_of(self, refs, g):
        e = self.b.inner // self.b.heads
        values = [ref[:, cols(g, 128)] for ref in refs]
        if e == 128:
            return [values]
        lane = lax.broadcasted_iota(jnp.int32, (1, 128), 1)
        return [
            [jnp.where((lane >= h * e) & (lane < (h + 1) * e), value, jnp.zeros((), BF16)) for value in values]
            for h in range(128 // e)]

    def attend(self, q, k, v, fill, p, c):
        b = self.b
        e = b.inner // b.heads
        scale = 1.0 / math.sqrt(e)
        per = max(128 // e, 1)

        def body(g, carry):
            keys = k[:, cols(g, 128)]
            total = None
            for h, (qh,) in enumerate(self.heads_of([q], g)):
                vh = self.heads_of([v], g)[h][0]
                s = dot(qh, keys, NT) * scale
                f = fill[...]
                s = jnp.where(f > 0, s, f)
                ex = jnp.exp(s - jnp.max(s, axis=-1, keepdims=True))
                probs = (ex * (1.0 / jnp.sum(ex, axis=-1, keepdims=True))).astype(BF16)
                p[g * per + h] = probs
                got = dot(probs, vh)
                total = got if total is None else total + got
            c[:, cols(g, 128)] = total.astype(BF16)
            return carry

        lax.fori_loop(0, b.inner // 128, body, 0, unroll=2)

    def attend_back(self, q, k, v, p, dc):
        b = self.b
        e = b.inner // b.heads
        scale = 1.0 / math.sqrt(e)
        per = max(128 // e, 1)

        def body(g, carry):
            values = v[:, cols(g, 128)]
            sums = None
            for h, (qh, kh, dh) in enumerate(self.heads_of([q, k, dc], g)):
                probs = p[g * per + h]
                dp = dot(dh, values, NT)
                wide = probs.astype(F32)
                ds = (wide * (dp - jnp.sum(wide * dp, axis=-1, keepdims=True))).astype(BF16)
                got = [dot(ds, kh), dot(ds, qh, TN), dot(probs, dh, TN)]
                sums = got if sums is None else [x + y for x, y in zip(sums, got)]
            q[:, cols(g, 128)] = (sums[0] * scale).astype(BF16)
            k[:, cols(g, 128)] = (sums[1] * scale).astype(BF16)
            v[:, cols(g, 128)] = sums[2].astype(BF16)
            return carry

        lax.fori_loop(0, b.inner // 128, body, 0, unroll=2)

    def forward(self, x, u, z, counts, tick=lambda k=1: None, need=lambda name: None):
        s, b = self.s, self.b
        need("o_w")
        self.load_vectors(GROUPS[:3])
        self.mask(s["fill"], counts)

        def put(ref, bias=None):
            def store(c, value):
                if bias is not None:
                    value = value + self.row(bias, c)
                ref[:, c] = value.astype(BF16)
            return store

        tick()
        self.nn(u, "q_w", put(s["q"], "q_b"))
        self.nn(z, "k_w", put(s["k"]))
        tick()
        self.nn(z, "v_w", put(s["v"], "v_b"))
        tick()
        self.attend(s["q"], s["k"], s["v"], s["fill"], s["p"], s["c"])

        tick()

        def first(c, value):
            s["r1"][:, c] = x[:, c].astype(F32) + (value + self.row("o_b", c))

        self.nn(s["c"], "o_w", first)
        y1 = self.norm(s["r1"][...], "g1", "b1")
        s["r2"][...] = y1
        s["y1"][...] = y1.astype(BF16)

        def up(c, value):
            value = value + self.row("i_b", c)
            half = 0.5 * (1.0 + lax.erf(value * (1.0 / math.sqrt(2.0))))
            s["a"][:, c] = (value * half).astype(BF16)
            s["gp"][:, c] = (half + value * (jnp.exp(-0.5 * value * value) * (1.0 / math.sqrt(2.0 * math.pi)))).astype(BF16)

        tick()
        need("i_w")
        self.load_vectors(GROUPS[3:4])
        self.nn(s["y1"], "i_w", up)
        tick()
        need("f_w")
        self.load_vectors(GROUPS[4:])

        def second(c, value):
            s["r2"][:, c] = s["r2"][:, c] + (value + self.row("f_b", c))

        self.nn(s["a"], "f_w", second)
        return self.norm(s["r2"][...], "g2", "b2")

    def backward(self, dy, u, z, put_resid, put_z, done, tick=lambda k=1: None):
        s, b = self.s, self.b
        small = s["small"]
        dr2 = self.norm_back(s["r2"][...], dy[...], "g2", "b2")
        dy[...] = dr2
        s["m"][...] = dr2.astype(BF16)
        self.put_sum("f_b", s["m"])

        def inner(c, value):
            s["gp"][:, c] = (value * s["gp"][:, c].astype(F32)).astype(BF16)

        self.nt(s["m"], "f_w", inner)
        self.store_vectors(GROUPS[4], small)
        self.tn(s["a"], s["m"], "f_w")
        done("f_w")
        self.put_sum("i_b", s["gp"])

        def mid(c, value):
            dy[:, c] = dy[:, c] + value

        self.nt(s["gp"], "i_w", mid)
        tick(4)
        self.store_vectors(GROUPS[3], small)
        self.tn(s["y1"], s["gp"], "i_w")
        done("i_w")
        tick()
        dr1 = self.norm_back(s["r1"][...], dy[...], "g1", "b1")
        dy[...] = dr1
        s["m"][...] = dr1.astype(BF16)
        self.put_sum("o_b", s["m"])

        def context(c, value):
            s["dc"][:, c] = value.astype(BF16)

        self.nt(s["m"], "o_w", context)
        self.store_vectors(GROUPS[2], small)
        self.tn(s["c"], s["m"], "o_w")
        done("o_w")
        tick(3)
        self.attend_back(s["q"], s["k"], s["v"], s["p"], s["dc"])

        tick(2)

        def resid(c, value):
            put_resid(c, dy[:, c] + value)

        self.nt(s["q"], "q_w", resid)
        k = b.place["v_w"][1]
        step = step_of(k, NT_STEP)

        def body(j, carry):
            value = dot(s["k"][...], self.rows_of("k_w", j, step), NT) + dot(s["v"][...], self.rows_of("v_w", j, step), NT)
            put_z(cols(j, step), value)
            return carry

        lax.fori_loop(0, k // step, body, 0)
        tick()
        self.put_sum("q_b", s["q"])
        self.put_sum("v_b", s["v"])
        self.store_vectors(GROUPS[0], small)
        self.store_vectors(GROUPS[1], small)
        self.tn(u, s["q"], "q_w")
        self.tn(z, s["k"], "k_w")
        self.tn(z, s["v"], "v_w")
        done("q_w")
        tick(2)


def scratch_of(b):
    return {
        "q": ((b.rows, b.inner), BF16), "k": ((b.other_rows, b.inner), BF16), "v": ((b.other_rows, b.inner), BF16),
        "p": ((b.heads, b.rows, b.other_rows), BF16), "c": ((b.rows, b.inner), BF16),
        "r1": ((b.rows, b.width), F32), "r2": ((b.rows, b.width), F32), "y1": ((b.rows, b.width), BF16),
        "a": ((b.rows, b.hidden), BF16), "gp": ((b.rows, b.hidden), BF16), "fill": ((b.rows, b.other_rows), F32)}


def compute_kernel(co, sa, lens, x, xp, gy, wco, wsa, out, own_grad, sent, gco, gsa, wc, ws, vec, vec2, small, sems, *scr):
    names = sorted(scratch_of(co))
    sc = dict(zip(names, scr[: len(names)]))
    ss = dict(zip(names, scr[len(names) : 2 * len(names)]))
    rest = scr[2 * len(names) :]
    m, dy, h, hb, dcc, dcs = rest
    for d, dc in ((sc, dcc), (ss, dcs)):
        d["m"], d["small"], d["dc"] = m, small, dc
    x, xp = View(x, (co.rows, co.width)), View(xp, (co.other_rows, co.other))
    own_grad, sent = View(own_grad, (co.rows, co.width)), View(sent, (co.other_rows, co.other))
    h, hb, dy = [View(r, (co.rows, co.width)) for r in (h, hb, dy)]
    for b, d in ((co, sc), (sa, ss)):
        shapes = {**{n: k[0] for n, k in scratch_of(b).items()}, "m": (b.rows, b.width), "dc": (b.rows, b.inner)}
        for n, shape in shapes.items():
            d[n] = View(d[n], shape)
    copies = [pltpu.make_async_copy(wco, wc, sems.at[0]), pltpu.make_async_copy(wsa, ws, sems.at[1])]
    for cp in copies:
        cp.start()
    copies[0].wait()
    a = Net(co, wc, vec, sc)
    bnet = Net(sa, ws, vec2, ss)
    value = a.forward(x, x, xp, lambda q: lens[1, q])
    h[...] = value
    hb[...] = value.astype(BF16)
    copies[1].wait()
    out[...] = bnet.forward(h, hb, hb, lambda q: lens[0, q]).astype(BF16)
    dy[...] = gy[...].astype(F32)

    def put_h(c, value):
        h[:, c] = value

    def add_h(c, value):
        h[:, c] = h[:, c] + value

    bnet.backward(dy, hb, hb, put_h, add_h, lambda name: None)
    back = pltpu.make_async_copy(ws, gsa, sems.at[1])
    back.start()

    def put_own(c, value):
        own_grad[:, c] = value

    def put_sent(c, value):
        sent[:, c] = value.astype(BF16)

    a.backward(h, x, xp, put_own, put_sent, lambda name: None)
    back2 = pltpu.make_async_copy(wc, gco, sems.at[0])
    back2.start()
    back.wait()
    back2.wait()


def compute(co, sa, lens, x, xp, gy, wco, wsa):
    any_ = pl.BlockSpec(memory_space=pl.ANY)
    vm = pl.BlockSpec(memory_space=pltpu.VMEM)
    names = sorted(scratch_of(co))
    V = lambda shape, dtype: pltpu.VMEM(shape, dtype)
    scr = [V(wco.shape, BF16), V(wsa.shape, BF16), V((16, 3072), F32), V((16, 3072), F32), V((32, 128), F32), pltpu.SemaphoreType.DMA((2,))]
    scr += [V(*scratch_of(co)[n]) for n in names] + [V(*scratch_of(sa)[n]) for n in names]
    rows, width = co.rows, co.width
    scr += [V((rows, width), BF16), V((rows, width), F32), V((rows, width), F32), V((rows, width), BF16)]
    scr += [V((b.rows, b.inner), BF16) for b in (co, sa)]
    return pl.pallas_call(
        functools.partial(compute_kernel, co, sa),
        out_shape=(jax.ShapeDtypeStruct((rows, width), BF16), jax.ShapeDtypeStruct((rows, width), F32),
                   jax.ShapeDtypeStruct((co.other_rows, co.other), BF16),
                   jax.ShapeDtypeStruct(wco.shape, BF16), jax.ShapeDtypeStruct(wsa.shape, BF16)),
        in_specs=[pl.BlockSpec(memory_space=pltpu.SMEM), vm, vm, vm, any_, any_],
        out_specs=(vm, vm, vm, any_, any_),
        scratch_shapes=scr,
        compiler_params=pltpu.CompilerParams(vmem_limit_bytes=63 * 2**20),
        name="compute",
    )(lens, x, xp, gy, wco, wsa)


PER = UNITS + 1
SLOTS_TEXT, SLOTS_IMAGE, SLOTS_CO = (2, 4, 3, 2, 1, 1), (2, 0, 4, 2, 1, 4), (1, 1, 0, 1, 0, 1)
BEHIND = 2


class Where:
    def __init__(self, line):
        self.line, self.last = line, line - 1
        self.z, self.x, self.c = place(line)
        self.s = lax.axis_index("stream")

    def copy(self, src, dst, send, recv, z, x, c, s=None):
        return pltpu.make_async_remote_copy(
            src_ref=src, dst_ref=dst, send_sem=send, recv_sem=recv,
            device_id=(self.s if s is None else s, (z * 2 + x) * 2 + c), device_id_type=MESH_ID)

    def greet(self):
        z, x, c, s = self.z, self.x, self.c, self.s
        barrier = pltpu.get_barrier_semaphore()

        def signal(zz, xx, cc, ss):
            pl.semaphore_signal(barrier, inc=1, device_id=(ss, (zz * 2 + xx) * 2 + cc), device_id_type=MESH_ID)

        signal(z, 1 - x, c, s)
        signal(z, x, 1 - c, s)
        signal(z, x, c, 1 - s)
        d = (z * 2 + x) * 2 + c
        beside = (1 - c) * jnp.minimum(d, 1) + c * jnp.minimum(4 * self.line - 1 - d, 1)

        @pl.when(beside > 0)
        def _():
            pl.semaphore_signal(barrier, inc=1, device_id=(s, d - 1 + 2 * c), device_id_type=MESH_ID)

        @pl.when(z > 0)
        def _():
            signal(z - 1, x, c, s)

        @pl.when(z < self.last)
        def _():
            signal(z + 1, x, c, s)

        pl.semaphore_wait(barrier, 3 + jnp.minimum(z, 1) + jnp.minimum(self.last - z, 1) + beside)


class Gather:
    def __init__(self, at, rows, w, sems):
        self.at, self.rows, self.w = at, rows, w
        self.n = self.rows // UNITS
        self.up_s, self.dn_s, self.z_r, self.x_s, self.x_r, self.c_s, self.c_r, self.o_s = sems

    def lies(self, u):
        return jnp.where(u == 0, 1, jnp.where(u < 4, u + 2, jnp.where(u == 4, 0, 2))) * self.n

    def spot(self, zo, xb, cc, u):
        return self.w.at[pl.ds(((zo * 2 + xb) * 2 + cc) * self.rows + self.lies(u), self.n)]

    def block_of(self, v):
        x = self.at.x
        return jnp.where(v == UNITS, 1 - x, x), jnp.minimum(v, UNITS - 1)

    def z_copy(self, zo, v, up):
        at = self.at
        xb, u = self.block_of(v)
        spot = self.spot(zo, xb, at.c, u)
        return at.copy(spot, spot, (self.up_s if up else self.dn_s).at[zo], self.z_r.at[zo * PER + v], at.z + 1 if up else at.z - 1, at.x, at.c)

    def x_copy(self, zo, u, arriving=False, first=False):
        at = self.at
        spot = self.spot(zo, 1 - at.x if arriving else at.x, at.c, u)
        return at.copy(spot, spot, self.o_s if first else self.x_s.at[zo], self.x_r.at[zo * UNITS + u], at.z, 1 - at.x, at.c)

    def c_copy(self, zo, xb, u):
        at = self.at
        spot = self.spot(zo, xb, at.c, u)
        return at.copy(spot, spot, self.c_s.at[zo], self.c_r.at[zo], at.z, at.x, 1 - at.c)

    def send_z(self, zo, v, up):
        at = self.at

        @pl.when(at.z < at.last if up else at.z > 0)
        def _():
            self.z_copy(zo, v, up).start()

    def first(self):
        self.x_copy(self.at.z, UNITS - 1, first=True).start()

    def start_unit(self, u):
        at = self.at

        @pl.when(u == UNITS - 1)
        def _():
            self.first()

        @pl.when(u != UNITS - 1)
        def _():
            self.x_copy(at.z, u).start()

        self.send_z(at.z, u, True)
        self.send_z(at.z, u, False)
        self.c_copy(at.z, at.x, u).start()

    def start(self):
        at = self.at
        for u in range(UNITS - 1):
            self.x_copy(at.z, u).start()
            self.send_z(at.z, u, False)
        self.send_z(at.z, UNITS - 1, False)
        for u in range(UNITS):
            self.c_copy(at.z, at.x, u).start()

    def other_last(self, up):
        at = self.at
        self.x_copy(at.z, UNITS - 1, arriving=True).wait_recv()
        self.send_z(at.z, UNITS, False)
        if up:
            self.send_z(at.z, UNITS, True)
        self.c_copy(at.z, 1 - at.x, UNITS - 1).start()

    def onward(self, zo, v, up):
        xb, u = self.block_of(v)
        self.z_copy(zo, v, up).wait_recv()
        self.send_z(zo, v, up)

        @pl.when(v < UNITS - 1)
        def _():
            self.x_copy(zo, u).start()

        self.c_copy(zo, xb, u).start()

    def from_below(self, t):
        h, v = t // PER, lax.rem(t, PER)

        @pl.when(self.at.z > h)
        def _():
            self.onward(self.at.z - 1 - h, v, True)

    def from_above(self, t):
        h, v = t // PER, lax.rem(t, PER)

        @pl.when(self.at.z + h < self.at.last)
        def _():
            self.onward(self.at.z + 1 + h, v, False)

    def in_order(self, i):
        z = self.at.z
        zo, v = i // PER, lax.rem(i, PER)

        @pl.when(jnp.logical_and(i >= 0, zo < z))
        def _():
            self.onward(zo, v, True)

        @pl.when(jnp.logical_and(i >= 0, zo == z))
        def _():
            self.send_z(z, v, True)

    def x_arrival(self, zo, u):
        self.x_copy(zo, u, arriving=True).wait_recv()
        self.c_copy(zo, 1 - self.at.x, u).start()

    def beside_own(self):
        for u in range(UNITS - 1):
            self.x_arrival(self.at.z, u)

    def beside_far(self, t):
        at = self.at
        h, v = t // PER, lax.rem(t, PER)

        @pl.when(jnp.logical_and(t >= 0, v < UNITS - 1))
        def _():
            @pl.when(at.z > h)
            def _():
                self.x_arrival(at.z - 1 - h, v)

            @pl.when(at.z + h < at.last)
            def _():
                self.x_arrival(at.z + 1 + h, v)

    def beside_order(self, i):
        zo, v = i // PER, lax.rem(i, PER)

        @pl.when(jnp.logical_and(jnp.logical_and(i >= 0, v < UNITS - 1), zo < self.at.z))
        def _():
            self.x_arrival(zo, v)

    def beside_above(self, t):
        at = self.at
        h, v = t // PER, lax.rem(t, PER)

        @pl.when(jnp.logical_and(jnp.logical_and(t >= 0, v < UNITS - 1), at.z + h < at.last))
        def _():
            self.x_arrival(at.z + 1 + h, v)

    def arrived(self, zo):
        at = self.at
        spot = self.w.at[pl.ds(0, 2 * self.rows)]
        at.copy(spot, spot, self.o_s, self.c_r.at[zo], at.z, at.x, 1 - at.c).wait_recv()

    def sent(self):
        at = self.at
        z = at.z

        def wait(tiles, sem):
            spot = self.w.at[pl.ds(0, tiles)]
            at.copy(spot, spot, sem, self.c_r.at[0], z, at.x, 1 - at.c).wait_send()

        def each(zo, carry):
            @pl.when(jnp.logical_and(z < at.last, zo <= z))
            def _():
                wait(PER * self.n, self.up_s.at[zo])

            @pl.when(jnp.logical_and(z > 0, zo >= z))
            def _():
                wait(PER * self.n, self.dn_s.at[zo])

            wait((UNITS - 1) * self.n, self.x_s.at[zo])
            wait(2 * self.rows, self.c_s.at[zo])
            return carry

        lax.fori_loop(0, at.line, each, 0)
        wait(self.n, self.o_s)


def gather_sems(line):
    dma = pltpu.SemaphoreType.DMA
    return [dma((line,)), dma((line,)), dma((line * PER,)), dma((line,)), dma((line * UNITS,)), dma((line,)), dma((line,)), dma]


class Scatter:
    def __init__(self, at, g, rows, cr, xr, zr, keep, stage, wide_stage, behind, lead, sems):
        self.at, self.g, self.rows, self.n = at, g, rows, rows // UNITS
        self.cr, self.xr, self.zr, self.keep, self.stage, self.wide = cr, xr, zr, keep, stage, wide_stage
        self.c_s, self.c_r, self.x_s, self.x_r, self.z_s, self.z_r, self.l_s, self.b_s = sems
        self.lead = lead
        self.behind = behind
        self.items = at.last * PER
        self.final = self.items + lead + at.last + behind
        self.slots = self.final + PER

    def lies(self, u):
        return (u + UNITS // 2) % UNITS * self.n if isinstance(u, int) else lax.rem(u + UNITS // 2, UNITS) * self.n

    def mine(self, zo, xb, u):
        return pl.ds(((zo * 2 + xb) * 2 + self.at.c) * self.rows + self.lies(u), self.n)

    def block_of(self, v):
        x = self.at.x
        return jnp.where(v == 0, 1 - x, x), jnp.where(v == 0, UNITS - 1, v - 1)

    def c_copy(self, zo, xb):
        at = self.at
        src = self.g.at[pl.ds(((zo * 2 + xb) * 2 + 1 - at.c) * self.rows, self.rows)]
        k = zo * 2 + xb
        return at.copy(src, self.cr.at[k], self.c_s.at[zo], self.c_r.at[k], at.z, at.x, 1 - at.c)

    def x_copy(self, zo, u, last=False):
        at = self.at
        k = zo * UNITS + u
        return at.copy(self.g.at[self.mine(zo, 1 - at.x, u)], self.xr.at[k], self.b_s if last else self.x_s.at[zo], self.x_r.at[k],
                       at.z, 1 - at.x, at.c)

    def z_copy(self, to, v, up):
        at = self.at
        xb, u = self.block_of(v)
        there = at.z + 1 if up else at.z - 1
        k = (to if up else jnp.where(to == there, at.line, to)) * PER + v
        return at.copy(self.g.at[self.mine(to, xb, u)], self.zr.at[k], self.z_s.at[to], self.z_r.at[k], there, at.x, at.c)

    def z_wait(self, k):
        at = self.at
        spot = self.zr.at[k]
        at.copy(spot, spot, self.z_s.at[0], self.z_r.at[k], at.z, 1 - at.x, at.c).wait_recv()

    def ready(self, zo):
        for xb in range(2):
            self.c_copy(zo, xb).start()

    def load(self, src, slot):
        return pltpu.make_async_copy(src, self.stage.at[slot, pl.ds(0, self.n)], self.l_s.at[slot])

    def core_part(self, zo, xb, u):
        return self.cr.at[zo * 2 + xb, pl.ds(self.lies(u), self.n)]

    def way(self, t, up):
        at = self.at
        i = t - (at.z if up else at.last - at.z + self.behind)
        to = (at.last if up else at.last - 1) - i // PER
        here = jnp.logical_and(jnp.logical_and(i >= 0, i < self.items), to > at.z if up else to < at.z)
        return to, lax.rem(i, PER), here

    def crossings(self, t):
        at = self.at
        found = []
        for up, slot in ((True, 0), (False, 11)):
            to, v, here = self.way(t, up)
            found.append((to, v - 1, jnp.logical_and(here, jnp.logical_and(v >= 1, v < UNITS)), slot))
        u = t - self.items - 1
        found.append((at.z, u, jnp.logical_and(u >= 0, u < UNITS - 1), 12))
        return found

    def parts(self, t, finals):
        found = [self.way(t - self.lead, up) + (up, slot) for up, slot in ((True, 1), (False, 4))]
        own = t - self.final
        return found + [(self.at.z, own, jnp.logical_and(own >= 0, own < PER), None, 7)] * finals

    def prepare(self, t, finals=False):
        at = self.at
        for to, u, here, slot in self.crossings(t):
            @pl.when(here)
            def _(to=to, u=u, slot=slot):
                @pl.when(u == 0)
                def _():
                    for xb in range(2):
                        self.c_copy(to, xb).wait_recv()

                self.load(self.core_part(to, 1 - at.x, u), slot).start()

        for to, v, here, up, slot in self.parts(t, finals):
            @pl.when(here)
            def _(to=to, v=v, up=up, slot=slot):
                xb, u = self.block_of(v)
                self.load(self.core_part(to, xb, u), slot).start()

                @pl.when(jnp.logical_and(v >= 1, v < (UNITS if up is not None else PER)))
                def _():
                    self.x_copy(to, u).wait_recv()
                    self.load(self.xr.at[to * UNITS + u], slot + 1).start()

                if up is None:
                    @pl.when(at.z > 0)
                    def _():
                        self.z_wait(to * PER + v)
                        self.load(self.zr.at[to * PER + v], slot + 2).start()

                    @pl.when(at.z < at.last)
                    def _():
                        self.z_wait(at.line * PER + v)
                        self.load(self.zr.at[at.line * PER + v], slot + 3).start()
                else:
                    @pl.when(at.z != (0 if up else at.last))
                    def _():
                        self.z_wait(to * PER + v)
                        self.load(self.zr.at[to * PER + v], slot + 2).start()

    def take(self, slot):
        self.load(self.xr.at[0], slot).wait()
        return self.stage[slot].astype(F32)

    def act(self, t, finals):
        at = self.at
        for to, v, here, up, slot in self.parts(t, finals):
            @pl.when(here)
            def _(to=to, v=v, up=up, slot=slot):
                xb, u = self.block_of(v)
                spot = self.mine(to, xb, u)
                acc = self.wide

                acc[: self.n] = self.g[spot].astype(F32) + self.take(slot)

                def more(k):
                    acc[: self.n] = acc[: self.n] + self.take(slot + k)

                @pl.when(jnp.logical_and(v >= 1, v < (UNITS if up is not None else PER)))
                def _():
                    more(1)

                if up is None:
                    @pl.when(at.z > 0)
                    def _():
                        more(2)

                    @pl.when(at.z < at.last)
                    def _():
                        more(3)

                    @pl.when(v == 0)
                    def _():
                        self.g[spot] = acc[: self.n].astype(BF16)
                        self.x_copy(to, UNITS - 1, True).start()

                    @pl.when(v >= 1)
                    def _():
                        self.keep(self.lies(u))
                else:
                    @pl.when(at.z != (0 if up else at.last))
                    def _():
                        more(2)

                    self.g[spot] = acc[: self.n].astype(BF16)
                    self.z_copy(to, v, up).start()

        for to, u, here, slot in self.crossings(t):
            @pl.when(here)
            def _(to=to, u=u, slot=slot):
                spot = self.mine(to, 1 - at.x, u)
                self.g[spot] = (self.g[spot].astype(F32) + self.take(slot)).astype(BF16)
                self.x_copy(to, u).start()

    def slot(self, t, finals=False):
        self.act(t, finals)
        self.prepare(t + 1, finals)

    def sent(self):
        at = self.at
        z = at.z

        def wait(tiles, sem):
            spot = self.g.at[pl.ds(0, tiles)]
            at.copy(spot, spot, sem, self.c_r.at[0], z, at.x, 1 - at.c).wait_send()

        def each(zo, carry):
            @pl.when(zo != z)
            def _():
                wait(PER * self.n, self.z_s.at[zo])

            wait((UNITS - 1) * self.n, self.x_s.at[zo])
            wait(2 * self.rows, self.c_s.at[zo])
            return carry

        lax.fori_loop(0, at.line, each, 0)
        wait(self.n, self.b_s)


def scatter_sems(line):
    dma = pltpu.SemaphoreType.DMA
    return [dma((line,)), dma((line * 2,)), dma((line,)), dma((line * UNITS,)), dma((line,)), dma(((line + 1) * PER,)), dma((13,)), dma]


def landing(line, rows):
    n = rows // UNITS
    shape = lambda *s: jax.ShapeDtypeStruct(s + (16, 128), BF16)
    return [shape(line * 2, rows), shape(line * UNITS, n), shape((line + 1) * PER, n)]


class Edges:
    def __init__(self, at, plan, window, first, spare, land, sems):
        self.at, self.plan, self.window, self.first, self.spare, self.land = at, plan, window, first, spare, land
        self.f_s, self.f_r, self.l_s, self.e_s, self.e_r = sems
        self.d = (at.z * 2 + at.x) * 2 + at.c
        self.end = plan.before + plan.shard

    def over(self, src, dst, send, recv, by):
        return pltpu.make_async_remote_copy(
            src_ref=src, dst_ref=dst, send_sem=send, recv_sem=recv, device_id=(self.at.s, self.d + by), device_id_type=MESH_ID)

    def both(self, up, down):
        @pl.when(self.d < 4 * self.at.line - 1)
        def _():
            up()

        @pl.when(self.d > 0)
        def _():
            down()

    def lands(self, ref):
        plan = self.plan
        return ref.at[pl.ds(0, plan.before)], ref.at[pl.ds(plan.before, plan.after)]

    def outer(self, own):
        plan = self.plan
        before, after = self.lands(self.first)
        return (self.over(own.at[pl.ds(plan.shard - plan.before, plan.before), 0], before, self.f_s.at[0], self.f_r.at[0], 1),
                self.over(own.at[pl.ds(0, plan.after), 0], after, self.f_s.at[1], self.f_r.at[1], -1))

    def send(self, own):
        up, down = self.outer(own)
        self.both(up.start, down.start)

    def inner(self, own):
        return pltpu.make_async_copy(own.at[:, 0], self.window.at[pl.ds(self.plan.before, self.plan.shard)], self.l_s)

    def clear_tiles(self, w):
        w[pl.ds(self.plan.rows * self.d, self.plan.rows)] = jnp.zeros((self.plan.rows, 16, 128), w.dtype)

    def enter(self, own):
        plan = self.plan
        up, down = self.outer(own)

        def above():
            down.wait_recv()
            self.window[self.end : self.end + plan.after, :] = self.first[plan.before : plan.before + plan.after, :]

        def below():
            up.wait_recv()
            self.window[: plan.before, :] = self.first[: plan.before, :]

        self.both(above, below)

    def tiles(self, kinds, w, first, count):
        lo = self.plan.rows * self.d + first

        def act(tile, row, stride, rows):
            value = self.window[pl.ds(row, rows, stride=stride), :]
            if rows < 16:
                value = jnp.concatenate([value, jnp.zeros((16 - rows, 128), value.dtype)], axis=0)
            w[tile] = value.astype(w.dtype)

        self.by_stream(kinds, lo, lo + count, act)

    def entered(self, own):
        up, down = self.outer(own)
        self.both(up.wait_send, down.wait_send)

    def by_stream(self, kinds, lo, hi, act):
        start = self.plan.shard * self.d - self.plan.before
        for s, b in enumerate(kinds):
            @pl.when(self.at.s == s)
            def _(b=b):
                each_tile(b, lo, hi, start, act)

    def clear(self):
        self.window[...] = jnp.zeros(self.window.shape, F32)

    def take(self, kinds, acc, n):
        def keep(first):
            lo = self.plan.rows * self.d + first

            def act(tile, row, stride, rows):
                self.window[pl.ds(row, rows, stride=stride), :] = acc[tile - lo][:rows]

            self.by_stream(kinds, lo, lo + n, act)

        return keep

    def back(self):
        plan = self.plan
        front, rear = self.lands(self.land)
        return (self.over(self.spare.at[pl.ds(0, plan.after)], rear, self.e_s.at[0], self.e_r.at[0], 1),
                self.over(self.window.at[pl.ds(0, plan.before)], front, self.e_s.at[1], self.e_r.at[1], -1))

    def give(self):
        self.spare[: self.plan.after, :] = self.window[self.end : self.end + self.plan.after, :]
        up, down = self.back()
        self.both(up.start, down.start)

    def finish(self, out):
        plan = self.plan
        up, down = self.back()

        def above():
            down.wait_recv()
            spot = slice(self.end - plan.before, self.end)
            self.window[spot, :] = self.window[spot, :] + self.land[: plan.before, :]

        def below():
            up.wait_recv()
            spot = slice(plan.before, plan.before + plan.after)
            self.window[spot, :] = self.window[spot, :] + self.land[plan.before : plan.before + plan.after, :]

        self.both(above, below)
        self.leave(out).start()

    def leave(self, out):
        return pltpu.make_async_copy(self.window.at[pl.ds(self.plan.before, self.plan.shard)], out.at[:, 0], self.l_s)

    def done(self, out):
        self.leave(out).wait()
        up, down = self.back()
        self.both(up.wait_send, down.wait_send)


def edge_sems():
    dma = pltpu.SemaphoreType.DMA
    return [dma((2,)), dma((2,)), dma, dma((2,)), dma((2,))]


def to_flat(flat, box):
    count = box.shape[1] // 128
    for b in range(count):
        flat[pl.ds(b, box.shape[0], stride=count), :] = box[:, b * 128 : (b + 1) * 128].astype(F32)


def from_flat(flat, rows, count, put):
    for j in range(count):
        put(j, flat[pl.ds(j, rows, stride=count), :])


def layer_kernel(plans, line, texts, regions, xbox, gbox, co_flat, sa_flat, *refs):
    kinds = list(zip(plans[0].blocks, plans[1].blocks))
    outs, refs = refs[:10], refs[10:]
    out_box, grad_box, co_out, sa_out = outs[:4]
    wc, ws, vec, vec2, small, pool, land, xp, xin, ret, stage_c, stage_s, acc = refs[:13]
    refs = refs[13:]
    names = sorted(KEPT)
    sc = dict(zip(names, refs[: len(names)]))
    refs = refs[len(names) :]
    ss = dict(zip(names, refs[: len(names)]))
    refs = refs[len(names) :]
    shared = dict(zip(sorted(SHARED), refs[: len(SHARED)]))
    refs = refs[len(SHARED) :]
    ag_c, ag_s, rs_c, rs_s, ed_c, ed_s, y_s, y_r = refs[:8], refs[8:16], refs[16:24], refs[24:32], refs[32:37], refs[37:42], refs[42], refs[43]
    sent = shared["dc"]
    span = pool_span(plans)
    flat = pool.at[pl.ds(6 * span, span)]

    at = Where(line)
    last = at.last
    gc, gs = Gather(at, plans[0].rows, wc, ag_c), Gather(at, plans[1].rows, ws, ag_s)
    edges = []
    rest = max(p.window for p in plans)
    for k, (p, sems) in enumerate(zip(plans, (ed_c, ed_s))):
        sizes = [q.before + q.after for q in plans]
        edges.append(Edges(at, p, pool.at[pl.ds(0, p.window)], pool.at[pl.ds(rest + k * sizes[0], sizes[k])], pool.at[pl.ds(rest, p.after)],
                           land.at[pl.ds(k * sizes[0], sizes[k])], sems))
    ec, es = edges
    own_kinds = [[k[i] for k in kinds] for i in range(2)]
    rc = Scatter(at, wc, plans[0].rows, *outs[4:7], ec.take(own_kinds[0], acc, gc.n), stage_c, acc, 0, 5, rs_c)
    rs = Scatter(at, ws, plans[1].rows, *outs[7:10], es.take(own_kinds[1], acc, gs.n), stage_s, acc, BEHIND, 3, rs_s)

    def over(k, src, dst):
        return at.copy(src, dst, y_s.at[k], y_r.at[k], at.z, at.x, at.c, 1 - at.s)

    ec.inner(co_flat).start()
    at.greet()
    ec.send(co_flat)
    es.send(sa_flat)
    ec.clear_tiles(wc)
    ec.inner(co_flat).wait()

    def begin(k, carry):
        @pl.when(k == 2)
        def _():
            ec.enter(co_flat)

        u = lax.rem(k + UNITS - 1, UNITS)
        ec.tiles(own_kinds[0], wc, gc.lies(u), gc.n)
        gc.start_unit(u)
        return carry

    lax.fori_loop(0, UNITS, begin, 0)
    es.inner(sa_flat).start()
    states = over(0, xbox, xp)
    states.start()
    ec.entered(co_flat)
    es.clear_tiles(ws)
    es.inner(sa_flat).wait()
    es.enter(sa_flat)
    es.tiles(own_kinds[1], ws, 0, plans[1].rows)
    es.entered(sa_flat)
    gs.first()
    gc.other_last(True)

    steps = PER * last
    early = PER

    def co_step(t, carry):
        gc.from_below(t)
        gc.from_above(t)

        @pl.when(t < UNITS - 1)
        def _():
            gc.x_arrival(at.z, t)

        gc.beside_far(t - PER)

        @pl.when(jnp.logical_and(t >= steps - early, at.z < last))
        def _():
            gs.in_order(t - (steps - early) - at.z)

        return carry

    lax.fori_loop(0, steps - early, co_step, 0)
    gs.start()
    gs.other_last(False)
    lax.fori_loop(steps - early, steps, co_step, 0)

    def co_rest(t, carry):
        gc.beside_far(t)
        return carry

    lax.fori_loop(steps - PER, steps, co_rest, 0)
    gs.beside_own()
    for zo in range(line):
        gc.arrived(zo)
    states.wait_recv()

    ahead = jnp.where(at.z < last, early - at.z, 0)

    def self_beside(t):
        gs.beside_order(t + ahead)
        gs.beside_above(t)

    def self_steps(a, b, lag):
        def step(t, carry):
            gs.in_order(t + ahead)
            gs.from_above(t)
            self_beside(t - lag)
            return carry

        lax.fori_loop(a, b, step, 0)

    def self_rest(a, b):
        lax.fori_loop(a, b, lambda t, carry: (self_beside(t), carry)[1], 0)

    gather_steps = steps
    scatter_ticks = sum(SLOTS_TEXT) + sum(SLOTS_CO)

    def run(text, co, sa):
        rows, width = co.rows, co.width

        def view(refs, b):
            d = {name: View(ref, kept_shapes(b)[name]) for name, ref in refs.items()}
            for name, ref in shared.items():
                d[name] = View(ref, shared_shapes(b)[name])
            for k, name in enumerate(("r1", "r2")):
                d[name] = Pooled(pool, (2 * (b is sa) + k) * span, b.rows, b.width)
            d["h"], d["dy"] = [Pooled(pool, k * span, b.rows, b.width) for k in (4, 5)]
            d["small"] = small
            return d

        a = Net(co, wc, vec, view(sc, co))
        b = Net(sa, ws, vec2, view(ss, sa))
        h, hb, dy = b.s["h"], b.s["hb"], b.s["dy"]

        own_in = View(xin, (rows, width))
        if text:
            to_flat(flat, xbox)

            def put(j, value):
                own_in[:, cols(j, 128)] = value.astype(BF16)

            from_flat(flat, rows, width // 128, put)
            x, z = own_in, View(xp, xp.shape)
        else:
            to_flat(flat, xp)
            other = View(xin, (co.other_rows, co.other))

            def put(j, value):
                other[:, cols(j, 128)] = value.astype(BF16)

            from_flat(flat, co.other_rows, co.other // 128, put)
            x, z = View(xbox, xbox.shape), other

        steps_done, beside_done, places = [0], [-PER], [0]

        def tick(k=1):
            a0 = steps_done[0]
            b0 = min(a0 + k, gather_steps)
            if b0 > a0:
                self_steps(a0, b0, a0 - beside_done[0])
                beside_done[0] += b0 - a0
                steps_done[0] = b0

        def need(name):
            later = [sa.place[n][0] for n in ("i_w", "f_w") if sa.place[n][0] > sa.place[name][0]]
            top = -(-min(later + [sa.tiles]) // (4 * gs.rows))
            wanted = min(PER * top, gather_steps)
            tick(min(wanted + 3, gather_steps) - steps_done[0])
            if beside_done[0] < wanted:
                self_rest(beside_done[0], wanted)
                beside_done[0] = wanted
            for zo in range(places[0], top):
                gs.arrived(zo)
            places[0] = max(places[0], top)

        own_counts, other_counts = (texts, regions) if text else (regions, texts)
        value = a.forward(x, x, z, lambda q: other_counts[q], tick)
        h[...] = value
        hb[...] = value.astype(BF16)
        gc.sent()
        if text:
            to_flat(flat, gbox)

            def put(j, value):
                dy[:, cols(j, 128)] = value

            from_flat(flat, rows, width // 128, put)
        else:
            dy[...] = gbox[...].astype(F32)
        value = b.forward(h, hb, hb, lambda q: own_counts[q], tick, need)
        if text:
            for j in range(width // 128):
                flat[pl.ds(j, rows, stride=width // 128), :] = value[:, j * 128 : (j + 1) * 128]
        else:
            out_box[...] = value.astype(BF16)
        gs.sent()

        def put_h(c, value):
            h[:, c] = value

        def add_h(c, value):
            h[:, c] = h[:, c] + value

        ticks = [0]

        def hooks(scatter, block):
            state = [line]

            def done(name):
                tile = block.place[name][0]
                ready = -(-tile // (4 * scatter.rows))
                while state[0] > ready:
                    state[0] -= 1
                    scatter.ready(state[0])
                    if scatter is rs and state[0] == last:
                        rs.prepare(0)

            return done

        def slots(k):
            a0 = ticks[0]
            ticks[0] = a0 + k
            if k:
                lax.fori_loop(a0, a0 + k, lambda t, carry: (rs.slot(t), carry)[1], 0)

        def rs_tick(counts):
            left = list(counts)
            return lambda k=1: slots(left.pop(0))

        b.backward(dy, hb, hb, put_h, add_h, hooks(rs, sa), rs_tick(SLOTS_TEXT if text else SLOTS_IMAGE))
        if text:
            def put(j, value):
                out_box[:, j * 128 : (j + 1) * 128] = value.astype(BF16)

            from_flat(flat, out_box.shape[0], out_box.shape[1] // 128, put)

        def put_own(c, value):
            dy[:, c] = value

        sent_rows = View(sent, (co.other_rows, co.other))

        def put_sent(c, value):
            sent_rows[:, c] = value.astype(BF16)

        a.backward(h, x, z, put_own, put_sent, hooks(rc, co), rs_tick(SLOTS_CO))
        over(1, sent, ret).start()
        assert ticks[0] == scatter_ticks

    for s, (co, sa) in enumerate(kinds):
        @pl.when(at.s == s)
        def _(s=s, co=co, sa=sa):
            run(s == 0, co, sa)

    back = over(1, sent, ret)

    def grads_of_states():
        back.wait_recv()
        for s, (co, sa) in enumerate(kinds):
            @pl.when(at.s == s)
            def _(s=s, co=co):
                mine = Pooled(pool, 5 * span, co.rows, co.width)
                got = View(ret, (co.rows, co.width))
                if s == 0:
                    count = co.width // 128
                    for j in range(count):
                        flat[pl.ds(j, co.rows, stride=count), :] = mine[:, cols(j, 128)] + got[:, cols(j, 128)].astype(F32)

                    def put(j, value):
                        grad_box[:, j * 128 : (j + 1) * 128] = value

                    from_flat(flat, grad_box.shape[0], grad_box.shape[1] // 128, put)
                else:
                    grad_box[...] = mine[...] + got[...].astype(F32)

    rc.prepare(0)
    es.clear()
    shift = rs.items
    steps = shift + rc.slots

    def both(t, carry):
        @pl.when(t < rs.slots)
        def _():
            rs.slot(t, True)

        @pl.when(t == rs.slots)
        def _():
            es.give()

        @pl.when(t == rs.slots + 2)
        def _():
            es.finish(sa_out)

        @pl.when(t == rs.slots + 4)
        def _():
            es.done(sa_out)
            ec.clear()
            rs.sent()

        @pl.when(t == shift + rc.final - 1)
        def _():
            grads_of_states()

        @pl.when(t >= shift)
        def _():
            rc.slot(t - shift, True)

        @pl.when(t == shift + rc.final + 4)
        def _():
            ec.give()

        return carry

    assert rs.slots + 4 < shift + rc.final
    lax.fori_loop(scatter_ticks, steps, both, 0)
    ec.finish(co_out)
    back.wait_send()
    states.wait_send()
    rc.sent()
    ec.done(co_out)


KEPT = ("q", "k", "v", "p", "c", "y1", "a", "gp")
SHARED = ("fill", "m", "hb", "dc")


def kept_shapes(b):
    return {k: v[0] for k, v in scratch_of(b).items()}


def shared_shapes(b):
    rows, width = b.rows, b.width
    return {"fill": (b.rows, b.other_rows), "m": (rows, width), "hb": (rows, width), "dc": (rows, b.inner)}


SHARED_TYPES = {"fill": F32}


def most(shapes):
    return tuple(max(k) for k in zip(*shapes))


def pool_span(plans):
    return max(b.rows * b.width // 128 for p in plans for b in p.blocks)


def layer_call(plans, line, texts, regions, xbox, gbox, co_flat, sa_flat, cid):
    vm = pl.BlockSpec(memory_space=pltpu.VMEM)
    any_ = pl.BlockSpec(memory_space=pl.ANY)
    rows_c, rows_s = [p.rows for p in plans]
    V = pltpu.VMEM
    cos, sas = [p.blocks for p in plans]
    wide = most([(b.rows, b.width) for b in cos] + [(b.other_rows, b.other) for b in cos])
    n = max(rows_c, rows_s) // UNITS
    edge = sum(p.before + p.after for p in plans)
    assert max(p.window for p in plans) + edge <= 5 * pool_span(plans)
    scr = [V((plans[0].tiles, 16, 128), BF16), V((plans[1].tiles, 16, 128), BF16), V((16, 3072), F32), V((16, 3072), F32), V((32, 128), F32),
           V((7 * pool_span(plans), 128), F32), V((edge, 128), F32), V(xbox.shape, BF16), V(wide, BF16), V(wide, BF16),
           V((13, rows_c // UNITS, 16, 128), BF16), V((13, rows_s // UNITS, 16, 128), BF16), V((n, 16, 128), F32)]
    for bs in (cos, sas):
        for name in sorted(KEPT):
            scr.append(V(most([kept_shapes(b)[name] for b in bs]), scratch_of(bs[0])[name][1]))
    for name in sorted(SHARED):
        shape = most([shared_shapes(b)[name] for b in cos + sas] + ([wide] if name == "dc" else []))
        scr.append(V(shape, SHARED_TYPES.get(name, BF16)))
    dma = pltpu.SemaphoreType.DMA
    scr += gather_sems(line) + gather_sems(line) + scatter_sems(line) + scatter_sems(line) + edge_sems() + edge_sems() + [dma((2,)), dma((2,))]
    struct = jax.ShapeDtypeStruct
    outs = [struct(xbox.shape, BF16), struct(xbox.shape, F32), struct(co_flat.shape, F32), struct(sa_flat.shape, F32)]
    outs += landing(line, rows_c) + landing(line, rows_s)
    return pl.pallas_call(
        functools.partial(layer_kernel, plans, line),
        out_shape=outs,
        in_specs=[pl.BlockSpec(memory_space=pltpu.SMEM)] * 2 + [vm, vm, any_, any_],
        out_specs=[vm, vm] + [any_] * 8,
        scratch_shapes=scr,
        compiler_params=pltpu.CompilerParams(collective_id=cid, has_side_effects=True, vmem_limit_bytes=64 * 2**20 - 2**16),
        name="layer",
    )(texts, regions, xbox, gbox, co_flat, sa_flat)[:4]


DT, HT, FT = 768, 12, 3072
DI, HI, FI = 1024, 8, 1024
DC, HC = 1024, 8
LT, LI = 128, 96
LINE_MAX = 8


def blocks_of(text, seqs):
    if text:
        return (Block(DT, DI, DC, FT, HC, LT, LI, seqs), Block(DT, DT, DT, FT, HT, LT, LT, seqs))
    return (Block(DI, DT, DC, FI, HC, LI, LT, seqs), Block(DI, DI, DI, FI, HI, LI, LI, seqs))


class Plan:
    def __init__(self, blocks, devices, flat_total):
        self.blocks = blocks
        self.shard = flat_total // 128 // devices
        tiles = max(b.tiles for b in blocks)
        self.rows = -(-tiles // (devices * UNITS)) * UNITS
        self.tiles = self.rows * devices
        tables = [self.table(b).reshape(self.tiles, 16) for b in blocks]
        before = after = 0
        inner = True
        for table in tables:
            most = table.max(axis=1)
            least = np.where(table >= 0, table, flat_total).min(axis=1)
            for d in range(devices):
                lo, hi, start, end = self.rows * d, self.rows * (d + 1), self.shard * d, self.shard * (d + 1)
                held = np.nonzero(most[lo:hi] >= 0)[0] + lo
                if held.size:
                    before = max(before, start - least[held].min())
                    after = max(after, most[held].max() + 1 - end)
                    unit = (held - lo) * UNITS // self.rows
                    outer = (least[held] < start) & (unit > 0) | (most[held] >= end) & (unit < UNITS // 2)
                    inner = inner and not outer.any()
        self.before, self.after = [max(-(-int(k) // 16) * 16, 16) for k in (before, after)]
        self.window = -(-(self.before + self.shard + self.after) // 8) * 8
        self.near = max(self.before, self.after) <= self.shard and inner

    def table(self, b):
        index = np.full((self.tiles * 16,), -1, np.int32)
        for first, flat, k, rows, nb in b.parts:
            if k:
                r, j = np.arange(k)[:, None], np.arange(nb)[None]
                at = first * 16 + ((r // 16) * nb + j) * 16 + r % 16
                index[at.reshape(-1)] = (flat + r * nb + j).reshape(-1)
            else:
                index[first * 16 : first * 16 + rows] = flat + np.arange(rows)
        return index


def each_tile(b, lo, hi, start, act):
    for first, flat, k, rows, nb in b.parts:
        if k:
            count = rows // 16
            a = jnp.clip(lo - first, 0, count)
            z = jnp.clip(hi - first, 0, count)

            def body(t, carry, first=first, flat=flat, nb=nb):
                i = t // nb
                act(first + t, flat + i * 16 * nb + (t - i * nb) - start, nb, 16)
                return carry

            lax.fori_loop(a, z, body, 0)
        else:
            for t in range((rows + 15) // 16):
                @pl.when(jnp.logical_and(first + t >= lo, first + t < hi))
                def _(t=t, first=first, flat=flat, rows=rows):
                    act(first + t, flat + 16 * t - start, 1, min(16, rows - 16 * t))


def gathered(plan, text, flat):
    whole = lax.all_gather(flat.astype(BF16), "dp", axis=0, tiled=True).reshape(-1, 128)
    index = jnp.where(text, *[jnp.asarray(plan.table(b)) for b in plan.blocks])
    rows = jnp.where((index >= 0)[:, None], whole[jnp.maximum(index, 0)], jnp.zeros((), BF16))
    return rows.reshape(plan.tiles, 16, 128)


def scattered(plan, text, tiles, flat_rows):
    tables = []
    for b in plan.blocks:
        table = plan.table(b)
        back = np.full((flat_rows,), -1, np.int32)
        held = np.nonzero(table >= 0)[0]
        back[table[held]] = held
        tables.append(jnp.asarray(back))
    index = jnp.where(text, *tables)
    rows = jnp.where((index >= 0)[:, None], tiles.reshape(-1, 128)[jnp.maximum(index, 0)], jnp.zeros((), BF16))
    return lax.psum_scatter(rows.astype(F32), "dp", scatter_dimension=0, tiled=True).reshape(-1)


def layer_alone(text, counts, own, partner, grad, wco, wsa):
    seqs = own.shape[0]
    co, sa = blocks_of(text, seqs)
    box = own.shape
    lens = counts if text else counts[::-1]
    out, own_grad, sent, gco, gsa = compute(
        co, sa, lens, own.reshape(co.rows, co.width), partner.reshape(co.other_rows, co.other),
        grad.reshape(co.rows, co.width), wco, wsa)
    return out.reshape(box), own_grad.reshape(box), sent.reshape(box), gco, gsa


def body(devices, states, out_grad, co_params, self_params, text_lengths, region_counts):
    own = states[0]
    seqs = own.shape[0]
    text = lax.axis_index("stream") == 0
    flats = (co_params[0], self_params[0])
    streams = [blocks_of(t, seqs) for t in (True, False)]
    plans = [Plan([k[i] for k in streams], devices, f.shape[0] * devices) for i, f in enumerate(flats)]
    line = devices // 4
    if devices % 4 == 0 and line <= LINE_MAX and all(p.near for p in plans):
        box = (own.shape[0] * own.shape[1], own.shape[2])
        flats = [f.reshape(p.shard, 1, 128) for p, f in zip(plans, flats)]
        out, grad, co_grad, sa_grad = layer_call(plans, line, text_lengths, region_counts, own.reshape(box), out_grad[0].reshape(box), *flats, 1)
        return (out.reshape(states.shape), grad.reshape(states.shape), co_grad.reshape(co_params.shape), sa_grad.reshape(self_params.shape))
    swap = [(0, 1), (1, 0)]
    partner = lax.ppermute(own, "stream", swap)
    wco, wsa = [gathered(p, text, f) for p, f in zip(plans, flats)]
    counts = jnp.stack([text_lengths, region_counts])
    out, own_grad, sent, gco, gsa = lax.cond(
        text, functools.partial(layer_alone, True), functools.partial(layer_alone, False),
        counts, own, partner, out_grad[0], wco, wsa)
    returned = lax.ppermute(sent, "stream", swap)
    flats = [scattered(p, text, g, p.shard * devices) for p, g in zip(plans, (gco, gsa))]
    return (out[None], (own_grad + returned.astype(F32))[None], flats[0][None], flats[1][None])


def solution(mesh):
    states = P("stream", "dp", None, None)
    flat = P("stream", "dp")
    return jax.shard_map(
        functools.partial(body, mesh.shape["dp"]), mesh=mesh, in_specs=(states, states, flat, flat, P("dp"), P("dp")),
        out_specs=(states, states, flat, flat), check_vma=False)
```

```python
import functools
import math

import jax
import jax.numpy as jnp
import numpy as np
from jax import lax
from jax.experimental import pallas as pl
from jax.experimental.pallas import tpu as pltpu
from jax.sharding import PartitionSpec as P


MESH_ID = pl.DeviceIdType.MESH
UNITS = 6


def place(line):
    d = lax.axis_index("dp")
    return d // 4, lax.rem(d // 2, 2), lax.rem(d, 2)


F32, BF16 = jnp.float32, jnp.bfloat16
NT = (((1,), (1,)), ((), ()))
TN = (((0,), (0,)), ((), ()))
norm_eps = 1e-12
masked_score = -1000000000.0
other_sequence = -3.0e38


def dot(a, b, dims=(((1,), (0,)), ((), ()))):
    return lax.dot_general(a, b, dims, preferred_element_type=F32)


class Block:
    def __init__(self, width, other, inner, hidden, heads, length, other_length, seqs, base=0):
        self.width, self.other, self.inner, self.hidden, self.heads = width, other, inner, hidden, heads
        self.length, self.other_length, self.seqs = length, other_length, seqs
        self.rows, self.other_rows = length * seqs, other_length * seqs
        self.base = base
        self.place = {}
        self.parts = []
        tile, flat = 0, 0

        def matrix(name, k, n):
            nonlocal tile, flat
            self.place[name] = (tile, k, n)
            self.parts.append((tile, flat, k, k * n // 128, n // 128))
            tile, flat = tile + k * n // 2048, flat + k * n // 128

        def vectors(*names):
            nonlocal tile, flat
            rows = 0
            for name, size in names:
                self.place[name] = (tile, rows, size)
                rows += size // 128
            self.parts.append((tile, flat, 0, rows, 0))
            tile, flat = tile + (rows + 15) // 16, flat + rows

        matrix("q_w", width, inner)
        vectors(("q_b", inner))
        matrix("k_w", other, inner)
        matrix("v_w", other, inner)
        vectors(("v_b", inner))
        matrix("o_w", inner, width)
        vectors(("o_b", width), ("g1", width), ("b1", width))
        matrix("i_w", width, hidden)
        vectors(("i_b", hidden))
        matrix("f_w", hidden, width)
        vectors(("f_b", width), ("g2", width), ("b2", width))
        self.tiles, self.flat_rows = tile, flat


VECS = ("q_b", "v_b", "o_b", "g1", "b1", "i_b", "f_b", "g2", "b2")
GROUPS = (("q_b",), ("v_b",), ("o_b", "g1", "b1"), ("i_b",), ("f_b", "g2", "b2"))


class Cols:
    def __init__(self, j, size):
        self.j, self.size = j, size

    def ds(self):
        return pl.ds(pl.multiple_of(self.j * self.size, self.size), self.size)


def cols(j, size=256):
    return Cols(j, size)


class Pooled:
    def __init__(self, pool, base, rows, width):
        self.pool, self.base, self.rows, self.count = pool, base, rows, width // 128

    def spots(self, index):
        if index is Ellipsis:
            first, count = 0, self.count
        else:
            run = index[1]
            count = run.size // 128
            first = run.j * count
        return [pl.ds(pl.multiple_of(self.base + (first + i) * self.rows, 8), self.rows) for i in range(count)]

    def __getitem__(self, index):
        return jnp.concatenate([self.pool[spot, :] for spot in self.spots(index)], axis=1)

    def __setitem__(self, index, value):
        for i, spot in enumerate(self.spots(index)):
            self.pool[spot, :] = value[:, i * 128 : (i + 1) * 128]


class View:
    def __init__(self, ref, shape):
        self.ref, self.shape = ref, tuple(shape)

    def whole(self, index):
        index = () if index is Ellipsis else index if isinstance(index, tuple) else (index,)
        index = index + (slice(None),) * (len(self.shape) - len(index))
        index = [i.ds() if isinstance(i, Cols) else i for i in index]
        return tuple(slice(0, k) if isinstance(i, slice) and i == slice(None) else i for i, k in zip(index, self.shape))

    def __getitem__(self, index):
        return self.ref[self.whole(index)]

    def __setitem__(self, index, value):
        self.ref[self.whole(index)] = value


NN_STEP, NT_STEP, TN_STEP, TN_WIDE = 1024, 1024, 1024, 768


def step_of(n, most):
    return max(k for k in range(256, most + 1, 256) if n % k == 0)


class Net:
    def __init__(self, b, w, vec, sc):
        self.b, self.w, self.vec, self.s = b, w, vec, sc

    def mat(self, name):
        tile, k, n = self.b.place[name]
        return self.w.at[pl.ds(self.b.base + tile, k * n // 2048)].reshape(k // 16, n // 128, 16, 128)

    def row(self, name, c=None):
        k = VECS.index(name)
        size = self.b.place[name][2]
        return self.vec[k : k + 1, :size] if c is None else self.vec[k : k + 1, c.ds()]

    def load_vectors(self, groups):
        for group in groups:
            tile = self.b.place[group[0]][0]
            rows = sum(self.b.place[g][2] for g in group) // 128
            count = (rows + 15) // 16
            value = self.w[pl.ds(self.b.base + tile, count)].reshape(count * 16, 128).astype(F32)
            r = 0
            for name in group:
                k = VECS.index(name)
                for j in range(self.b.place[name][2] // 128):
                    self.vec[k : k + 1, j * 128 : (j + 1) * 128] = value[r : r + 1]
                    r += 1

    def store_vectors(self, group, scratch):
        tile = self.b.place[group[0]][0]
        rows = sum(self.b.place[g][2] for g in group) // 128
        count = (rows + 15) // 16
        scratch[0 : count * 16] = jnp.zeros((count * 16, 128), F32)
        r = 0
        for name in group:
            k = VECS.index(name)
            for j in range(self.b.place[name][2] // 128):
                scratch[r : r + 1, :] = self.vec[k : k + 1, j * 128 : (j + 1) * 128]
                r += 1
        self.w[pl.ds(self.b.base + tile, count)] = scratch[0 : count * 16].astype(BF16).reshape(count, 16, 128)

    def nn(self, x, name, put):
        m = self.mat(name)
        k, n = self.b.place[name][1:]
        step = step_of(n, NN_STEP)

        def body(j, carry):
            per = step // 128
            w = jnp.concatenate([m[:, per * j + i].reshape(k, 128) for i in range(per)], axis=1)
            put(cols(j, step), dot(x[...], w))
            return carry

        lax.fori_loop(0, n // step, body, 0)

    def rows_of(self, name, j, step):
        m = self.mat(name)
        strips = step // 16
        return jnp.concatenate([m[pl.ds(j * strips, strips), i].reshape(step, 128) for i in range(m.shape[1])], axis=1)

    def nt(self, g, name, put):
        k, n = self.b.place[name][1:]
        step = step_of(k, NT_STEP)

        def body(j, carry):
            put(cols(j, step), dot(g[...], self.rows_of(name, j, step), NT))
            return carry

        lax.fori_loop(0, k // step, body, 0)

    def tn(self, a, g, name):
        m = self.mat(name)
        k, n = self.b.place[name][1:]
        step, wide = step_of(k, TN_STEP), step_of(n, TN_WIDE)
        strips = step // 16

        def body(j, carry):
            left = a[:, cols(j, step)].T
            for i in range(n // wide):
                got = dot(left, g[:, cols(i, wide)]).astype(BF16)
                for c in range(wide // 128):
                    m[pl.ds(j * strips, strips), i * (wide // 128) + c] = got[:, c * 128 : (c + 1) * 128].reshape(strips, 16, 128)
            return carry

        lax.fori_loop(0, k // step, body, 0)

    def norm(self, r, gain, shift):
        centre = r - jnp.mean(r, axis=-1, keepdims=True)
        spread = jnp.mean(centre * centre, axis=-1, keepdims=True)
        return centre * lax.rsqrt(spread + norm_eps) * self.row(gain) + self.row(shift)

    def norm_back(self, r, dy, gain, shift):
        centre = r - jnp.mean(r, axis=-1, keepdims=True)
        spread = jnp.mean(centre * centre, axis=-1, keepdims=True)
        s = lax.rsqrt(spread + norm_eps)
        xh = centre * s
        t = dy * self.row(gain)
        dr = s * (t - jnp.mean(t, axis=-1, keepdims=True) - xh * jnp.mean(t * xh, axis=-1, keepdims=True))
        size = self.b.width
        kg, kb = VECS.index(gain), VECS.index(shift)
        self.vec[kg : kg + 1, :size] = jnp.sum(dy * xh, axis=0, keepdims=True)
        self.vec[kb : kb + 1, :size] = jnp.sum(dy, axis=0, keepdims=True)
        return dr

    def put_sum(self, name, ref):
        k = VECS.index(name)
        self.vec[k : k + 1, : self.b.place[name][2]] = jnp.sum(ref[...].astype(F32), axis=0, keepdims=True)

    def mask(self, fill, counts):
        b = self.b
        shape = (b.rows, b.other_rows)
        row = lax.broadcasted_iota(jnp.int32, shape, 0)
        col = lax.broadcasted_iota(jnp.int32, shape, 1)
        value = jnp.full(shape, other_sequence, F32)
        for q in range(b.seqs):
            mine = (row >= q * b.length) & (row < (q + 1) * b.length)
            mine = mine & (col >= q * b.other_length) & (col < (q + 1) * b.other_length)
            value = jnp.where(mine, jnp.where(col < q * b.other_length + counts(q), 1.0, masked_score), value)
        fill[...] = value

    def heads_of(self, refs, g):
        e = self.b.inner // self.b.heads
        values = [ref[:, cols(g, 128)] for ref in refs]
        if e == 128:
            return [values]
        lane = lax.broadcasted_iota(jnp.int32, (1, 128), 1)
        return [
            [jnp.where((lane >= h * e) & (lane < (h + 1) * e), value, jnp.zeros((), BF16)) for value in values]
            for h in range(128 // e)]

    def attend(self, q, k, v, fill, p, c):
        b = self.b
        e = b.inner // b.heads
        scale = 1.0 / math.sqrt(e)
        per = max(128 // e, 1)

        def body(g, carry):
            keys = k[:, cols(g, 128)]
            total = None
            for h, (qh,) in enumerate(self.heads_of([q], g)):
                vh = self.heads_of([v], g)[h][0]
                s = dot(qh, keys, NT) * scale
                f = fill[...]
                s = jnp.where(f > 0, s, f)
                ex = jnp.exp(s - jnp.max(s, axis=-1, keepdims=True))
                probs = (ex * (1.0 / jnp.sum(ex, axis=-1, keepdims=True))).astype(BF16)
                p[g * per + h] = probs
                got = dot(probs, vh)
                total = got if total is None else total + got
            c[:, cols(g, 128)] = total.astype(BF16)
            return carry

        lax.fori_loop(0, b.inner // 128, body, 0, unroll=2)

    def attend_back(self, q, k, v, p, dc):
        b = self.b
        e = b.inner // b.heads
        scale = 1.0 / math.sqrt(e)
        per = max(128 // e, 1)

        def body(g, carry):
            values = v[:, cols(g, 128)]
            sums = None
            for h, (qh, kh, dh) in enumerate(self.heads_of([q, k, dc], g)):
                probs = p[g * per + h]
                dp = dot(dh, values, NT)
                wide = probs.astype(F32)
                ds = (wide * (dp - jnp.sum(wide * dp, axis=-1, keepdims=True))).astype(BF16)
                got = [dot(ds, kh), dot(ds, qh, TN), dot(probs, dh, TN)]
                sums = got if sums is None else [x + y for x, y in zip(sums, got)]
            q[:, cols(g, 128)] = (sums[0] * scale).astype(BF16)
            k[:, cols(g, 128)] = (sums[1] * scale).astype(BF16)
            v[:, cols(g, 128)] = sums[2].astype(BF16)
            return carry

        lax.fori_loop(0, b.inner // 128, body, 0, unroll=2)

    def forward(self, x, u, z, counts, tick=lambda k=1: None, need=lambda name: None):
        s, b = self.s, self.b
        need("o_w")
        self.load_vectors(GROUPS[:3])
        self.mask(s["fill"], counts)

        def put(ref, bias=None):
            def store(c, value):
                if bias is not None:
                    value = value + self.row(bias, c)
                ref[:, c] = value.astype(BF16)
            return store

        tick()
        self.nn(u, "q_w", put(s["q"], "q_b"))
        self.nn(z, "k_w", put(s["k"]))
        tick()
        self.nn(z, "v_w", put(s["v"], "v_b"))
        tick()
        self.attend(s["q"], s["k"], s["v"], s["fill"], s["p"], s["c"])

        tick()

        def first(c, value):
            s["r1"][:, c] = x[:, c].astype(F32) + (value + self.row("o_b", c))

        self.nn(s["c"], "o_w", first)
        y1 = self.norm(s["r1"][...], "g1", "b1")
        s["r2"][...] = y1
        s["y1"][...] = y1.astype(BF16)

        def up(c, value):
            value = value + self.row("i_b", c)
            half = 0.5 * (1.0 + lax.erf(value * (1.0 / math.sqrt(2.0))))
            s["a"][:, c] = (value * half).astype(BF16)
            s["gp"][:, c] = (half + value * (jnp.exp(-0.5 * value * value) * (1.0 / math.sqrt(2.0 * math.pi)))).astype(BF16)

        tick()
        need("i_w")
        self.load_vectors(GROUPS[3:4])
        self.nn(s["y1"], "i_w", up)
        tick()
        need("f_w")
        self.load_vectors(GROUPS[4:])

        def second(c, value):
            s["r2"][:, c] = s["r2"][:, c] + (value + self.row("f_b", c))

        self.nn(s["a"], "f_w", second)
        return self.norm(s["r2"][...], "g2", "b2")

    def backward(self, dy, u, z, put_resid, put_z, done, tick=lambda k=1: None):
        s, b = self.s, self.b
        small = s["small"]
        dr2 = self.norm_back(s["r2"][...], dy[...], "g2", "b2")
        dy[...] = dr2
        s["m"][...] = dr2.astype(BF16)
        self.put_sum("f_b", s["m"])

        def inner(c, value):
            s["gp"][:, c] = (value * s["gp"][:, c].astype(F32)).astype(BF16)

        self.nt(s["m"], "f_w", inner)
        self.store_vectors(GROUPS[4], small)
        self.tn(s["a"], s["m"], "f_w")
        done("f_w")
        self.put_sum("i_b", s["gp"])

        def mid(c, value):
            dy[:, c] = dy[:, c] + value

        self.nt(s["gp"], "i_w", mid)
        tick(4)
        self.store_vectors(GROUPS[3], small)
        self.tn(s["y1"], s["gp"], "i_w")
        done("i_w")
        tick()
        dr1 = self.norm_back(s["r1"][...], dy[...], "g1", "b1")
        dy[...] = dr1
        s["m"][...] = dr1.astype(BF16)
        self.put_sum("o_b", s["m"])

        def context(c, value):
            s["dc"][:, c] = value.astype(BF16)

        self.nt(s["m"], "o_w", context)
        self.store_vectors(GROUPS[2], small)
        self.tn(s["c"], s["m"], "o_w")
        done("o_w")
        tick(3)
        self.attend_back(s["q"], s["k"], s["v"], s["p"], s["dc"])

        tick(2)

        def resid(c, value):
            put_resid(c, dy[:, c] + value)

        self.nt(s["q"], "q_w", resid)
        k = b.place["v_w"][1]
        step = step_of(k, NT_STEP)

        def body(j, carry):
            value = dot(s["k"][...], self.rows_of("k_w", j, step), NT) + dot(s["v"][...], self.rows_of("v_w", j, step), NT)
            put_z(cols(j, step), value)
            return carry

        lax.fori_loop(0, k // step, body, 0)
        tick()
        self.put_sum("q_b", s["q"])
        self.put_sum("v_b", s["v"])
        self.store_vectors(GROUPS[0], small)
        self.store_vectors(GROUPS[1], small)
        self.tn(u, s["q"], "q_w")
        self.tn(z, s["k"], "k_w")
        self.tn(z, s["v"], "v_w")
        done("q_w")
        tick(2)


def scratch_of(b):
    return {
        "q": ((b.rows, b.inner), BF16), "k": ((b.other_rows, b.inner), BF16), "v": ((b.other_rows, b.inner), BF16),
        "p": ((b.heads, b.rows, b.other_rows), BF16), "c": ((b.rows, b.inner), BF16),
        "r1": ((b.rows, b.width), F32), "r2": ((b.rows, b.width), F32), "y1": ((b.rows, b.width), BF16),
        "a": ((b.rows, b.hidden), BF16), "gp": ((b.rows, b.hidden), BF16), "fill": ((b.rows, b.other_rows), F32)}


def compute_kernel(co, sa, lens, x, xp, gy, wco, wsa, out, own_grad, sent, gco, gsa, wc, ws, vec, vec2, small, sems, *scr):
    names = sorted(scratch_of(co))
    sc = dict(zip(names, scr[: len(names)]))
    ss = dict(zip(names, scr[len(names) : 2 * len(names)]))
    rest = scr[2 * len(names) :]
    m, dy, h, hb, dcc, dcs = rest
    for d, dc in ((sc, dcc), (ss, dcs)):
        d["m"], d["small"], d["dc"] = m, small, dc
    x, xp = View(x, (co.rows, co.width)), View(xp, (co.other_rows, co.other))
    own_grad, sent = View(own_grad, (co.rows, co.width)), View(sent, (co.other_rows, co.other))
    h, hb, dy = [View(r, (co.rows, co.width)) for r in (h, hb, dy)]
    for b, d in ((co, sc), (sa, ss)):
        shapes = {**{n: k[0] for n, k in scratch_of(b).items()}, "m": (b.rows, b.width), "dc": (b.rows, b.inner)}
        for n, shape in shapes.items():
            d[n] = View(d[n], shape)
    copies = [pltpu.make_async_copy(wco, wc, sems.at[0]), pltpu.make_async_copy(wsa, ws, sems.at[1])]
    for cp in copies:
        cp.start()
    copies[0].wait()
    a = Net(co, wc, vec, sc)
    bnet = Net(sa, ws, vec2, ss)
    value = a.forward(x, x, xp, lambda q: lens[1, q])
    h[...] = value
    hb[...] = value.astype(BF16)
    copies[1].wait()
    out[...] = bnet.forward(h, hb, hb, lambda q: lens[0, q]).astype(BF16)
    dy[...] = gy[...].astype(F32)

    def put_h(c, value):
        h[:, c] = value

    def add_h(c, value):
        h[:, c] = h[:, c] + value

    bnet.backward(dy, hb, hb, put_h, add_h, lambda name: None)
    back = pltpu.make_async_copy(ws, gsa, sems.at[1])
    back.start()

    def put_own(c, value):
        own_grad[:, c] = value

    def put_sent(c, value):
        sent[:, c] = value.astype(BF16)

    a.backward(h, x, xp, put_own, put_sent, lambda name: None)
    back2 = pltpu.make_async_copy(wc, gco, sems.at[0])
    back2.start()
    back.wait()
    back2.wait()


def compute(co, sa, lens, x, xp, gy, wco, wsa):
    any_ = pl.BlockSpec(memory_space=pl.ANY)
    vm = pl.BlockSpec(memory_space=pltpu.VMEM)
    names = sorted(scratch_of(co))
    V = lambda shape, dtype: pltpu.VMEM(shape, dtype)
    scr = [V(wco.shape, BF16), V(wsa.shape, BF16), V((16, 3072), F32), V((16, 3072), F32), V((32, 128), F32), pltpu.SemaphoreType.DMA((2,))]
    scr += [V(*scratch_of(co)[n]) for n in names] + [V(*scratch_of(sa)[n]) for n in names]
    rows, width = co.rows, co.width
    scr += [V((rows, width), BF16), V((rows, width), F32), V((rows, width), F32), V((rows, width), BF16)]
    scr += [V((b.rows, b.inner), BF16) for b in (co, sa)]
    return pl.pallas_call(
        functools.partial(compute_kernel, co, sa),
        out_shape=(jax.ShapeDtypeStruct((rows, width), BF16), jax.ShapeDtypeStruct((rows, width), F32),
                   jax.ShapeDtypeStruct((co.other_rows, co.other), BF16),
                   jax.ShapeDtypeStruct(wco.shape, BF16), jax.ShapeDtypeStruct(wsa.shape, BF16)),
        in_specs=[pl.BlockSpec(memory_space=pltpu.SMEM), vm, vm, vm, any_, any_],
        out_specs=(vm, vm, vm, any_, any_),
        scratch_shapes=scr,
        compiler_params=pltpu.CompilerParams(vmem_limit_bytes=63 * 2**20),
        name="compute",
    )(lens, x, xp, gy, wco, wsa)


PER = UNITS + 1
SLOTS_TEXT, SLOTS_IMAGE, SLOTS_CO = (2, 4, 3, 2, 1, 1), (2, 0, 4, 2, 1, 4), (1, 1, 0, 1, 0, 1)
HOP = 3
BEHIND = 2


class Where:
    def __init__(self, line):
        self.line, self.last = line, line - 1
        self.z, self.x, self.c = place(line)
        self.s = lax.axis_index("stream")

    def copy(self, src, dst, send, recv, z, x, c, s=None):
        return pltpu.make_async_remote_copy(
            src_ref=src, dst_ref=dst, send_sem=send, recv_sem=recv,
            device_id=(self.s if s is None else s, (z * 2 + x) * 2 + c), device_id_type=MESH_ID)

    def greet(self):
        z, x, c, s = self.z, self.x, self.c, self.s
        barrier = pltpu.get_barrier_semaphore()

        def signal(zz, xx, cc, ss):
            pl.semaphore_signal(barrier, inc=1, device_id=(ss, (zz * 2 + xx) * 2 + cc), device_id_type=MESH_ID)

        signal(z, 1 - x, c, s)
        signal(z, x, 1 - c, s)
        signal(z, x, c, 1 - s)
        d = (z * 2 + x) * 2 + c
        beside = (1 - c) * jnp.minimum(d, 1) + c * jnp.minimum(4 * self.line - 1 - d, 1)

        @pl.when(beside > 0)
        def _():
            pl.semaphore_signal(barrier, inc=1, device_id=(s, d - 1 + 2 * c), device_id_type=MESH_ID)

        @pl.when(z > 0)
        def _():
            signal(z - 1, x, c, s)

        @pl.when(z < self.last)
        def _():
            signal(z + 1, x, c, s)

        pl.semaphore_wait(barrier, 3 + jnp.minimum(z, 1) + jnp.minimum(self.last - z, 1) + beside)


class Gather:
    def __init__(self, at, rows, w, sems):
        self.at, self.rows, self.w = at, rows, w
        self.n = self.rows // UNITS
        self.up_s, self.dn_s, self.z_r, self.x_s, self.x_r, self.c_s, self.c_r, self.o_s = sems

    def lies(self, u):
        return jnp.where(u == 0, 1, jnp.where(u < 4, u + 2, jnp.where(u == 4, 0, 2))) * self.n

    def spot(self, zo, xb, cc, u):
        return self.w.at[pl.ds(((zo * 2 + xb) * 2 + cc) * self.rows + self.lies(u), self.n)]

    def block_of(self, v):
        x = self.at.x
        return jnp.where(v == UNITS, 1 - x, x), jnp.minimum(v, UNITS - 1)

    def z_copy(self, zo, v, up):
        at = self.at
        xb, u = self.block_of(v)
        spot = self.spot(zo, xb, at.c, u)
        return at.copy(spot, spot, (self.up_s if up else self.dn_s).at[zo], self.z_r.at[zo * PER + v], at.z + 1 if up else at.z - 1, at.x, at.c)

    def x_copy(self, zo, u, arriving=False, first=False):
        at = self.at
        spot = self.spot(zo, 1 - at.x if arriving else at.x, at.c, u)
        return at.copy(spot, spot, self.o_s if first else self.x_s.at[zo], self.x_r.at[zo * UNITS + u], at.z, 1 - at.x, at.c)

    def c_copy(self, zo, xb, u):
        at = self.at
        spot = self.spot(zo, xb, at.c, u)
        return at.copy(spot, spot, self.c_s.at[zo], self.c_r.at[zo], at.z, at.x, 1 - at.c)

    def send_z(self, zo, v, up):
        at = self.at

        @pl.when(at.z < at.last if up else at.z > 0)
        def _():
            self.z_copy(zo, v, up).start()

    def first(self):
        self.x_copy(self.at.z, UNITS - 1, first=True).start()

    def start_unit(self, u):
        at = self.at

        @pl.when(u == UNITS - 1)
        def _():
            self.first()

        @pl.when(u != UNITS - 1)
        def _():
            self.x_copy(at.z, u).start()

        self.send_z(at.z, u, True)
        self.send_z(at.z, u, False)
        self.c_copy(at.z, at.x, u).start()

    def start(self):
        at = self.at
        for u in range(UNITS - 1):
            self.x_copy(at.z, u).start()
            self.send_z(at.z, u, False)
        self.send_z(at.z, UNITS - 1, False)
        for u in range(UNITS):
            self.c_copy(at.z, at.x, u).start()

    def other_last(self, up):
        at = self.at
        self.x_copy(at.z, UNITS - 1, arriving=True).wait_recv()
        self.send_z(at.z, UNITS, False)
        if up:
            self.send_z(at.z, UNITS, True)
        self.c_copy(at.z, 1 - at.x, UNITS - 1).start()

    def onward(self, zo, v, up):
        xb, u = self.block_of(v)
        self.z_copy(zo, v, up).wait_recv()
        self.send_z(zo, v, up)

        @pl.when(v < UNITS - 1)
        def _():
            self.x_copy(zo, u).start()

        self.c_copy(zo, xb, u).start()

    def from_below(self, t):
        h, v = t // PER, lax.rem(t, PER)

        @pl.when(self.at.z > h)
        def _():
            self.onward(self.at.z - 1 - h, v, True)

    def from_above(self, t):
        h, v = t // PER, lax.rem(t, PER)

        @pl.when(self.at.z + h < self.at.last)
        def _():
            self.onward(self.at.z + 1 + h, v, False)

    def in_order(self, i):
        z = self.at.z
        zo, v = i // PER, lax.rem(i, PER)

        @pl.when(jnp.logical_and(i >= 0, zo < z))
        def _():
            self.onward(zo, v, True)

        @pl.when(jnp.logical_and(i >= 0, zo == z))
        def _():
            self.send_z(z, v, True)

    def x_arrival(self, zo, u):
        self.x_copy(zo, u, arriving=True).wait_recv()
        self.c_copy(zo, 1 - self.at.x, u).start()

    def beside_own(self):
        for u in range(UNITS - 1):
            self.x_arrival(self.at.z, u)

    def beside_far(self, t):
        at = self.at
        h, v = t // PER, lax.rem(t, PER)

        @pl.when(jnp.logical_and(t >= 0, v < UNITS - 1))
        def _():
            @pl.when(at.z > h)
            def _():
                self.x_arrival(at.z - 1 - h, v)

            @pl.when(at.z + h < at.last)
            def _():
                self.x_arrival(at.z + 1 + h, v)

    def beside_order(self, i):
        zo, v = i // PER, lax.rem(i, PER)

        @pl.when(jnp.logical_and(jnp.logical_and(i >= 0, v < UNITS - 1), zo < self.at.z))
        def _():
            self.x_arrival(zo, v)

    def beside_above(self, t):
        at = self.at
        h, v = t // PER, lax.rem(t, PER)

        @pl.when(jnp.logical_and(jnp.logical_and(t >= 0, v < UNITS - 1), at.z + h < at.last))
        def _():
            self.x_arrival(at.z + 1 + h, v)

    def arrived(self, zo):
        at = self.at
        spot = self.w.at[pl.ds(0, 2 * self.rows)]
        at.copy(spot, spot, self.o_s, self.c_r.at[zo], at.z, at.x, 1 - at.c).wait_recv()

    def sent(self):
        at = self.at
        z = at.z

        def wait(tiles, sem):
            spot = self.w.at[pl.ds(0, tiles)]
            at.copy(spot, spot, sem, self.c_r.at[0], z, at.x, 1 - at.c).wait_send()

        def each(zo, carry):
            @pl.when(jnp.logical_and(z < at.last, zo <= z))
            def _():
                wait(PER * self.n, self.up_s.at[zo])

            @pl.when(jnp.logical_and(z > 0, zo >= z))
            def _():
                wait(PER * self.n, self.dn_s.at[zo])

            wait((UNITS - 1) * self.n, self.x_s.at[zo])
            wait(2 * self.rows, self.c_s.at[zo])
            return carry

        lax.fori_loop(0, at.line, each, 0)
        wait(self.n, self.o_s)


def gather_sems(line):
    dma = pltpu.SemaphoreType.DMA
    return [dma((line,)), dma((line,)), dma((line * PER,)), dma((line,)), dma((line * UNITS,)), dma((line,)), dma((line,)), dma]


class Scatter:
    def __init__(self, at, g, rows, cr, xr, zr, keep, stage, wide_stage, behind, lead, hop, sems):
        self.at, self.g, self.rows, self.n = at, g, rows, rows // UNITS
        self.cr, self.xr, self.zr, self.keep, self.stage, self.wide = cr, xr, zr, keep, stage, wide_stage
        self.c_s, self.c_r, self.x_s, self.x_r, self.z_s, self.z_r, self.l_s, self.b_s = sems
        self.hop = hop
        self.lead = lead
        self.behind = behind
        self.items = at.last * PER
        self.final = self.items + lead + at.last * hop + behind
        self.slots = self.final + PER

    def lies(self, u):
        return (u + UNITS // 2) % UNITS * self.n if isinstance(u, int) else lax.rem(u + UNITS // 2, UNITS) * self.n

    def mine(self, zo, xb, u):
        return pl.ds(((zo * 2 + xb) * 2 + self.at.c) * self.rows + self.lies(u), self.n)

    def block_of(self, v):
        x = self.at.x
        return jnp.where(v == 0, 1 - x, x), jnp.where(v == 0, UNITS - 1, v - 1)

    def c_copy(self, zo, xb):
        at = self.at
        src = self.g.at[pl.ds(((zo * 2 + xb) * 2 + 1 - at.c) * self.rows, self.rows)]
        k = zo * 2 + xb
        return at.copy(src, self.cr.at[k], self.c_s.at[zo], self.c_r.at[k], at.z, at.x, 1 - at.c)

    def x_copy(self, zo, u, last=False):
        at = self.at
        k = zo * UNITS + u
        return at.copy(self.g.at[self.mine(zo, 1 - at.x, u)], self.xr.at[k], self.b_s if last else self.x_s.at[zo], self.x_r.at[k],
                       at.z, 1 - at.x, at.c)

    def z_copy(self, to, v, up):
        at = self.at
        xb, u = self.block_of(v)
        there = at.z + 1 if up else at.z - 1
        k = (to if up else jnp.where(to == there, at.line, to)) * PER + v
        return at.copy(self.g.at[self.mine(to, xb, u)], self.zr.at[k], self.z_s.at[to], self.z_r.at[k], there, at.x, at.c)

    def z_wait(self, k):
        at = self.at
        spot = self.zr.at[k]
        at.copy(spot, spot, self.z_s.at[0], self.z_r.at[k], at.z, 1 - at.x, at.c).wait_recv()

    def ready(self, zo):
        for xb in range(2):
            self.c_copy(zo, xb).start()

    def load(self, src, slot):
        return pltpu.make_async_copy(src, self.stage.at[slot, pl.ds(0, self.n)], self.l_s.at[slot])

    def core_part(self, zo, xb, u):
        return self.cr.at[zo * 2 + xb, pl.ds(self.lies(u), self.n)]

    def way(self, t, up):
        at = self.at
        i = t - (at.z * self.hop if up else (at.last - at.z) * self.hop + self.behind)
        to = (at.last if up else at.last - 1) - i // PER
        here = jnp.logical_and(jnp.logical_and(i >= 0, i < self.items), to > at.z if up else to < at.z)
        return to, lax.rem(i, PER), here

    def crossings(self, t):
        at = self.at
        found = []
        for up, slot in ((True, 0), (False, 11)):
            to, v, here = self.way(t, up)
            found.append((to, v - 1, jnp.logical_and(here, jnp.logical_and(v >= 1, v < UNITS)), slot))
        u = t - self.items - 1
        found.append((at.z, u, jnp.logical_and(u >= 0, u < UNITS - 1), 12))
        return found

    def parts(self, t, finals):
        found = [self.way(t - self.lead, up) + (up, slot) for up, slot in ((True, 1), (False, 4))]
        own = t - self.final
        return found + [(self.at.z, own, jnp.logical_and(own >= 0, own < PER), None, 7)] * finals

    def prepare(self, t, finals=False):
        at = self.at
        for to, u, here, slot in self.crossings(t):
            @pl.when(here)
            def _(to=to, u=u, slot=slot):
                @pl.when(u == 0)
                def _():
                    for xb in range(2):
                        self.c_copy(to, xb).wait_recv()

                self.load(self.core_part(to, 1 - at.x, u), slot).start()

        for to, v, here, up, slot in self.parts(t, finals):
            @pl.when(here)
            def _(to=to, v=v, up=up, slot=slot):
                xb, u = self.block_of(v)
                self.load(self.core_part(to, xb, u), slot).start()

                @pl.when(jnp.logical_and(v >= 1, v < (UNITS if up is not None else PER)))
                def _():
                    self.x_copy(to, u).wait_recv()
                    self.load(self.xr.at[to * UNITS + u], slot + 1).start()

                if up is None:
                    @pl.when(at.z > 0)
                    def _():
                        self.z_wait(to * PER + v)
                        self.load(self.zr.at[to * PER + v], slot + 2).start()

                    @pl.when(at.z < at.last)
                    def _():
                        self.z_wait(at.line * PER + v)
                        self.load(self.zr.at[at.line * PER + v], slot + 3).start()
                else:
                    @pl.when(at.z != (0 if up else at.last))
                    def _():
                        self.z_wait(to * PER + v)
                        self.load(self.zr.at[to * PER + v], slot + 2).start()

    def take(self, slot):
        self.load(self.xr.at[0], slot).wait()
        return self.stage[slot].astype(F32)

    def act(self, t, finals):
        at = self.at
        for to, v, here, up, slot in self.parts(t, finals):
            @pl.when(here)
            def _(to=to, v=v, up=up, slot=slot):
                xb, u = self.block_of(v)
                spot = self.mine(to, xb, u)
                acc = self.wide

                acc[: self.n] = self.g[spot].astype(F32) + self.take(slot)

                def more(k):
                    acc[: self.n] = acc[: self.n] + self.take(slot + k)

                @pl.when(jnp.logical_and(v >= 1, v < (UNITS if up is not None else PER)))
                def _():
                    more(1)

                if up is None:
                    @pl.when(at.z > 0)
                    def _():
                        more(2)

                    @pl.when(at.z < at.last)
                    def _():
                        more(3)

                    @pl.when(v == 0)
                    def _():
                        self.g[spot] = acc[: self.n].astype(BF16)
                        self.x_copy(to, UNITS - 1, True).start()

                    @pl.when(v >= 1)
                    def _():
                        self.keep(self.lies(u))
                else:
                    @pl.when(at.z != (0 if up else at.last))
                    def _():
                        more(2)

                    self.g[spot] = acc[: self.n].astype(BF16)
                    self.z_copy(to, v, up).start()

        for to, u, here, slot in self.crossings(t):
            @pl.when(here)
            def _(to=to, u=u, slot=slot):
                spot = self.mine(to, 1 - at.x, u)
                self.g[spot] = (self.g[spot].astype(F32) + self.take(slot)).astype(BF16)
                self.x_copy(to, u).start()

    def slot(self, t, finals=False):
        self.act(t, finals)
        self.prepare(t + 1, finals)

    def sent(self):
        at = self.at
        z = at.z

        def wait(tiles, sem):
            spot = self.g.at[pl.ds(0, tiles)]
            at.copy(spot, spot, sem, self.c_r.at[0], z, at.x, 1 - at.c).wait_send()

        def each(zo, carry):
            @pl.when(zo != z)
            def _():
                wait(PER * self.n, self.z_s.at[zo])

            wait((UNITS - 1) * self.n, self.x_s.at[zo])
            wait(2 * self.rows, self.c_s.at[zo])
            return carry

        lax.fori_loop(0, at.line, each, 0)
        wait(self.n, self.b_s)


def scatter_sems(line):
    dma = pltpu.SemaphoreType.DMA
    return [dma((line,)), dma((line * 2,)), dma((line,)), dma((line * UNITS,)), dma((line,)), dma(((line + 1) * PER,)), dma((13,)), dma]


def landing(line, rows):
    n = rows // UNITS
    shape = lambda *s: jax.ShapeDtypeStruct(s + (16, 128), BF16)
    return [shape(line * 2, rows), shape(line * UNITS, n), shape((line + 1) * PER, n)]


class Edges:
    def __init__(self, at, plan, window, first, spare, land, sems):
        self.at, self.plan, self.window, self.first, self.spare, self.land = at, plan, window, first, spare, land
        self.f_s, self.f_r, self.l_s, self.e_s, self.e_r = sems
        self.d = (at.z * 2 + at.x) * 2 + at.c
        self.end = plan.before + plan.shard

    def over(self, src, dst, send, recv, by):
        return pltpu.make_async_remote_copy(
            src_ref=src, dst_ref=dst, send_sem=send, recv_sem=recv, device_id=(self.at.s, self.d + by), device_id_type=MESH_ID)

    def both(self, up, down):
        @pl.when(self.d < 4 * self.at.line - 1)
        def _():
            up()

        @pl.when(self.d > 0)
        def _():
            down()

    def lands(self, ref):
        plan = self.plan
        return ref.at[pl.ds(0, plan.before)], ref.at[pl.ds(plan.before, plan.after)]

    def outer(self, own):
        plan = self.plan
        before, after = self.lands(self.first)
        return (self.over(own.at[pl.ds(plan.shard - plan.before, plan.before), 0], before, self.f_s.at[0], self.f_r.at[0], 1),
                self.over(own.at[pl.ds(0, plan.after), 0], after, self.f_s.at[1], self.f_r.at[1], -1))

    def send(self, own):
        up, down = self.outer(own)
        self.both(up.start, down.start)

    def inner(self, own):
        return pltpu.make_async_copy(own.at[:, 0], self.window.at[pl.ds(self.plan.before, self.plan.shard)], self.l_s)

    def clear_tiles(self, w):
        w[pl.ds(self.plan.rows * self.d, self.plan.rows)] = jnp.zeros((self.plan.rows, 16, 128), w.dtype)

    def enter(self, own):
        plan = self.plan
        up, down = self.outer(own)

        def above():
            down.wait_recv()
            self.window[self.end : self.end + plan.after, :] = self.first[plan.before : plan.before + plan.after, :]

        def below():
            up.wait_recv()
            self.window[: plan.before, :] = self.first[: plan.before, :]

        self.both(above, below)

    def tiles(self, kinds, w, first, count):
        lo = self.plan.rows * self.d + first

        def act(tile, row, stride, rows):
            value = self.window[pl.ds(row, rows, stride=stride), :]
            if rows < 16:
                value = jnp.concatenate([value, jnp.zeros((16 - rows, 128), value.dtype)], axis=0)
            w[tile] = value.astype(w.dtype)

        self.by_stream(kinds, lo, lo + count, act)

    def entered(self, own):
        up, down = self.outer(own)
        self.both(up.wait_send, down.wait_send)

    def by_stream(self, kinds, lo, hi, act):
        start = self.plan.shard * self.d - self.plan.before
        for s, b in enumerate(kinds):
            @pl.when(self.at.s == s)
            def _(b=b):
                each_tile(b, lo, hi, start, act)

    def clear(self):
        self.window[...] = jnp.zeros(self.window.shape, F32)

    def take(self, kinds, acc, n):
        def keep(first):
            lo = self.plan.rows * self.d + first

            def act(tile, row, stride, rows):
                self.window[pl.ds(row, rows, stride=stride), :] = acc[tile - lo][:rows]

            self.by_stream(kinds, lo, lo + n, act)

        return keep

    def back(self):
        plan = self.plan
        front, rear = self.lands(self.land)
        return (self.over(self.spare.at[pl.ds(0, plan.after)], rear, self.e_s.at[0], self.e_r.at[0], 1),
                self.over(self.window.at[pl.ds(0, plan.before)], front, self.e_s.at[1], self.e_r.at[1], -1))

    def give(self):
        self.spare[: self.plan.after, :] = self.window[self.end : self.end + self.plan.after, :]
        up, down = self.back()
        self.both(up.start, down.start)

    def finish(self, out):
        plan = self.plan
        up, down = self.back()

        def above():
            down.wait_recv()
            spot = slice(self.end - plan.before, self.end)
            self.window[spot, :] = self.window[spot, :] + self.land[: plan.before, :]

        def below():
            up.wait_recv()
            spot = slice(plan.before, plan.before + plan.after)
            self.window[spot, :] = self.window[spot, :] + self.land[plan.before : plan.before + plan.after, :]

        self.both(above, below)
        self.leave(out).start()

    def leave(self, out):
        return pltpu.make_async_copy(self.window.at[pl.ds(self.plan.before, self.plan.shard)], out.at[:, 0], self.l_s)

    def done(self, out):
        self.leave(out).wait()
        up, down = self.back()
        self.both(up.wait_send, down.wait_send)


def edge_sems():
    dma = pltpu.SemaphoreType.DMA
    return [dma((2,)), dma((2,)), dma, dma((2,)), dma((2,))]


def to_flat(flat, box):
    count = box.shape[1] // 128
    for b in range(count):
        flat[pl.ds(b, box.shape[0], stride=count), :] = box[:, b * 128 : (b + 1) * 128].astype(F32)


def from_flat(flat, rows, count, put):
    for j in range(count):
        put(j, flat[pl.ds(j, rows, stride=count), :])


def layer_kernel(plans, line, texts, regions, xbox, gbox, co_flat, sa_flat, *refs):
    kinds = list(zip(plans[0].blocks, plans[1].blocks))
    outs, refs = refs[:10], refs[10:]
    out_box, grad_box, co_out, sa_out = outs[:4]
    wc, ws, vec, vec2, small, pool, land, xp, xin, ret, stage_c, stage_s, acc = refs[:13]
    refs = refs[13:]
    names = sorted(KEPT)
    sc = dict(zip(names, refs[: len(names)]))
    refs = refs[len(names) :]
    ss = dict(zip(names, refs[: len(names)]))
    refs = refs[len(names) :]
    shared = dict(zip(sorted(SHARED), refs[: len(SHARED)]))
    refs = refs[len(SHARED) :]
    ag_c, ag_s, rs_c, rs_s, ed_c, ed_s, y_s, y_r = refs[:8], refs[8:16], refs[16:24], refs[24:32], refs[32:37], refs[37:42], refs[42], refs[43]
    sent = shared["dc"]
    span = pool_span(plans)
    flat = pool.at[pl.ds(6 * span, span)]

    at = Where(line)
    last = at.last
    gc, gs = Gather(at, plans[0].rows, wc, ag_c), Gather(at, plans[1].rows, ws, ag_s)
    edges = []
    rest = max(p.window for p in plans)
    for k, (p, sems) in enumerate(zip(plans, (ed_c, ed_s))):
        sizes = [q.before + q.after for q in plans]
        edges.append(Edges(at, p, pool.at[pl.ds(0, p.window)], pool.at[pl.ds(rest + k * sizes[0], sizes[k])], pool.at[pl.ds(rest, p.after)],
                           land.at[pl.ds(k * sizes[0], sizes[k])], sems))
    ec, es = edges
    own_kinds = [[k[i] for k in kinds] for i in range(2)]
    rc = Scatter(at, wc, plans[0].rows, *outs[4:7], ec.take(own_kinds[0], acc, gc.n), stage_c, acc, 0, 5, 1, rs_c)
    rs = Scatter(at, ws, plans[1].rows, *outs[7:10], es.take(own_kinds[1], acc, gs.n), stage_s, acc, BEHIND, 3, HOP, rs_s)

    def over(k, src, dst):
        return at.copy(src, dst, y_s.at[k], y_r.at[k], at.z, at.x, at.c, 1 - at.s)

    ec.inner(co_flat).start()
    at.greet()
    ec.send(co_flat)
    es.send(sa_flat)
    ec.clear_tiles(wc)
    ec.inner(co_flat).wait()

    def begin(k, carry):
        @pl.when(k == 2)
        def _():
            ec.enter(co_flat)

        u = lax.rem(k + UNITS - 1, UNITS)
        ec.tiles(own_kinds[0], wc, gc.lies(u), gc.n)
        gc.start_unit(u)
        return carry

    lax.fori_loop(0, UNITS, begin, 0)
    es.inner(sa_flat).start()
    states = over(0, xbox, xp)
    states.start()
    ec.entered(co_flat)
    es.clear_tiles(ws)
    es.inner(sa_flat).wait()
    es.enter(sa_flat)
    es.tiles(own_kinds[1], ws, 0, plans[1].rows)
    es.entered(sa_flat)
    gs.first()
    gc.other_last(True)

    steps = PER * last
    early = PER

    def co_step(t, carry):
        gc.from_below(t)
        gc.from_above(t)

        @pl.when(t < UNITS - 1)
        def _():
            gc.x_arrival(at.z, t)

        gc.beside_far(t - PER)

        @pl.when(jnp.logical_and(t >= steps - early, at.z < last))
        def _():
            gs.in_order(t - (steps - early) - at.z)

        return carry

    lax.fori_loop(0, steps - early, co_step, 0)
    gs.start()
    gs.other_last(False)
    lax.fori_loop(steps - early, steps, co_step, 0)

    def co_rest(t, carry):
        gc.beside_far(t)
        return carry

    lax.fori_loop(steps - PER, steps, co_rest, 0)
    gs.beside_own()
    for zo in range(line):
        gc.arrived(zo)
    states.wait_recv()

    ahead = jnp.where(at.z < last, early - at.z, 0)

    def self_beside(t):
        gs.beside_order(t + ahead)
        gs.beside_above(t)

    def self_steps(a, b, lag):
        def step(t, carry):
            gs.in_order(t + ahead)
            gs.from_above(t)
            self_beside(t - lag)
            return carry

        lax.fori_loop(a, b, step, 0)

    def self_rest(a, b):
        lax.fori_loop(a, b, lambda t, carry: (self_beside(t), carry)[1], 0)

    gather_steps = steps
    scatter_ticks = sum(SLOTS_TEXT) + sum(SLOTS_CO)

    def run(text, co, sa):
        rows, width = co.rows, co.width

        def view(refs, b):
            d = {name: View(ref, kept_shapes(b)[name]) for name, ref in refs.items()}
            for name, ref in shared.items():
                d[name] = View(ref, shared_shapes(b)[name])
            for k, name in enumerate(("r1", "r2")):
                d[name] = Pooled(pool, (2 * (b is sa) + k) * span, b.rows, b.width)
            d["h"], d["dy"] = [Pooled(pool, k * span, b.rows, b.width) for k in (4, 5)]
            d["small"] = small
            return d

        a = Net(co, wc, vec, view(sc, co))
        b = Net(sa, ws, vec2, view(ss, sa))
        h, hb, dy = b.s["h"], b.s["hb"], b.s["dy"]

        own_in = View(xin, (rows, width))
        if text:
            to_flat(flat, xbox)

            def put(j, value):
                own_in[:, cols(j, 128)] = value.astype(BF16)

            from_flat(flat, rows, width // 128, put)
            x, z = own_in, View(xp, xp.shape)
        else:
            to_flat(flat, xp)
            other = View(xin, (co.other_rows, co.other))

            def put(j, value):
                other[:, cols(j, 128)] = value.astype(BF16)

            from_flat(flat, co.other_rows, co.other // 128, put)
            x, z = View(xbox, xbox.shape), other

        steps_done, beside_done, places = [0], [-PER], [0]

        def tick(k=1):
            a0 = steps_done[0]
            b0 = min(a0 + k, gather_steps)
            if b0 > a0:
                self_steps(a0, b0, a0 - beside_done[0])
                beside_done[0] += b0 - a0
                steps_done[0] = b0

        def need(name):
            later = [sa.place[n][0] for n in ("i_w", "f_w") if sa.place[n][0] > sa.place[name][0]]
            top = -(-min(later + [sa.tiles]) // (4 * gs.rows))
            wanted = min(PER * top, gather_steps)
            tick(min(wanted + 3, gather_steps) - steps_done[0])
            if beside_done[0] < wanted:
                self_rest(beside_done[0], wanted)
                beside_done[0] = wanted
            for zo in range(places[0], top):
                gs.arrived(zo)
            places[0] = max(places[0], top)

        own_counts, other_counts = (texts, regions) if text else (regions, texts)
        value = a.forward(x, x, z, lambda q: other_counts[q], tick)
        h[...] = value
        hb[...] = value.astype(BF16)
        gc.sent()
        if text:
            to_flat(flat, gbox)

            def put(j, value):
                dy[:, cols(j, 128)] = value

            from_flat(flat, rows, width // 128, put)
        else:
            dy[...] = gbox[...].astype(F32)
        value = b.forward(h, hb, hb, lambda q: own_counts[q], tick, need)
        if text:
            for j in range(width // 128):
                flat[pl.ds(j, rows, stride=width // 128), :] = value[:, j * 128 : (j + 1) * 128]
        else:
            out_box[...] = value.astype(BF16)
        gs.sent()

        def put_h(c, value):
            h[:, c] = value

        def add_h(c, value):
            h[:, c] = h[:, c] + value

        ticks = [0]

        def hooks(scatter, block):
            state = [line]

            def done(name):
                tile = block.place[name][0]
                ready = -(-tile // (4 * scatter.rows))
                while state[0] > ready:
                    state[0] -= 1
                    scatter.ready(state[0])
                    if scatter is rs and state[0] == last:
                        rs.prepare(0)

            return done

        def slots(k):
            a0 = ticks[0]
            ticks[0] = a0 + k
            if k:
                lax.fori_loop(a0, a0 + k, lambda t, carry: (rs.slot(t), carry)[1], 0)

        def rs_tick(counts):
            left = list(counts)
            return lambda k=1: slots(left.pop(0))

        b.backward(dy, hb, hb, put_h, add_h, hooks(rs, sa), rs_tick(SLOTS_TEXT if text else SLOTS_IMAGE))
        if text:
            def put(j, value):
                out_box[:, j * 128 : (j + 1) * 128] = value.astype(BF16)

            from_flat(flat, out_box.shape[0], out_box.shape[1] // 128, put)

        def put_own(c, value):
            dy[:, c] = value

        sent_rows = View(sent, (co.other_rows, co.other))

        def put_sent(c, value):
            sent_rows[:, c] = value.astype(BF16)

        a.backward(h, x, z, put_own, put_sent, hooks(rc, co), rs_tick(SLOTS_CO))
        over(1, sent, ret).start()
        assert ticks[0] == scatter_ticks

    for s, (co, sa) in enumerate(kinds):
        @pl.when(at.s == s)
        def _(s=s, co=co, sa=sa):
            run(s == 0, co, sa)

    back = over(1, sent, ret)

    def grads_of_states():
        back.wait_recv()
        for s, (co, sa) in enumerate(kinds):
            @pl.when(at.s == s)
            def _(s=s, co=co):
                mine = Pooled(pool, 5 * span, co.rows, co.width)
                got = View(ret, (co.rows, co.width))
                if s == 0:
                    count = co.width // 128
                    for j in range(count):
                        flat[pl.ds(j, co.rows, stride=count), :] = mine[:, cols(j, 128)] + got[:, cols(j, 128)].astype(F32)

                    def put(j, value):
                        grad_box[:, j * 128 : (j + 1) * 128] = value

                    from_flat(flat, grad_box.shape[0], grad_box.shape[1] // 128, put)
                else:
                    grad_box[...] = mine[...] + got[...].astype(F32)

    rc.prepare(0)
    es.clear()
    shift = rs.items
    steps = shift + rc.slots

    def both(t, carry):
        @pl.when(t < rs.slots)
        def _():
            rs.slot(t, True)

        @pl.when(t == rs.slots)
        def _():
            es.give()

        @pl.when(t == rs.slots + 2)
        def _():
            es.finish(sa_out)

        @pl.when(t == rs.slots + 4)
        def _():
            es.done(sa_out)
            ec.clear()
            rs.sent()

        @pl.when(t == shift + rc.final - 1)
        def _():
            grads_of_states()

        @pl.when(t >= shift)
        def _():
            rc.slot(t - shift, True)

        @pl.when(t == shift + rc.final + 4)
        def _():
            ec.give()

        return carry

    assert rs.slots + 4 < shift + rc.final
    lax.fori_loop(scatter_ticks, steps, both, 0)
    ec.finish(co_out)
    back.wait_send()
    states.wait_send()
    rc.sent()
    ec.done(co_out)


KEPT = ("q", "k", "v", "p", "c", "y1", "a", "gp")
SHARED = ("fill", "m", "hb", "dc")


def kept_shapes(b):
    return {k: v[0] for k, v in scratch_of(b).items()}


def shared_shapes(b):
    rows, width = b.rows, b.width
    return {"fill": (b.rows, b.other_rows), "m": (rows, width), "hb": (rows, width), "dc": (rows, b.inner)}


SHARED_TYPES = {"fill": F32}


def most(shapes):
    return tuple(max(k) for k in zip(*shapes))


def pool_span(plans):
    return max(b.rows * b.width // 128 for p in plans for b in p.blocks)


def layer_call(plans, line, texts, regions, xbox, gbox, co_flat, sa_flat, cid):
    vm = pl.BlockSpec(memory_space=pltpu.VMEM)
    any_ = pl.BlockSpec(memory_space=pl.ANY)
    rows_c, rows_s = [p.rows for p in plans]
    V = pltpu.VMEM
    cos, sas = [p.blocks for p in plans]
    wide = most([(b.rows, b.width) for b in cos] + [(b.other_rows, b.other) for b in cos])
    n = max(rows_c, rows_s) // UNITS
    edge = sum(p.before + p.after for p in plans)
    assert max(p.window for p in plans) + edge <= 5 * pool_span(plans)
    scr = [V((plans[0].tiles, 16, 128), BF16), V((plans[1].tiles, 16, 128), BF16), V((16, 3072), F32), V((16, 3072), F32), V((32, 128), F32),
           V((7 * pool_span(plans), 128), F32), V((edge, 128), F32), V(xbox.shape, BF16), V(wide, BF16), V(wide, BF16),
           V((13, rows_c // UNITS, 16, 128), BF16), V((13, rows_s // UNITS, 16, 128), BF16), V((n, 16, 128), F32)]
    for bs in (cos, sas):
        for name in sorted(KEPT):
            scr.append(V(most([kept_shapes(b)[name] for b in bs]), scratch_of(bs[0])[name][1]))
    for name in sorted(SHARED):
        shape = most([shared_shapes(b)[name] for b in cos + sas] + ([wide] if name == "dc" else []))
        scr.append(V(shape, SHARED_TYPES.get(name, BF16)))
    dma = pltpu.SemaphoreType.DMA
    scr += gather_sems(line) + gather_sems(line) + scatter_sems(line) + scatter_sems(line) + edge_sems() + edge_sems() + [dma((2,)), dma((2,))]
    struct = jax.ShapeDtypeStruct
    outs = [struct(xbox.shape, BF16), struct(xbox.shape, F32), struct(co_flat.shape, F32), struct(sa_flat.shape, F32)]
    outs += landing(line, rows_c) + landing(line, rows_s)
    return pl.pallas_call(
        functools.partial(layer_kernel, plans, line),
        out_shape=outs,
        in_specs=[pl.BlockSpec(memory_space=pltpu.SMEM)] * 2 + [vm, vm, any_, any_],
        out_specs=[vm, vm] + [any_] * 8,
        scratch_shapes=scr,
        compiler_params=pltpu.CompilerParams(collective_id=cid, has_side_effects=True, vmem_limit_bytes=64 * 2**20 - 2**16),
        name="layer",
    )(texts, regions, xbox, gbox, co_flat, sa_flat)[:4]


DT, HT, FT = 768, 12, 3072
DI, HI, FI = 1024, 8, 1024
DC, HC = 1024, 8
LT, LI = 128, 96
LINE_MAX = 8


def blocks_of(text, seqs):
    if text:
        return (Block(DT, DI, DC, FT, HC, LT, LI, seqs), Block(DT, DT, DT, FT, HT, LT, LT, seqs))
    return (Block(DI, DT, DC, FI, HC, LI, LT, seqs), Block(DI, DI, DI, FI, HI, LI, LI, seqs))


class Plan:
    def __init__(self, blocks, devices, flat_total):
        self.blocks = blocks
        self.shard = flat_total // 128 // devices
        tiles = max(b.tiles for b in blocks)
        self.rows = -(-tiles // (devices * UNITS)) * UNITS
        self.tiles = self.rows * devices
        tables = [self.table(b).reshape(self.tiles, 16) for b in blocks]
        before = after = 0
        inner = True
        for table in tables:
            most = table.max(axis=1)
            least = np.where(table >= 0, table, flat_total).min(axis=1)
            for d in range(devices):
                lo, hi, start, end = self.rows * d, self.rows * (d + 1), self.shard * d, self.shard * (d + 1)
                held = np.nonzero(most[lo:hi] >= 0)[0] + lo
                if held.size:
                    before = max(before, start - least[held].min())
                    after = max(after, most[held].max() + 1 - end)
                    unit = (held - lo) * UNITS // self.rows
                    outer = (least[held] < start) & (unit > 0) | (most[held] >= end) & (unit < UNITS // 2)
                    inner = inner and not outer.any()
        self.before, self.after = [max(-(-int(k) // 16) * 16, 16) for k in (before, after)]
        self.window = -(-(self.before + self.shard + self.after) // 8) * 8
        self.near = max(self.before, self.after) <= self.shard and inner

    def table(self, b):
        index = np.full((self.tiles * 16,), -1, np.int32)
        for first, flat, k, rows, nb in b.parts:
            if k:
                r, j = np.arange(k)[:, None], np.arange(nb)[None]
                at = first * 16 + ((r // 16) * nb + j) * 16 + r % 16
                index[at.reshape(-1)] = (flat + r * nb + j).reshape(-1)
            else:
                index[first * 16 : first * 16 + rows] = flat + np.arange(rows)
        return index


def each_tile(b, lo, hi, start, act):
    for first, flat, k, rows, nb in b.parts:
        if k:
            count = rows // 16
            a = jnp.clip(lo - first, 0, count)
            z = jnp.clip(hi - first, 0, count)

            def body(t, carry, first=first, flat=flat, nb=nb):
                i = t // nb
                act(first + t, flat + i * 16 * nb + (t - i * nb) - start, nb, 16)
                return carry

            lax.fori_loop(a, z, body, 0)
        else:
            for t in range((rows + 15) // 16):
                @pl.when(jnp.logical_and(first + t >= lo, first + t < hi))
                def _(t=t, first=first, flat=flat, rows=rows):
                    act(first + t, flat + 16 * t - start, 1, min(16, rows - 16 * t))


def gathered(plan, text, flat):
    whole = lax.all_gather(flat.astype(BF16), "dp", axis=0, tiled=True).reshape(-1, 128)
    index = jnp.where(text, *[jnp.asarray(plan.table(b)) for b in plan.blocks])
    rows = jnp.where((index >= 0)[:, None], whole[jnp.maximum(index, 0)], jnp.zeros((), BF16))
    return rows.reshape(plan.tiles, 16, 128)


def scattered(plan, text, tiles, flat_rows):
    tables = []
    for b in plan.blocks:
        table = plan.table(b)
        back = np.full((flat_rows,), -1, np.int32)
        held = np.nonzero(table >= 0)[0]
        back[table[held]] = held
        tables.append(jnp.asarray(back))
    index = jnp.where(text, *tables)
    rows = jnp.where((index >= 0)[:, None], tiles.reshape(-1, 128)[jnp.maximum(index, 0)], jnp.zeros((), BF16))
    return lax.psum_scatter(rows.astype(F32), "dp", scatter_dimension=0, tiled=True).reshape(-1)


def layer_alone(text, counts, own, partner, grad, wco, wsa):
    seqs = own.shape[0]
    co, sa = blocks_of(text, seqs)
    box = own.shape
    lens = counts if text else counts[::-1]
    out, own_grad, sent, gco, gsa = compute(
        co, sa, lens, own.reshape(co.rows, co.width), partner.reshape(co.other_rows, co.other),
        grad.reshape(co.rows, co.width), wco, wsa)
    return out.reshape(box), own_grad.reshape(box), sent.reshape(box), gco, gsa


def body(devices, states, out_grad, co_params, self_params, text_lengths, region_counts):
    own = states[0]
    seqs = own.shape[0]
    text = lax.axis_index("stream") == 0
    flats = (co_params[0], self_params[0])
    streams = [blocks_of(t, seqs) for t in (True, False)]
    plans = [Plan([k[i] for k in streams], devices, f.shape[0] * devices) for i, f in enumerate(flats)]
    line = devices // 4
    if devices % 4 == 0 and line <= LINE_MAX and all(p.near for p in plans):
        box = (own.shape[0] * own.shape[1], own.shape[2])
        flats = [f.reshape(p.shard, 1, 128) for p, f in zip(plans, flats)]
        out, grad, co_grad, sa_grad = layer_call(plans, line, text_lengths, region_counts, own.reshape(box), out_grad[0].reshape(box), *flats, 1)
        return (out.reshape(states.shape), grad.reshape(states.shape), co_grad.reshape(co_params.shape), sa_grad.reshape(self_params.shape))
    swap = [(0, 1), (1, 0)]
    partner = lax.ppermute(own, "stream", swap)
    wco, wsa = [gathered(p, text, f) for p, f in zip(plans, flats)]
    counts = jnp.stack([text_lengths, region_counts])
    out, own_grad, sent, gco, gsa = lax.cond(
        text, functools.partial(layer_alone, True), functools.partial(layer_alone, False),
        counts, own, partner, out_grad[0], wco, wsa)
    returned = lax.ppermute(sent, "stream", swap)
    flats = [scattered(p, text, g, p.shard * devices) for p, g in zip(plans, (gco, gsa))]
    return (out[None], (own_grad + returned.astype(F32))[None], flats[0][None], flats[1][None])


def solution(mesh):
    states = P("stream", "dp", None, None)
    flat = P("stream", "dp")
    return jax.shard_map(
        functools.partial(body, mesh.shape["dp"]), mesh=mesh, in_specs=(states, states, flat, flat, P("dp"), P("dp")),
        out_specs=(states, states, flat, flat), check_vma=False)
```

```python
import functools
import math

import jax
import jax.numpy as jnp
import numpy as np
from jax import lax
from jax.experimental import pallas as pl
from jax.experimental.pallas import tpu as pltpu
from jax.sharding import PartitionSpec as P


MESH_ID = pl.DeviceIdType.MESH
UNITS = 6


def place(line):
    d = lax.axis_index("dp")
    return d // 4, lax.rem(d // 2, 2), lax.rem(d, 2)


F32, BF16 = jnp.float32, jnp.bfloat16
NT = (((1,), (1,)), ((), ()))
TN = (((0,), (0,)), ((), ()))
norm_eps = 1e-12
masked_score = -1000000000.0
other_sequence = -3.0e38


def dot(a, b, dims=(((1,), (0,)), ((), ()))):
    return lax.dot_general(a, b, dims, preferred_element_type=F32)


class Block:
    def __init__(self, width, other, inner, hidden, heads, length, other_length, seqs, base=0):
        self.width, self.other, self.inner, self.hidden, self.heads = width, other, inner, hidden, heads
        self.length, self.other_length, self.seqs = length, other_length, seqs
        self.rows, self.other_rows = length * seqs, other_length * seqs
        self.base = base
        self.place = {}
        self.parts = []
        tile, flat = 0, 0

        def matrix(name, k, n):
            nonlocal tile, flat
            self.place[name] = (tile, k, n)
            self.parts.append((tile, flat, k, k * n // 128, n // 128))
            tile, flat = tile + k * n // 2048, flat + k * n // 128

        def vectors(*names):
            nonlocal tile, flat
            rows = 0
            for name, size in names:
                self.place[name] = (tile, rows, size)
                rows += size // 128
            self.parts.append((tile, flat, 0, rows, 0))
            tile, flat = tile + (rows + 15) // 16, flat + rows

        matrix("q_w", width, inner)
        vectors(("q_b", inner))
        matrix("k_w", other, inner)
        matrix("v_w", other, inner)
        vectors(("v_b", inner))
        matrix("o_w", inner, width)
        vectors(("o_b", width), ("g1", width), ("b1", width))
        matrix("i_w", width, hidden)
        vectors(("i_b", hidden))
        matrix("f_w", hidden, width)
        vectors(("f_b", width), ("g2", width), ("b2", width))
        self.tiles, self.flat_rows = tile, flat


VECS = ("q_b", "v_b", "o_b", "g1", "b1", "i_b", "f_b", "g2", "b2")
GROUPS = (("q_b",), ("v_b",), ("o_b", "g1", "b1"), ("i_b",), ("f_b", "g2", "b2"))


class Cols:
    def __init__(self, j, size):
        self.j, self.size = j, size

    def ds(self):
        return pl.ds(pl.multiple_of(self.j * self.size, self.size), self.size)


def cols(j, size=256):
    return Cols(j, size)


class Pooled:
    def __init__(self, pool, base, rows, width):
        self.pool, self.base, self.rows, self.count = pool, base, rows, width // 128

    def spots(self, index):
        if index is Ellipsis:
            first, count = 0, self.count
        else:
            run = index[1]
            count = run.size // 128
            first = run.j * count
        return [pl.ds(pl.multiple_of(self.base + (first + i) * self.rows, 8), self.rows) for i in range(count)]

    def __getitem__(self, index):
        return jnp.concatenate([self.pool[spot, :] for spot in self.spots(index)], axis=1)

    def __setitem__(self, index, value):
        for i, spot in enumerate(self.spots(index)):
            self.pool[spot, :] = value[:, i * 128 : (i + 1) * 128]


class View:
    def __init__(self, ref, shape):
        self.ref, self.shape = ref, tuple(shape)

    def whole(self, index):
        index = () if index is Ellipsis else index if isinstance(index, tuple) else (index,)
        index = index + (slice(None),) * (len(self.shape) - len(index))
        index = [i.ds() if isinstance(i, Cols) else i for i in index]
        return tuple(slice(0, k) if isinstance(i, slice) and i == slice(None) else i for i, k in zip(index, self.shape))

    def __getitem__(self, index):
        return self.ref[self.whole(index)]

    def __setitem__(self, index, value):
        self.ref[self.whole(index)] = value


NN_STEP, NT_STEP, TN_STEP, TN_WIDE = 1024, 1024, 1024, 768


def step_of(n, most):
    return max(k for k in range(256, most + 1, 256) if n % k == 0)


class Net:
    def __init__(self, b, w, vec, sc):
        self.b, self.w, self.vec, self.s = b, w, vec, sc

    def mat(self, name):
        tile, k, n = self.b.place[name]
        return self.w.at[pl.ds(self.b.base + tile, k * n // 2048)].reshape(k // 16, n // 128, 16, 128)

    def row(self, name, c=None):
        k = VECS.index(name)
        size = self.b.place[name][2]
        return self.vec[k : k + 1, :size] if c is None else self.vec[k : k + 1, c.ds()]

    def load_vectors(self, groups):
        for group in groups:
            tile = self.b.place[group[0]][0]
            rows = sum(self.b.place[g][2] for g in group) // 128
            count = (rows + 15) // 16
            value = self.w[pl.ds(self.b.base + tile, count)].reshape(count * 16, 128).astype(F32)
            r = 0
            for name in group:
                k = VECS.index(name)
                for j in range(self.b.place[name][2] // 128):
                    self.vec[k : k + 1, j * 128 : (j + 1) * 128] = value[r : r + 1]
                    r += 1

    def store_vectors(self, group, scratch):
        tile = self.b.place[group[0]][0]
        rows = sum(self.b.place[g][2] for g in group) // 128
        count = (rows + 15) // 16
        scratch[0 : count * 16] = jnp.zeros((count * 16, 128), F32)
        r = 0
        for name in group:
            k = VECS.index(name)
            for j in range(self.b.place[name][2] // 128):
                scratch[r : r + 1, :] = self.vec[k : k + 1, j * 128 : (j + 1) * 128]
                r += 1
        self.w[pl.ds(self.b.base + tile, count)] = scratch[0 : count * 16].astype(BF16).reshape(count, 16, 128)

    def nn(self, x, name, put):
        m = self.mat(name)
        k, n = self.b.place[name][1:]
        step = step_of(n, NN_STEP)

        def body(j, carry):
            per = step // 128
            w = jnp.concatenate([m[:, per * j + i].reshape(k, 128) for i in range(per)], axis=1)
            put(cols(j, step), dot(x[...], w))
            return carry

        lax.fori_loop(0, n // step, body, 0)

    def rows_of(self, name, j, step):
        m = self.mat(name)
        strips = step // 16
        return jnp.concatenate([m[pl.ds(j * strips, strips), i].reshape(step, 128) for i in range(m.shape[1])], axis=1)

    def nt(self, g, name, put):
        k, n = self.b.place[name][1:]
        step = step_of(k, NT_STEP)

        def body(j, carry):
            put(cols(j, step), dot(g[...], self.rows_of(name, j, step), NT))
            return carry

        lax.fori_loop(0, k // step, body, 0)

    def tn(self, a, g, name):
        m = self.mat(name)
        k, n = self.b.place[name][1:]
        step, wide = step_of(k, TN_STEP), step_of(n, TN_WIDE)
        strips = step // 16

        def body(j, carry):
            left = a[:, cols(j, step)].T
            for i in range(n // wide):
                got = dot(left, g[:, cols(i, wide)]).astype(BF16)
                for c in range(wide // 128):
                    m[pl.ds(j * strips, strips), i * (wide // 128) + c] = got[:, c * 128 : (c + 1) * 128].reshape(strips, 16, 128)
            return carry

        lax.fori_loop(0, k // step, body, 0)

    def norm(self, r, gain, shift):
        centre = r - jnp.mean(r, axis=-1, keepdims=True)
        spread = jnp.mean(centre * centre, axis=-1, keepdims=True)
        return centre * lax.rsqrt(spread + norm_eps) * self.row(gain) + self.row(shift)

    def norm_back(self, r, dy, gain, shift):
        centre = r - jnp.mean(r, axis=-1, keepdims=True)
        spread = jnp.mean(centre * centre, axis=-1, keepdims=True)
        s = lax.rsqrt(spread + norm_eps)
        xh = centre * s
        t = dy * self.row(gain)
        dr = s * (t - jnp.mean(t, axis=-1, keepdims=True) - xh * jnp.mean(t * xh, axis=-1, keepdims=True))
        size = self.b.width
        kg, kb = VECS.index(gain), VECS.index(shift)
        self.vec[kg : kg + 1, :size] = jnp.sum(dy * xh, axis=0, keepdims=True)
        self.vec[kb : kb + 1, :size] = jnp.sum(dy, axis=0, keepdims=True)
        return dr

    def put_sum(self, name, ref):
        k = VECS.index(name)
        self.vec[k : k + 1, : self.b.place[name][2]] = jnp.sum(ref[...].astype(F32), axis=0, keepdims=True)

    def mask(self, fill, counts):
        b = self.b
        shape = (b.rows, b.other_rows)
        row = lax.broadcasted_iota(jnp.int32, shape, 0)
        col = lax.broadcasted_iota(jnp.int32, shape, 1)
        value = jnp.full(shape, other_sequence, F32)
        for q in range(b.seqs):
            mine = (row >= q * b.length) & (row < (q + 1) * b.length)
            mine = mine & (col >= q * b.other_length) & (col < (q + 1) * b.other_length)
            value = jnp.where(mine, jnp.where(col < q * b.other_length + counts(q), 1.0, masked_score), value)
        fill[...] = value

    def heads_of(self, refs, g):
        e = self.b.inner // self.b.heads
        values = [ref[:, cols(g, 128)] for ref in refs]
        if e == 128:
            return [values]
        lane = lax.broadcasted_iota(jnp.int32, (1, 128), 1)
        return [
            [jnp.where((lane >= h * e) & (lane < (h + 1) * e), value, jnp.zeros((), BF16)) for value in values]
            for h in range(128 // e)]

    def attend(self, q, k, v, fill, p, c):
        b = self.b
        e = b.inner // b.heads
        scale = 1.0 / math.sqrt(e)
        per = max(128 // e, 1)

        def body(g, carry):
            keys = k[:, cols(g, 128)]
            total = None
            for h, (qh,) in enumerate(self.heads_of([q], g)):
                vh = self.heads_of([v], g)[h][0]
                s = dot(qh, keys, NT) * scale
                f = fill[...]
                s = jnp.where(f > 0, s, f)
                ex = jnp.exp(s - jnp.max(s, axis=-1, keepdims=True))
                probs = (ex * (1.0 / jnp.sum(ex, axis=-1, keepdims=True))).astype(BF16)
                p[g * per + h] = probs
                got = dot(probs, vh)
                total = got if total is None else total + got
            c[:, cols(g, 128)] = total.astype(BF16)
            return carry

        lax.fori_loop(0, b.inner // 128, body, 0, unroll=2)

    def attend_back(self, q, k, v, p, dc):
        b = self.b
        e = b.inner // b.heads
        scale = 1.0 / math.sqrt(e)
        per = max(128 // e, 1)

        def body(g, carry):
            values = v[:, cols(g, 128)]
            sums = None
            for h, (qh, kh, dh) in enumerate(self.heads_of([q, k, dc], g)):
                probs = p[g * per + h]
                dp = dot(dh, values, NT)
                wide = probs.astype(F32)
                ds = (wide * (dp - jnp.sum(wide * dp, axis=-1, keepdims=True))).astype(BF16)
                got = [dot(ds, kh), dot(ds, qh, TN), dot(probs, dh, TN)]
                sums = got if sums is None else [x + y for x, y in zip(sums, got)]
            q[:, cols(g, 128)] = (sums[0] * scale).astype(BF16)
            k[:, cols(g, 128)] = (sums[1] * scale).astype(BF16)
            v[:, cols(g, 128)] = sums[2].astype(BF16)
            return carry

        lax.fori_loop(0, b.inner // 128, body, 0, unroll=2)

    def forward(self, x, u, z, counts, tick=lambda k=1: None, need=lambda name: None):
        s, b = self.s, self.b
        need("o_w")
        self.load_vectors(GROUPS[:3])
        self.mask(s["fill"], counts)

        def put(ref, bias=None):
            def store(c, value):
                if bias is not None:
                    value = value + self.row(bias, c)
                ref[:, c] = value.astype(BF16)
            return store

        tick()
        self.nn(u, "q_w", put(s["q"], "q_b"))
        self.nn(z, "k_w", put(s["k"]))
        tick()
        self.nn(z, "v_w", put(s["v"], "v_b"))
        tick()
        self.attend(s["q"], s["k"], s["v"], s["fill"], s["p"], s["c"])

        tick()

        def first(c, value):
            s["r1"][:, c] = x[:, c].astype(F32) + (value + self.row("o_b", c))

        self.nn(s["c"], "o_w", first)
        y1 = self.norm(s["r1"][...], "g1", "b1")
        s["r2"][...] = y1
        s["y1"][...] = y1.astype(BF16)

        def up(c, value):
            value = value + self.row("i_b", c)
            half = 0.5 * (1.0 + lax.erf(value * (1.0 / math.sqrt(2.0))))
            s["a"][:, c] = (value * half).astype(BF16)
            s["gp"][:, c] = (half + value * (jnp.exp(-0.5 * value * value) * (1.0 / math.sqrt(2.0 * math.pi)))).astype(BF16)

        tick()
        need("i_w")
        self.load_vectors(GROUPS[3:4])
        self.nn(s["y1"], "i_w", up)
        tick()
        need("f_w")
        self.load_vectors(GROUPS[4:])

        def second(c, value):
            s["r2"][:, c] = s["r2"][:, c] + (value + self.row("f_b", c))

        self.nn(s["a"], "f_w", second)
        return self.norm(s["r2"][...], "g2", "b2")

    def backward(self, dy, u, z, put_resid, put_z, done, tick=lambda k=1: None):
        s, b = self.s, self.b
        small = s["small"]
        dr2 = self.norm_back(s["r2"][...], dy[...], "g2", "b2")
        dy[...] = dr2
        s["m"][...] = dr2.astype(BF16)
        self.put_sum("f_b", s["m"])

        def inner(c, value):
            s["gp"][:, c] = (value * s["gp"][:, c].astype(F32)).astype(BF16)

        self.nt(s["m"], "f_w", inner)
        self.store_vectors(GROUPS[4], small)
        self.tn(s["a"], s["m"], "f_w")
        done("f_w")
        self.put_sum("i_b", s["gp"])

        def mid(c, value):
            dy[:, c] = dy[:, c] + value

        self.nt(s["gp"], "i_w", mid)
        tick(4)
        self.store_vectors(GROUPS[3], small)
        self.tn(s["y1"], s["gp"], "i_w")
        done("i_w")
        tick()
        dr1 = self.norm_back(s["r1"][...], dy[...], "g1", "b1")
        dy[...] = dr1
        s["m"][...] = dr1.astype(BF16)
        self.put_sum("o_b", s["m"])

        def context(c, value):
            s["dc"][:, c] = value.astype(BF16)

        self.nt(s["m"], "o_w", context)
        self.store_vectors(GROUPS[2], small)
        self.tn(s["c"], s["m"], "o_w")
        done("o_w")
        tick(3)
        self.attend_back(s["q"], s["k"], s["v"], s["p"], s["dc"])

        tick(2)

        def resid(c, value):
            put_resid(c, dy[:, c] + value)

        self.nt(s["q"], "q_w", resid)
        k = b.place["v_w"][1]
        step = step_of(k, NT_STEP)

        def body(j, carry):
            value = dot(s["k"][...], self.rows_of("k_w", j, step), NT) + dot(s["v"][...], self.rows_of("v_w", j, step), NT)
            put_z(cols(j, step), value)
            return carry

        lax.fori_loop(0, k // step, body, 0)
        tick()
        self.put_sum("q_b", s["q"])
        self.put_sum("v_b", s["v"])
        self.store_vectors(GROUPS[0], small)
        self.store_vectors(GROUPS[1], small)
        self.tn(u, s["q"], "q_w")
        self.tn(z, s["k"], "k_w")
        self.tn(z, s["v"], "v_w")
        done("q_w")
        tick(2)


def scratch_of(b):
    return {
        "q": ((b.rows, b.inner), BF16), "k": ((b.other_rows, b.inner), BF16), "v": ((b.other_rows, b.inner), BF16),
        "p": ((b.heads, b.rows, b.other_rows), BF16), "c": ((b.rows, b.inner), BF16),
        "r1": ((b.rows, b.width), F32), "r2": ((b.rows, b.width), F32), "y1": ((b.rows, b.width), BF16),
        "a": ((b.rows, b.hidden), BF16), "gp": ((b.rows, b.hidden), BF16), "fill": ((b.rows, b.other_rows), F32)}


def compute_kernel(co, sa, lens, x, xp, gy, wco, wsa, out, own_grad, sent, gco, gsa, wc, ws, vec, vec2, small, sems, *scr):
    names = sorted(scratch_of(co))
    sc = dict(zip(names, scr[: len(names)]))
    ss = dict(zip(names, scr[len(names) : 2 * len(names)]))
    rest = scr[2 * len(names) :]
    m, dy, h, hb, dcc, dcs = rest
    for d, dc in ((sc, dcc), (ss, dcs)):
        d["m"], d["small"], d["dc"] = m, small, dc
    x, xp = View(x, (co.rows, co.width)), View(xp, (co.other_rows, co.other))
    own_grad, sent = View(own_grad, (co.rows, co.width)), View(sent, (co.other_rows, co.other))
    h, hb, dy = [View(r, (co.rows, co.width)) for r in (h, hb, dy)]
    for b, d in ((co, sc), (sa, ss)):
        shapes = {**{n: k[0] for n, k in scratch_of(b).items()}, "m": (b.rows, b.width), "dc": (b.rows, b.inner)}
        for n, shape in shapes.items():
            d[n] = View(d[n], shape)
    copies = [pltpu.make_async_copy(wco, wc, sems.at[0]), pltpu.make_async_copy(wsa, ws, sems.at[1])]
    for cp in copies:
        cp.start()
    copies[0].wait()
    a = Net(co, wc, vec, sc)
    bnet = Net(sa, ws, vec2, ss)
    value = a.forward(x, x, xp, lambda q: lens[1, q])
    h[...] = value
    hb[...] = value.astype(BF16)
    copies[1].wait()
    out[...] = bnet.forward(h, hb, hb, lambda q: lens[0, q]).astype(BF16)
    dy[...] = gy[...].astype(F32)

    def put_h(c, value):
        h[:, c] = value

    def add_h(c, value):
        h[:, c] = h[:, c] + value

    bnet.backward(dy, hb, hb, put_h, add_h, lambda name: None)
    back = pltpu.make_async_copy(ws, gsa, sems.at[1])
    back.start()

    def put_own(c, value):
        own_grad[:, c] = value

    def put_sent(c, value):
        sent[:, c] = value.astype(BF16)

    a.backward(h, x, xp, put_own, put_sent, lambda name: None)
    back2 = pltpu.make_async_copy(wc, gco, sems.at[0])
    back2.start()
    back.wait()
    back2.wait()


def compute(co, sa, lens, x, xp, gy, wco, wsa):
    any_ = pl.BlockSpec(memory_space=pl.ANY)
    vm = pl.BlockSpec(memory_space=pltpu.VMEM)
    names = sorted(scratch_of(co))
    V = lambda shape, dtype: pltpu.VMEM(shape, dtype)
    scr = [V(wco.shape, BF16), V(wsa.shape, BF16), V((16, 3072), F32), V((16, 3072), F32), V((32, 128), F32), pltpu.SemaphoreType.DMA((2,))]
    scr += [V(*scratch_of(co)[n]) for n in names] + [V(*scratch_of(sa)[n]) for n in names]
    rows, width = co.rows, co.width
    scr += [V((rows, width), BF16), V((rows, width), F32), V((rows, width), F32), V((rows, width), BF16)]
    scr += [V((b.rows, b.inner), BF16) for b in (co, sa)]
    return pl.pallas_call(
        functools.partial(compute_kernel, co, sa),
        out_shape=(jax.ShapeDtypeStruct((rows, width), BF16), jax.ShapeDtypeStruct((rows, width), F32),
                   jax.ShapeDtypeStruct((co.other_rows, co.other), BF16),
                   jax.ShapeDtypeStruct(wco.shape, BF16), jax.ShapeDtypeStruct(wsa.shape, BF16)),
        in_specs=[pl.BlockSpec(memory_space=pltpu.SMEM), vm, vm, vm, any_, any_],
        out_specs=(vm, vm, vm, any_, any_),
        scratch_shapes=scr,
        compiler_params=pltpu.CompilerParams(vmem_limit_bytes=63 * 2**20),
        name="compute",
    )(lens, x, xp, gy, wco, wsa)


PER = UNITS + 1
SLOTS_TEXT, SLOTS_IMAGE, SLOTS_CO = (2, 4, 3, 2, 1, 1), (2, 0, 4, 2, 1, 4), (1, 1, 0, 1, 0, 1)
HOP = 3
BEHIND = 2


class Where:
    def __init__(self, line):
        self.line, self.last = line, line - 1
        self.z, self.x, self.c = place(line)
        self.s = lax.axis_index("stream")

    def copy(self, src, dst, send, recv, z, x, c, s=None):
        return pltpu.make_async_remote_copy(
            src_ref=src, dst_ref=dst, send_sem=send, recv_sem=recv,
            device_id=(self.s if s is None else s, (z * 2 + x) * 2 + c), device_id_type=MESH_ID)

    def greet(self):
        z, x, c, s = self.z, self.x, self.c, self.s
        barrier = pltpu.get_barrier_semaphore()

        def signal(zz, xx, cc, ss):
            pl.semaphore_signal(barrier, inc=1, device_id=(ss, (zz * 2 + xx) * 2 + cc), device_id_type=MESH_ID)

        signal(z, 1 - x, c, s)
        signal(z, x, 1 - c, s)
        signal(z, x, c, 1 - s)
        d = (z * 2 + x) * 2 + c
        beside = (1 - c) * jnp.minimum(d, 1) + c * jnp.minimum(4 * self.line - 1 - d, 1)

        @pl.when(beside > 0)
        def _():
            pl.semaphore_signal(barrier, inc=1, device_id=(s, d - 1 + 2 * c), device_id_type=MESH_ID)

        @pl.when(z > 0)
        def _():
            signal(z - 1, x, c, s)

        @pl.when(z < self.last)
        def _():
            signal(z + 1, x, c, s)

        pl.semaphore_wait(barrier, 3 + jnp.minimum(z, 1) + jnp.minimum(self.last - z, 1) + beside)


class Gather:
    def __init__(self, at, rows, w, sems):
        self.at, self.rows, self.w = at, rows, w
        self.n = self.rows // UNITS
        self.up_s, self.dn_s, self.z_r, self.x_s, self.x_r, self.c_s, self.c_r, self.o_s = sems

    def lies(self, u):
        return jnp.where(u == 0, 1, jnp.where(u < 4, u + 2, jnp.where(u == 4, 0, 2))) * self.n

    def spot(self, zo, xb, cc, u):
        return self.w.at[pl.ds(((zo * 2 + xb) * 2 + cc) * self.rows + self.lies(u), self.n)]

    def block_of(self, v):
        x = self.at.x
        return jnp.where(v == UNITS, 1 - x, x), jnp.minimum(v, UNITS - 1)

    def z_copy(self, zo, v, up):
        at = self.at
        xb, u = self.block_of(v)
        spot = self.spot(zo, xb, at.c, u)
        return at.copy(spot, spot, (self.up_s if up else self.dn_s).at[zo], self.z_r.at[zo * PER + v], at.z + 1 if up else at.z - 1, at.x, at.c)

    def x_copy(self, zo, u, arriving=False, first=False):
        at = self.at
        spot = self.spot(zo, 1 - at.x if arriving else at.x, at.c, u)
        return at.copy(spot, spot, self.o_s if first else self.x_s.at[zo], self.x_r.at[zo * UNITS + u], at.z, 1 - at.x, at.c)

    def c_copy(self, zo, xb, u):
        at = self.at
        spot = self.spot(zo, xb, at.c, u)
        return at.copy(spot, spot, self.c_s.at[zo], self.c_r.at[zo], at.z, at.x, 1 - at.c)

    def send_z(self, zo, v, up):
        at = self.at

        @pl.when(at.z < at.last if up else at.z > 0)
        def _():
            self.z_copy(zo, v, up).start()

    def first(self):
        self.x_copy(self.at.z, UNITS - 1, first=True).start()

    def start_unit(self, u):
        at = self.at

        @pl.when(u == UNITS - 1)
        def _():
            self.first()

        @pl.when(u != UNITS - 1)
        def _():
            self.x_copy(at.z, u).start()

        self.send_z(at.z, u, True)
        self.send_z(at.z, u, False)
        self.c_copy(at.z, at.x, u).start()

    def start(self):
        at = self.at
        for u in range(UNITS - 1):
            self.x_copy(at.z, u).start()
            self.send_z(at.z, u, False)
        self.send_z(at.z, UNITS - 1, False)
        for u in range(UNITS):
            self.c_copy(at.z, at.x, u).start()

    def other_last(self, up):
        at = self.at
        self.x_copy(at.z, UNITS - 1, arriving=True).wait_recv()
        self.send_z(at.z, UNITS, False)
        if up:
            self.send_z(at.z, UNITS, True)
        self.c_copy(at.z, 1 - at.x, UNITS - 1).start()

    def onward(self, zo, v, up):
        xb, u = self.block_of(v)
        self.z_copy(zo, v, up).wait_recv()
        self.send_z(zo, v, up)

        @pl.when(v < UNITS - 1)
        def _():
            self.x_copy(zo, u).start()

        self.c_copy(zo, xb, u).start()

    def from_below(self, t):
        h, v = t // PER, lax.rem(t, PER)

        @pl.when(self.at.z > h)
        def _():
            self.onward(self.at.z - 1 - h, v, True)

    def from_above(self, t):
        h, v = t // PER, lax.rem(t, PER)

        @pl.when(self.at.z + h < self.at.last)
        def _():
            self.onward(self.at.z + 1 + h, v, False)

    def in_order(self, i):
        z = self.at.z
        zo, v = i // PER, lax.rem(i, PER)

        @pl.when(jnp.logical_and(i >= 0, zo < z))
        def _():
            self.onward(zo, v, True)

        @pl.when(jnp.logical_and(i >= 0, zo == z))
        def _():
            self.send_z(z, v, True)

    def x_arrival(self, zo, u):
        self.x_copy(zo, u, arriving=True).wait_recv()
        self.c_copy(zo, 1 - self.at.x, u).start()

    def beside_own(self):
        for u in range(UNITS - 1):
            self.x_arrival(self.at.z, u)

    def beside_far(self, t):
        at = self.at
        h, v = t // PER, lax.rem(t, PER)

        @pl.when(jnp.logical_and(t >= 0, v < UNITS - 1))
        def _():
            @pl.when(at.z > h)
            def _():
                self.x_arrival(at.z - 1 - h, v)

            @pl.when(at.z + h < at.last)
            def _():
                self.x_arrival(at.z + 1 + h, v)

    def beside_order(self, i):
        zo, v = i // PER, lax.rem(i, PER)

        @pl.when(jnp.logical_and(jnp.logical_and(i >= 0, v < UNITS - 1), zo < self.at.z))
        def _():
            self.x_arrival(zo, v)

    def beside_above(self, t):
        at = self.at
        h, v = t // PER, lax.rem(t, PER)

        @pl.when(jnp.logical_and(jnp.logical_and(t >= 0, v < UNITS - 1), at.z + h < at.last))
        def _():
            self.x_arrival(at.z + 1 + h, v)

    def arrived(self, zo):
        at = self.at
        spot = self.w.at[pl.ds(0, 2 * self.rows)]
        at.copy(spot, spot, self.o_s, self.c_r.at[zo], at.z, at.x, 1 - at.c).wait_recv()

    def sent(self):
        at = self.at
        z = at.z

        def wait(tiles, sem):
            spot = self.w.at[pl.ds(0, tiles)]
            at.copy(spot, spot, sem, self.c_r.at[0], z, at.x, 1 - at.c).wait_send()

        def each(zo, carry):
            @pl.when(jnp.logical_and(z < at.last, zo <= z))
            def _():
                wait(PER * self.n, self.up_s.at[zo])

            @pl.when(jnp.logical_and(z > 0, zo >= z))
            def _():
                wait(PER * self.n, self.dn_s.at[zo])

            wait((UNITS - 1) * self.n, self.x_s.at[zo])
            wait(2 * self.rows, self.c_s.at[zo])
            return carry

        lax.fori_loop(0, at.line, each, 0)
        wait(self.n, self.o_s)


def gather_sems(line):
    dma = pltpu.SemaphoreType.DMA
    return [dma((line,)), dma((line,)), dma((line * PER,)), dma((line,)), dma((line * UNITS,)), dma((line,)), dma((line,)), dma]


class Scatter:
    def __init__(self, at, g, rows, cr, xr, zr, keep, stage, wide_stage, behind, lead, hop, sems):
        self.at, self.g, self.rows, self.n = at, g, rows, rows // UNITS
        self.cr, self.xr, self.zr, self.keep, self.stage, self.wide = cr, xr, zr, keep, stage, wide_stage
        self.c_s, self.c_r, self.x_s, self.x_r, self.z_s, self.z_r, self.l_s, self.b_s = sems
        self.hop = hop
        self.lead = lead
        self.behind = behind
        self.items = at.last * PER
        self.final = self.items + lead + at.last * hop + behind
        self.slots = self.final + PER

    def lies(self, u):
        return (u + UNITS // 2) % UNITS * self.n if isinstance(u, int) else lax.rem(u + UNITS // 2, UNITS) * self.n

    def mine(self, zo, xb, u):
        return pl.ds(((zo * 2 + xb) * 2 + self.at.c) * self.rows + self.lies(u), self.n)

    def block_of(self, v):
        x = self.at.x
        return jnp.where(v == 0, 1 - x, x), jnp.where(v == 0, UNITS - 1, v - 1)

    def c_copy(self, zo, xb):
        at = self.at
        src = self.g.at[pl.ds(((zo * 2 + xb) * 2 + 1 - at.c) * self.rows, self.rows)]
        k = zo * 2 + xb
        return at.copy(src, self.cr.at[k], self.c_s.at[zo], self.c_r.at[k], at.z, at.x, 1 - at.c)

    def x_copy(self, zo, u, last=False):
        at = self.at
        k = zo * UNITS + u
        return at.copy(self.g.at[self.mine(zo, 1 - at.x, u)], self.xr.at[k], self.b_s if last else self.x_s.at[zo], self.x_r.at[k],
                       at.z, 1 - at.x, at.c)

    def z_copy(self, to, v, up):
        at = self.at
        xb, u = self.block_of(v)
        there = at.z + 1 if up else at.z - 1
        k = (to if up else jnp.where(to == there, at.line, to)) * PER + v
        return at.copy(self.g.at[self.mine(to, xb, u)], self.zr.at[k], self.z_s.at[to], self.z_r.at[k], there, at.x, at.c)

    def z_wait(self, k):
        at = self.at
        spot = self.zr.at[k]
        at.copy(spot, spot, self.z_s.at[0], self.z_r.at[k], at.z, 1 - at.x, at.c).wait_recv()

    def ready(self, zo):
        for xb in range(2):
            self.c_copy(zo, xb).start()

    def load(self, src, slot):
        return pltpu.make_async_copy(src, self.stage.at[slot, pl.ds(0, self.n)], self.l_s.at[slot])

    def core_part(self, zo, xb, u):
        return self.cr.at[zo * 2 + xb, pl.ds(self.lies(u), self.n)]

    def way(self, t, up):
        at = self.at
        i = t - (at.z * self.hop if up else (at.last - at.z) * self.hop + self.behind)
        to = (at.last if up else at.last - 1) - i // PER
        here = jnp.logical_and(jnp.logical_and(i >= 0, i < self.items), to > at.z if up else to < at.z)
        return to, lax.rem(i, PER), here

    def crossings(self, t):
        at = self.at
        found = []
        for up, slot in ((True, 0), (False, 11)):
            to, v, here = self.way(t, up)
            found.append((to, v - 1, jnp.logical_and(here, jnp.logical_and(v >= 1, v < UNITS)), slot))
        u = t - self.items - 1
        found.append((at.z, u, jnp.logical_and(u >= 0, u < UNITS - 1), 12))
        return found

    def parts(self, t, finals):
        found = [self.way(t - self.lead, up) + (up, slot) for up, slot in ((True, 1), (False, 4))]
        own = t - self.final
        return found + [(self.at.z, own, jnp.logical_and(own >= 0, own < PER), None, 7)] * finals

    def prepare(self, t, finals=False):
        at = self.at
        for to, u, here, slot in self.crossings(t):
            @pl.when(here)
            def _(to=to, u=u, slot=slot):
                @pl.when(u == 0)
                def _():
                    for xb in range(2):
                        self.c_copy(to, xb).wait_recv()

                self.load(self.core_part(to, 1 - at.x, u), slot).start()

        for to, v, here, up, slot in self.parts(t, finals):
            @pl.when(here)
            def _(to=to, v=v, up=up, slot=slot):
                xb, u = self.block_of(v)
                self.load(self.core_part(to, xb, u), slot).start()

                @pl.when(jnp.logical_and(v >= 1, v < (UNITS if up is not None else PER)))
                def _():
                    self.x_copy(to, u).wait_recv()
                    self.load(self.xr.at[to * UNITS + u], slot + 1).start()

                if up is None:
                    @pl.when(at.z > 0)
                    def _():
                        self.z_wait(to * PER + v)
                        self.load(self.zr.at[to * PER + v], slot + 2).start()

                    @pl.when(at.z < at.last)
                    def _():
                        self.z_wait(at.line * PER + v)
                        self.load(self.zr.at[at.line * PER + v], slot + 3).start()
                else:
                    @pl.when(at.z != (0 if up else at.last))
                    def _():
                        self.z_wait(to * PER + v)
                        self.load(self.zr.at[to * PER + v], slot + 2).start()

    def take(self, slot):
        self.load(self.xr.at[0], slot).wait()
        return self.stage[slot].astype(F32)

    def act(self, t, finals):
        at = self.at
        for to, v, here, up, slot in self.parts(t, finals):
            @pl.when(here)
            def _(to=to, v=v, up=up, slot=slot):
                xb, u = self.block_of(v)
                spot = self.mine(to, xb, u)
                acc = self.wide

                acc[: self.n] = self.g[spot].astype(F32) + self.take(slot)

                def more(k):
                    acc[: self.n] = acc[: self.n] + self.take(slot + k)

                @pl.when(jnp.logical_and(v >= 1, v < (UNITS if up is not None else PER)))
                def _():
                    more(1)

                if up is None:
                    @pl.when(at.z > 0)
                    def _():
                        more(2)

                    @pl.when(at.z < at.last)
                    def _():
                        more(3)

                    @pl.when(v == 0)
                    def _():
                        self.g[spot] = acc[: self.n].astype(BF16)
                        self.x_copy(to, UNITS - 1, True).start()

                    @pl.when(v >= 1)
                    def _():
                        self.keep(self.lies(u))
                else:
                    @pl.when(at.z != (0 if up else at.last))
                    def _():
                        more(2)

                    self.g[spot] = acc[: self.n].astype(BF16)
                    self.z_copy(to, v, up).start()

        for to, u, here, slot in self.crossings(t):
            @pl.when(here)
            def _(to=to, u=u, slot=slot):
                spot = self.mine(to, 1 - at.x, u)
                self.g[spot] = (self.g[spot].astype(F32) + self.take(slot)).astype(BF16)
                self.x_copy(to, u).start()

    def slot(self, t, finals=False):
        self.act(t, finals)
        self.prepare(t + 1, finals)

    def sent(self):
        at = self.at
        z = at.z

        def wait(tiles, sem):
            spot = self.g.at[pl.ds(0, tiles)]
            at.copy(spot, spot, sem, self.c_r.at[0], z, at.x, 1 - at.c).wait_send()

        def each(zo, carry):
            @pl.when(zo != z)
            def _():
                wait(PER * self.n, self.z_s.at[zo])

            wait((UNITS - 1) * self.n, self.x_s.at[zo])
            wait(2 * self.rows, self.c_s.at[zo])
            return carry

        lax.fori_loop(0, at.line, each, 0)
        wait(self.n, self.b_s)


def scatter_sems(line):
    dma = pltpu.SemaphoreType.DMA
    return [dma((line,)), dma((line * 2,)), dma((line,)), dma((line * UNITS,)), dma((line,)), dma(((line + 1) * PER,)), dma((13,)), dma]


def landing(line, rows):
    n = rows // UNITS
    shape = lambda *s: jax.ShapeDtypeStruct(s + (16, 128), BF16)
    return [shape(line * 2, rows), shape(line * UNITS, n), shape((line + 1) * PER, n)]


class Edges:
    def __init__(self, at, plan, window, first, spare, land, sems):
        self.at, self.plan, self.window, self.first, self.spare, self.land = at, plan, window, first, spare, land
        self.f_s, self.f_r, self.l_s, self.e_s, self.e_r = sems
        self.d = (at.z * 2 + at.x) * 2 + at.c
        self.end = plan.before + plan.shard

    def over(self, src, dst, send, recv, by):
        return pltpu.make_async_remote_copy(
            src_ref=src, dst_ref=dst, send_sem=send, recv_sem=recv, device_id=(self.at.s, self.d + by), device_id_type=MESH_ID)

    def both(self, up, down):
        @pl.when(self.d < 4 * self.at.line - 1)
        def _():
            up()

        @pl.when(self.d > 0)
        def _():
            down()

    def lands(self, ref):
        plan = self.plan
        return ref.at[pl.ds(0, plan.before)], ref.at[pl.ds(plan.before, plan.after)]

    def outer(self, own):
        plan = self.plan
        before, after = self.lands(self.first)
        return (self.over(own.at[pl.ds(plan.shard - plan.before, plan.before), 0], before, self.f_s.at[0], self.f_r.at[0], 1),
                self.over(own.at[pl.ds(0, plan.after), 0], after, self.f_s.at[1], self.f_r.at[1], -1))

    def send(self, own):
        up, down = self.outer(own)
        self.both(up.start, down.start)

    def inner(self, own):
        return pltpu.make_async_copy(own.at[:, 0], self.window.at[pl.ds(self.plan.before, self.plan.shard)], self.l_s)

    def clear_tiles(self, w):
        w[pl.ds(self.plan.rows * self.d, self.plan.rows)] = jnp.zeros((self.plan.rows, 16, 128), w.dtype)

    def enter(self, own):
        plan = self.plan
        up, down = self.outer(own)

        def above():
            down.wait_recv()
            self.window[self.end : self.end + plan.after, :] = self.first[plan.before : plan.before + plan.after, :]

        def below():
            up.wait_recv()
            self.window[: plan.before, :] = self.first[: plan.before, :]

        self.both(above, below)

    def tiles(self, kinds, w, first, count):
        lo = self.plan.rows * self.d + first

        def act(tile, row, stride, rows):
            value = self.window[pl.ds(row, rows, stride=stride), :]
            if rows < 16:
                value = jnp.concatenate([value, jnp.zeros((16 - rows, 128), value.dtype)], axis=0)
            w[tile] = value.astype(w.dtype)

        self.by_stream(kinds, lo, lo + count, act)

    def entered(self, own):
        up, down = self.outer(own)
        self.both(up.wait_send, down.wait_send)

    def by_stream(self, kinds, lo, hi, act):
        start = self.plan.shard * self.d - self.plan.before
        for s, b in enumerate(kinds):
            @pl.when(self.at.s == s)
            def _(b=b):
                each_tile(b, lo, hi, start, act)

    def clear(self):
        self.window[...] = jnp.zeros(self.window.shape, F32)

    def take(self, kinds, acc, n):
        def keep(first):
            lo = self.plan.rows * self.d + first

            def act(tile, row, stride, rows):
                self.window[pl.ds(row, rows, stride=stride), :] = acc[tile - lo][:rows]

            self.by_stream(kinds, lo, lo + n, act)

        return keep

    def back(self):
        plan = self.plan
        front, rear = self.lands(self.land)
        return (self.over(self.spare.at[pl.ds(0, plan.after)], rear, self.e_s.at[0], self.e_r.at[0], 1),
                self.over(self.window.at[pl.ds(0, plan.before)], front, self.e_s.at[1], self.e_r.at[1], -1))

    def give(self):
        self.spare[: self.plan.after, :] = self.window[self.end : self.end + self.plan.after, :]
        up, down = self.back()
        self.both(up.start, down.start)

    def finish(self, out):
        plan = self.plan
        up, down = self.back()

        def above():
            down.wait_recv()
            spot = slice(self.end - plan.before, self.end)
            self.window[spot, :] = self.window[spot, :] + self.land[: plan.before, :]

        def below():
            up.wait_recv()
            spot = slice(plan.before, plan.before + plan.after)
            self.window[spot, :] = self.window[spot, :] + self.land[plan.before : plan.before + plan.after, :]

        self.both(above, below)
        self.leave(out).start()

    def leave(self, out):
        return pltpu.make_async_copy(self.window.at[pl.ds(self.plan.before, self.plan.shard)], out.at[:, 0], self.l_s)

    def done(self, out):
        self.leave(out).wait()
        up, down = self.back()
        self.both(up.wait_send, down.wait_send)


def edge_sems():
    dma = pltpu.SemaphoreType.DMA
    return [dma((2,)), dma((2,)), dma, dma((2,)), dma((2,))]


def to_flat(flat, box):
    count = box.shape[1] // 128
    for b in range(count):
        flat[pl.ds(b, box.shape[0], stride=count), :] = box[:, b * 128 : (b + 1) * 128].astype(F32)


def from_flat(flat, rows, count, put):
    for j in range(count):
        put(j, flat[pl.ds(j, rows, stride=count), :])


def layer_kernel(plans, line, texts, regions, xbox, gbox, co_flat, sa_flat, *refs):
    kinds = list(zip(plans[0].blocks, plans[1].blocks))
    outs, refs = refs[:10], refs[10:]
    out_box, grad_box, co_out, sa_out = outs[:4]
    wc, ws, vec, vec2, small, pool, land, xp, xin, ret, stage_c, stage_s, acc = refs[:13]
    refs = refs[13:]
    names = sorted(KEPT)
    sc = dict(zip(names, refs[: len(names)]))
    refs = refs[len(names) :]
    ss = dict(zip(names, refs[: len(names)]))
    refs = refs[len(names) :]
    shared = dict(zip(sorted(SHARED), refs[: len(SHARED)]))
    refs = refs[len(SHARED) :]
    ag_c, ag_s, rs_c, rs_s, ed_c, ed_s, y_s, y_r = refs[:8], refs[8:16], refs[16:24], refs[24:32], refs[32:37], refs[37:42], refs[42], refs[43]
    sent = shared["dc"]
    span = pool_span(plans)
    flat = pool.at[pl.ds(6 * span, span)]

    at = Where(line)
    last = at.last
    gc, gs = Gather(at, plans[0].rows, wc, ag_c), Gather(at, plans[1].rows, ws, ag_s)
    edges = []
    rest = max(p.window for p in plans)
    for k, (p, sems) in enumerate(zip(plans, (ed_c, ed_s))):
        sizes = [q.before + q.after for q in plans]
        edges.append(Edges(at, p, pool.at[pl.ds(0, p.window)], pool.at[pl.ds(rest + k * sizes[0], sizes[k])], pool.at[pl.ds(rest, p.after)],
                           land.at[pl.ds(k * sizes[0], sizes[k])], sems))
    ec, es = edges
    own_kinds = [[k[i] for k in kinds] for i in range(2)]
    rc = Scatter(at, wc, plans[0].rows, *outs[4:7], ec.take(own_kinds[0], acc, gc.n), stage_c, acc, 0, 5, 1, rs_c)
    rs = Scatter(at, ws, plans[1].rows, *outs[7:10], es.take(own_kinds[1], acc, gs.n), stage_s, acc, BEHIND, 4, HOP, rs_s)

    def over(k, src, dst):
        return at.copy(src, dst, y_s.at[k], y_r.at[k], at.z, at.x, at.c, 1 - at.s)

    ec.inner(co_flat).start()
    at.greet()
    ec.send(co_flat)
    es.send(sa_flat)
    ec.clear_tiles(wc)
    ec.inner(co_flat).wait()

    def begin(k, carry):
        @pl.when(k == 2)
        def _():
            ec.enter(co_flat)

        u = lax.rem(k + UNITS - 1, UNITS)
        ec.tiles(own_kinds[0], wc, gc.lies(u), gc.n)
        gc.start_unit(u)
        return carry

    lax.fori_loop(0, UNITS, begin, 0)
    es.inner(sa_flat).start()
    states = over(0, xbox, xp)
    states.start()
    ec.entered(co_flat)
    es.clear_tiles(ws)
    es.inner(sa_flat).wait()
    es.enter(sa_flat)
    es.tiles(own_kinds[1], ws, 0, plans[1].rows)
    es.entered(sa_flat)
    gs.first()
    gc.other_last(True)

    steps = PER * last
    early = PER

    def co_step(t, carry):
        gc.from_below(t)
        gc.from_above(t)

        @pl.when(t < UNITS - 1)
        def _():
            gc.x_arrival(at.z, t)

        gc.beside_far(t - PER)

        @pl.when(jnp.logical_and(t >= steps - early, at.z < last))
        def _():
            gs.in_order(t - (steps - early) - at.z)

        return carry

    lax.fori_loop(0, steps - early, co_step, 0)
    gs.start()
    gs.other_last(False)
    lax.fori_loop(steps - early, steps, co_step, 0)

    def co_rest(t, carry):
        gc.beside_far(t)
        return carry

    lax.fori_loop(steps - PER, steps, co_rest, 0)
    gs.beside_own()
    for zo in range(line):
        gc.arrived(zo)
    states.wait_recv()

    ahead = jnp.where(at.z < last, early - at.z, 0)

    def self_beside(t):
        gs.beside_order(t + ahead)
        gs.beside_above(t)

    def self_steps(a, b, lag):
        def step(t, carry):
            gs.in_order(t + ahead)
            gs.from_above(t)
            self_beside(t - lag)
            return carry

        lax.fori_loop(a, b, step, 0)

    def self_rest(a, b):
        lax.fori_loop(a, b, lambda t, carry: (self_beside(t), carry)[1], 0)

    gather_steps = steps
    scatter_ticks = sum(SLOTS_TEXT) + sum(SLOTS_CO)

    def run(text, co, sa):
        rows, width = co.rows, co.width

        def view(refs, b):
            d = {name: View(ref, kept_shapes(b)[name]) for name, ref in refs.items()}
            for name, ref in shared.items():
                d[name] = View(ref, shared_shapes(b)[name])
            for k, name in enumerate(("r1", "r2")):
                d[name] = Pooled(pool, (2 * (b is sa) + k) * span, b.rows, b.width)
            d["h"], d["dy"] = [Pooled(pool, k * span, b.rows, b.width) for k in (4, 5)]
            d["small"] = small
            return d

        a = Net(co, wc, vec, view(sc, co))
        b = Net(sa, ws, vec2, view(ss, sa))
        h, hb, dy = b.s["h"], b.s["hb"], b.s["dy"]

        own_in = View(xin, (rows, width))
        if text:
            to_flat(flat, xbox)

            def put(j, value):
                own_in[:, cols(j, 128)] = value.astype(BF16)

            from_flat(flat, rows, width // 128, put)
            x, z = own_in, View(xp, xp.shape)
        else:
            to_flat(flat, xp)
            other = View(xin, (co.other_rows, co.other))

            def put(j, value):
                other[:, cols(j, 128)] = value.astype(BF16)

            from_flat(flat, co.other_rows, co.other // 128, put)
            x, z = View(xbox, xbox.shape), other

        steps_done, beside_done, places = [0], [-PER], [0]

        def tick(k=1):
            a0 = steps_done[0]
            b0 = min(a0 + k, gather_steps)
            if b0 > a0:
                self_steps(a0, b0, a0 - beside_done[0])
                beside_done[0] += b0 - a0
                steps_done[0] = b0

        def need(name):
            later = [sa.place[n][0] for n in ("i_w", "f_w") if sa.place[n][0] > sa.place[name][0]]
            top = -(-min(later + [sa.tiles]) // (4 * gs.rows))
            wanted = min(PER * top, gather_steps)
            tick(min(wanted + 3, gather_steps) - steps_done[0])
            if beside_done[0] < wanted:
                self_rest(beside_done[0], wanted)
                beside_done[0] = wanted
            for zo in range(places[0], top):
                gs.arrived(zo)
            places[0] = max(places[0], top)

        own_counts, other_counts = (texts, regions) if text else (regions, texts)
        value = a.forward(x, x, z, lambda q: other_counts[q], tick)
        h[...] = value
        hb[...] = value.astype(BF16)
        gc.sent()
        if text:
            to_flat(flat, gbox)

            def put(j, value):
                dy[:, cols(j, 128)] = value

            from_flat(flat, rows, width // 128, put)
        else:
            dy[...] = gbox[...].astype(F32)
        value = b.forward(h, hb, hb, lambda q: own_counts[q], tick, need)
        if text:
            for j in range(width // 128):
                flat[pl.ds(j, rows, stride=width // 128), :] = value[:, j * 128 : (j + 1) * 128]
        else:
            out_box[...] = value.astype(BF16)
        gs.sent()

        def put_h(c, value):
            h[:, c] = value

        def add_h(c, value):
            h[:, c] = h[:, c] + value

        ticks = [0]

        def hooks(scatter, block):
            state = [line]

            def done(name):
                tile = block.place[name][0]
                ready = -(-tile // (4 * scatter.rows))
                while state[0] > ready:
                    state[0] -= 1
                    scatter.ready(state[0])
                    if scatter is rs and state[0] == last:
                        rs.prepare(0)

            return done

        def slots(k):
            a0 = ticks[0]
            ticks[0] = a0 + k
            if k:
                lax.fori_loop(a0, a0 + k, lambda t, carry: (rs.slot(t), carry)[1], 0)

        def rs_tick(counts):
            left = list(counts)
            return lambda k=1: slots(left.pop(0))

        b.backward(dy, hb, hb, put_h, add_h, hooks(rs, sa), rs_tick(SLOTS_TEXT if text else SLOTS_IMAGE))
        if text:
            def put(j, value):
                out_box[:, j * 128 : (j + 1) * 128] = value.astype(BF16)

            from_flat(flat, out_box.shape[0], out_box.shape[1] // 128, put)

        def put_own(c, value):
            dy[:, c] = value

        sent_rows = View(sent, (co.other_rows, co.other))

        def put_sent(c, value):
            sent_rows[:, c] = value.astype(BF16)

        a.backward(h, x, z, put_own, put_sent, hooks(rc, co), rs_tick(SLOTS_CO))
        over(1, sent, ret).start()
        assert ticks[0] == scatter_ticks

    for s, (co, sa) in enumerate(kinds):
        @pl.when(at.s == s)
        def _(s=s, co=co, sa=sa):
            run(s == 0, co, sa)

    back = over(1, sent, ret)

    def grads_of_states():
        back.wait_recv()
        for s, (co, sa) in enumerate(kinds):
            @pl.when(at.s == s)
            def _(s=s, co=co):
                mine = Pooled(pool, 5 * span, co.rows, co.width)
                got = View(ret, (co.rows, co.width))
                if s == 0:
                    count = co.width // 128
                    for j in range(count):
                        flat[pl.ds(j, co.rows, stride=count), :] = mine[:, cols(j, 128)] + got[:, cols(j, 128)].astype(F32)

                    def put(j, value):
                        grad_box[:, j * 128 : (j + 1) * 128] = value

                    from_flat(flat, grad_box.shape[0], grad_box.shape[1] // 128, put)
                else:
                    grad_box[...] = mine[...] + got[...].astype(F32)

    rc.prepare(0)
    es.clear()
    shift = rs.items
    steps = shift + rc.slots

    def both(t, carry):
        @pl.when(t < rs.slots)
        def _():
            rs.slot(t, True)

        @pl.when(t == rs.slots)
        def _():
            es.give()

        @pl.when(t == rs.slots + 2)
        def _():
            es.finish(sa_out)

        @pl.when(t == rs.slots + 4)
        def _():
            es.done(sa_out)
            ec.clear()
            rs.sent()

        @pl.when(t == shift + rc.final - 1)
        def _():
            grads_of_states()

        @pl.when(t >= shift)
        def _():
            rc.slot(t - shift, True)

        @pl.when(t == shift + rc.final + 4)
        def _():
            ec.give()

        return carry

    assert rs.slots + 4 < shift + rc.final
    lax.fori_loop(scatter_ticks, steps, both, 0)
    ec.finish(co_out)
    back.wait_send()
    states.wait_send()
    rc.sent()
    ec.done(co_out)


KEPT = ("q", "k", "v", "p", "c", "y1", "a", "gp")
SHARED = ("fill", "m", "hb", "dc")


def kept_shapes(b):
    return {k: v[0] for k, v in scratch_of(b).items()}


def shared_shapes(b):
    rows, width = b.rows, b.width
    return {"fill": (b.rows, b.other_rows), "m": (rows, width), "hb": (rows, width), "dc": (rows, b.inner)}


SHARED_TYPES = {"fill": F32}


def most(shapes):
    return tuple(max(k) for k in zip(*shapes))


def pool_span(plans):
    return max(b.rows * b.width // 128 for p in plans for b in p.blocks)


def layer_call(plans, line, texts, regions, xbox, gbox, co_flat, sa_flat, cid):
    vm = pl.BlockSpec(memory_space=pltpu.VMEM)
    any_ = pl.BlockSpec(memory_space=pl.ANY)
    rows_c, rows_s = [p.rows for p in plans]
    V = pltpu.VMEM
    cos, sas = [p.blocks for p in plans]
    wide = most([(b.rows, b.width) for b in cos] + [(b.other_rows, b.other) for b in cos])
    n = max(rows_c, rows_s) // UNITS
    edge = sum(p.before + p.after for p in plans)
    assert max(p.window for p in plans) + edge <= 5 * pool_span(plans)
    scr = [V((plans[0].tiles, 16, 128), BF16), V((plans[1].tiles, 16, 128), BF16), V((16, 3072), F32), V((16, 3072), F32), V((32, 128), F32),
           V((7 * pool_span(plans), 128), F32), V((edge, 128), F32), V(xbox.shape, BF16), V(wide, BF16), V(wide, BF16),
           V((13, rows_c // UNITS, 16, 128), BF16), V((13, rows_s // UNITS, 16, 128), BF16), V((n, 16, 128), F32)]
    for bs in (cos, sas):
        for name in sorted(KEPT):
            scr.append(V(most([kept_shapes(b)[name] for b in bs]), scratch_of(bs[0])[name][1]))
    for name in sorted(SHARED):
        shape = most([shared_shapes(b)[name] for b in cos + sas] + ([wide] if name == "dc" else []))
        scr.append(V(shape, SHARED_TYPES.get(name, BF16)))
    dma = pltpu.SemaphoreType.DMA
    scr += gather_sems(line) + gather_sems(line) + scatter_sems(line) + scatter_sems(line) + edge_sems() + edge_sems() + [dma((2,)), dma((2,))]
    struct = jax.ShapeDtypeStruct
    outs = [struct(xbox.shape, BF16), struct(xbox.shape, F32), struct(co_flat.shape, F32), struct(sa_flat.shape, F32)]
    outs += landing(line, rows_c) + landing(line, rows_s)
    return pl.pallas_call(
        functools.partial(layer_kernel, plans, line),
        out_shape=outs,
        in_specs=[pl.BlockSpec(memory_space=pltpu.SMEM)] * 2 + [vm, vm, any_, any_],
        out_specs=[vm, vm] + [any_] * 8,
        scratch_shapes=scr,
        compiler_params=pltpu.CompilerParams(collective_id=cid, has_side_effects=True, vmem_limit_bytes=64 * 2**20 - 2**16),
        name="layer",
    )(texts, regions, xbox, gbox, co_flat, sa_flat)[:4]


DT, HT, FT = 768, 12, 3072
DI, HI, FI = 1024, 8, 1024
DC, HC = 1024, 8
LT, LI = 128, 96
LINE_MAX = 8


def blocks_of(text, seqs):
    if text:
        return (Block(DT, DI, DC, FT, HC, LT, LI, seqs), Block(DT, DT, DT, FT, HT, LT, LT, seqs))
    return (Block(DI, DT, DC, FI, HC, LI, LT, seqs), Block(DI, DI, DI, FI, HI, LI, LI, seqs))


class Plan:
    def __init__(self, blocks, devices, flat_total):
        self.blocks = blocks
        self.shard = flat_total // 128 // devices
        tiles = max(b.tiles for b in blocks)
        self.rows = -(-tiles // (devices * UNITS)) * UNITS
        self.tiles = self.rows * devices
        tables = [self.table(b).reshape(self.tiles, 16) for b in blocks]
        before = after = 0
        inner = True
        for table in tables:
            most = table.max(axis=1)
            least = np.where(table >= 0, table, flat_total).min(axis=1)
            for d in range(devices):
                lo, hi, start, end = self.rows * d, self.rows * (d + 1), self.shard * d, self.shard * (d + 1)
                held = np.nonzero(most[lo:hi] >= 0)[0] + lo
                if held.size:
                    before = max(before, start - least[held].min())
                    after = max(after, most[held].max() + 1 - end)
                    unit = (held - lo) * UNITS // self.rows
                    outer = (least[held] < start) & (unit > 0) | (most[held] >= end) & (unit < UNITS // 2)
                    inner = inner and not outer.any()
        self.before, self.after = [max(-(-int(k) // 16) * 16, 16) for k in (before, after)]
        self.window = -(-(self.before + self.shard + self.after) // 8) * 8
        self.near = max(self.before, self.after) <= self.shard and inner

    def table(self, b):
        index = np.full((self.tiles * 16,), -1, np.int32)
        for first, flat, k, rows, nb in b.parts:
            if k:
                r, j = np.arange(k)[:, None], np.arange(nb)[None]
                at = first * 16 + ((r // 16) * nb + j) * 16 + r % 16
                index[at.reshape(-1)] = (flat + r * nb + j).reshape(-1)
            else:
                index[first * 16 : first * 16 + rows] = flat + np.arange(rows)
        return index


def each_tile(b, lo, hi, start, act):
    for first, flat, k, rows, nb in b.parts:
        if k:
            count = rows // 16
            a = jnp.clip(lo - first, 0, count)
            z = jnp.clip(hi - first, 0, count)

            def body(t, carry, first=first, flat=flat, nb=nb):
                i = t // nb
                act(first + t, flat + i * 16 * nb + (t - i * nb) - start, nb, 16)
                return carry

            lax.fori_loop(a, z, body, 0)
        else:
            for t in range((rows + 15) // 16):
                @pl.when(jnp.logical_and(first + t >= lo, first + t < hi))
                def _(t=t, first=first, flat=flat, rows=rows):
                    act(first + t, flat + 16 * t - start, 1, min(16, rows - 16 * t))


def gathered(plan, text, flat):
    whole = lax.all_gather(flat.astype(BF16), "dp", axis=0, tiled=True).reshape(-1, 128)
    index = jnp.where(text, *[jnp.asarray(plan.table(b)) for b in plan.blocks])
    rows = jnp.where((index >= 0)[:, None], whole[jnp.maximum(index, 0)], jnp.zeros((), BF16))
    return rows.reshape(plan.tiles, 16, 128)


def scattered(plan, text, tiles, flat_rows):
    tables = []
    for b in plan.blocks:
        table = plan.table(b)
        back = np.full((flat_rows,), -1, np.int32)
        held = np.nonzero(table >= 0)[0]
        back[table[held]] = held
        tables.append(jnp.asarray(back))
    index = jnp.where(text, *tables)
    rows = jnp.where((index >= 0)[:, None], tiles.reshape(-1, 128)[jnp.maximum(index, 0)], jnp.zeros((), BF16))
    return lax.psum_scatter(rows.astype(F32), "dp", scatter_dimension=0, tiled=True).reshape(-1)


def layer_alone(text, counts, own, partner, grad, wco, wsa):
    seqs = own.shape[0]
    co, sa = blocks_of(text, seqs)
    box = own.shape
    lens = counts if text else counts[::-1]
    out, own_grad, sent, gco, gsa = compute(
        co, sa, lens, own.reshape(co.rows, co.width), partner.reshape(co.other_rows, co.other),
        grad.reshape(co.rows, co.width), wco, wsa)
    return out.reshape(box), own_grad.reshape(box), sent.reshape(box), gco, gsa


def body(devices, states, out_grad, co_params, self_params, text_lengths, region_counts):
    own = states[0]
    seqs = own.shape[0]
    text = lax.axis_index("stream") == 0
    flats = (co_params[0], self_params[0])
    streams = [blocks_of(t, seqs) for t in (True, False)]
    plans = [Plan([k[i] for k in streams], devices, f.shape[0] * devices) for i, f in enumerate(flats)]
    line = devices // 4
    if devices % 4 == 0 and line <= LINE_MAX and all(p.near for p in plans):
        box = (own.shape[0] * own.shape[1], own.shape[2])
        flats = [f.reshape(p.shard, 1, 128) for p, f in zip(plans, flats)]
        out, grad, co_grad, sa_grad = layer_call(plans, line, text_lengths, region_counts, own.reshape(box), out_grad[0].reshape(box), *flats, 1)
        return (out.reshape(states.shape), grad.reshape(states.shape), co_grad.reshape(co_params.shape), sa_grad.reshape(self_params.shape))
    swap = [(0, 1), (1, 0)]
    partner = lax.ppermute(own, "stream", swap)
    wco, wsa = [gathered(p, text, f) for p, f in zip(plans, flats)]
    counts = jnp.stack([text_lengths, region_counts])
    out, own_grad, sent, gco, gsa = lax.cond(
        text, functools.partial(layer_alone, True), functools.partial(layer_alone, False),
        counts, own, partner, out_grad[0], wco, wsa)
    returned = lax.ppermute(sent, "stream", swap)
    flats = [scattered(p, text, g, p.shard * devices) for p, g in zip(plans, (gco, gsa))]
    return (out[None], (own_grad + returned.astype(F32))[None], flats[0][None], flats[1][None])


def solution(mesh):
    states = P("stream", "dp", None, None)
    flat = P("stream", "dp")
    return jax.shard_map(
        functools.partial(body, mesh.shape["dp"]), mesh=mesh, in_specs=(states, states, flat, flat, P("dp"), P("dp")),
        out_specs=(states, states, flat, flat), check_vma=False)
```
